512 devices in a mesh: context: 64 (over y_hi, x, z), dp: 8 (over y_lo, core).
Axes of the slice: x: 4, y: 8 (y_hi: 2, y_lo: 4; y = y_hi * 4 + y_lo), z: 8, core: 2. Of those that a mesh axis runs over, the one named last changes fastest.
Arguments:
- features: bfloat16 [4096, 3, 4096], P('context', None, 'dp'), may hold values from -6 to 6
- feat_weight: float32 [3, 3, 4096], P(None, None, 'dp'), may hold values from -30 to 30
- skip: float32 [4096], P('dp'), may hold values from -3 to 3
- residues: float32 [16, 4096], P(None, 'dp'), may hold values from -1.5 to 1.5
- rates: float32 [16, 4096], P(None, 'dp'), may hold values from 9.9e-06 to 0.0301
- norm_gain: float32 [4096], P('dp'), may hold values from 0.1 to 1.9
- attn_in: bfloat16 [4096, 3, 4096], P('context', None, 'dp'), may hold values from -8 to 8
Outputs:
- hyena_out: bfloat16 [4096, 4096], P('context', 'dp')
- attn_out: bfloat16 [4096, 4096], P('context', 'dp')
The draws below stay inside these ranges and needn't reach their ends.
All inputs are finite; a program needn't handle non-finite values.
Results may differ from the reference program's by a relative error of at most 0.012.
The reference program's roundings to bfloat16 on the way count: a program that leaves them out, or rounds other values in their place, can miss the bound.
Values may be sent and summed in bfloat16 or wider, within the bound.
No kernel may reach another device: no remote copies, remote signals or barrier semaphores. Data moves between devices by JAX's collectives and lax.ppermute only.
A program may use at most 64 MiB of HBM per device.

```python
import math
import jax
import jax.numpy as jnp
from jax import lax

DH = 4096
HEADS = 32
HEAD = 128
MODES = 16
FEAT = 3
TOK_DEV = 64
SPAN = 64
ROWS = 4096
N_CONTEXT = 64


def draw_feat_weight(key, part):
    key = jax.random.fold_in(key, 11)
    channel_pos = jnp.arange(DH, dtype=jnp.float32) / max(DH - 1, 1)
    values = jnp.clip(jax.random.normal(key, (FEAT, 3, DH), jnp.float32), -4.0, 4.0) * 0.6
    ramp_scale = jnp.exp(channel_pos * math.log(10.0))
    group_scale = jnp.where(jnp.arange(3)[None, :, None] == 0, ramp_scale[None, None, :], 1.0)
    return values * group_scale


def draw_rates(key, part):
    key = jax.random.fold_in(key, 23)
    key_fast = jax.random.fold_in(key, 0)
    spread = jax.random.uniform(key_fast, (MODES, DH), jnp.float32, math.log(1e-05), math.log(0.03))
    return jnp.exp(spread)


def draw_attn_in(key, part):
    key = jax.random.fold_in(key, 37)
    key_base = jax.random.fold_in(key, 0)
    width = HEADS * HEAD
    return jnp.clip(jax.random.normal(key_base, (ROWS, 3, width), jnp.float32), -5.0, 5.0).astype(jnp.bfloat16)


def levels(own_key, dims, pieces, low, top_value):
    level = 1.0
    for dim, shards_of in pieces:
        heights = jax.random.uniform(jax.random.fold_in(jax.random.fold_in(own_key, 6), dim), (shards_of,), jnp.float32, low / len(pieces), top_value / len(pieces))
        level = level * jnp.repeat(jnp.exp(heights), dims[dim] // shards_of).reshape((-1,) + (1,) * (len(dims) - 1 - dim))
    return level


def centred(key, extent, deviation, limit, shards=(), kind=jnp.bfloat16):
    values = jax.random.normal(key, extent, jnp.float32) * deviation
    if len(shards) > 0:
        values = levels(key, extent, shards, -0.22, 0.18) * values
    return jnp.clip(values, min=-limit, max=limit).astype(kind)


def setup_inputs(seed: int = 0) -> dict:
    arg_keys = jax.random.split(jax.random.key(seed), 8)
    return {
        "features": centred(arg_keys[0], (ROWS, 3, DH), 1.0, 6.0, ((0, 64), (2, 8))),
        "feat_weight": draw_feat_weight(jax.random.fold_in(arg_keys[7], 71), 0),
        "skip": centred(arg_keys[2], (DH,), 0.5, 3.0, ((0, 8),), jnp.float32),
        "residues": centred(arg_keys[3], (MODES, DH), 0.25, 1.5, ((1, 8),), jnp.float32),
        "rates": draw_rates(jax.random.fold_in(arg_keys[7], 71), 0),
        "norm_gain": jnp.clip(1.0 + 0.18 * jax.random.normal(arg_keys[5], (DH,), jnp.float32), 0.1, 1.9),
        "attn_in": draw_attn_in(jax.random.fold_in(arg_keys[7], 71), 0),
    }


rope_base = 1000000.0

def rotary(tensor, position):
    halfway = tensor.shape[-1] // 2
    inverse = jnp.exp(jnp.arange(halfway, dtype=jnp.float32) * (-2.0 * math.log(rope_base) / tensor.shape[-1]))
    angle = position[:, None] * inverse[None, :]
    cosine = jnp.cos(angle)[:, None, :]
    sine = jnp.sin(angle)[:, None, :]
    first_half = tensor[..., :halfway]
    second_half = tensor[..., halfway:]
    return jnp.concatenate([first_half * cosine - second_half * sine, second_half * cosine + first_half * sine], -1)

def reference(features, feat_weight, skip, residues, rates, norm_gain, attn_in):
    seq_len = TOK_DEV * SPAN
    groups = N_CONTEXT // SPAN
    inputs = features.astype(jnp.float32).reshape(groups, seq_len, 3, DH)
    padded = jnp.pad(inputs, ((0, 0), (FEAT - 1, 0), (0, 0), (0, 0)))
    featured = sum((feat_weight[offset] * padded[:, FEAT - 1 - offset:FEAT - 1 - offset + seq_len] for offset in range(FEAT)))
    query_gate = featured[:, :, 0]
    product = (featured[:, :, 1] * featured[:, :, 2]).astype(jnp.bfloat16)
    product = lax.optimization_barrier(product).astype(jnp.float32)
    time_steps = jnp.arange(seq_len, dtype=jnp.float32)

    def add_mode(impulse, operands):
        residue, mode_rate = operands
        weight = residue * jnp.sqrt(-jnp.expm1(-2.0 * mode_rate))
        return (impulse + weight[None, :] * jnp.exp(-mode_rate[None, :] * time_steps[:, None]), None)
    impulse, _ = lax.scan(add_mode, jnp.zeros((seq_len, DH), jnp.float32), (residues, rates))
    filter_spec = jnp.fft.rfft(impulse, n=2 * seq_len, axis=0)
    input_spec = jnp.fft.rfft(product, n=2 * seq_len, axis=1)
    convolved = jnp.fft.irfft(input_spec * filter_spec[None], n=2 * seq_len, axis=1)[:, :seq_len]
    convolved = convolved + skip * product
    gated_rows = query_gate * convolved
    mean_square = lax.optimization_barrier(jnp.sum(gated_rows * gated_rows, -1, keepdims=True)) / DH
    hyena_out = (gated_rows * lax.rsqrt(mean_square + 1e-06) * norm_gain).astype(jnp.bfloat16).reshape(ROWS, DH)
    attention = attn_in.astype(jnp.float32).reshape(ROWS, 3, HEADS, HEAD)
    positions = jnp.tile(jnp.arange(seq_len, dtype=jnp.float32), groups)
    query_rot = rotary(attention[:, 0], positions).astype(jnp.bfloat16)
    key_rot = rotary(attention[:, 1], positions).astype(jnp.bfloat16)
    values = attn_in[:, 2].reshape(ROWS, HEADS, HEAD)
    scale = 1.0 / math.sqrt(HEAD)
    block_len = min(1024, seq_len)

    def arrange(tensor):
        return tensor.reshape(groups, seq_len, HEADS, HEAD).transpose(0, 2, 1, 3).reshape(groups * HEADS, seq_len, HEAD)

    def one_head(operands):
        queries, keys, vals = operands
        outputs = []
        for block_start in range(0, seq_len, block_len):
            block_end = block_start + block_len
            scores = jnp.dot(queries[block_start:block_end], keys[:block_end].T, preferred_element_type=jnp.float32) * scale
            row_index = jnp.arange(block_start, block_end)[:, None]
            col_index = jnp.arange(block_end)[None, :]
            scores = jnp.where(col_index <= row_index, scores, -jnp.inf)
            row_max = lax.optimization_barrier(jnp.max(scores, -1, keepdims=True))
            weights = jnp.exp(scores - row_max)
            row_total = lax.optimization_barrier(jnp.sum(weights, -1, keepdims=True))
            mixed_rows = jnp.dot(weights.astype(jnp.bfloat16), vals[:block_end], preferred_element_type=jnp.float32) / row_total
            outputs.append(mixed_rows)
        return jnp.concatenate(outputs, 0)
    result = lax.map(one_head, (arrange(query_rot), arrange(key_rot), arrange(values)))
    attn_out = result.reshape(groups, HEADS, seq_len, HEAD).transpose(0, 2, 1, 3).reshape(ROWS, HEADS * HEAD).astype(jnp.bfloat16)
    return (hyena_out, attn_out)
```

```python
import functools
import itertools
import math

import jax
import jax.numpy as jnp
from jax import lax
from jax.experimental import pallas as pl
from jax.experimental.pallas import tpu as pltpu
from jax.sharding import PartitionSpec as P

DH = 4096
HEAD = 128
HEADS_DEV = 4
FEAT = 3
MODES = 16
TOK = 64
CH = 512
ROPE_BASE = 1000000.0
NEG = -1e30
BF = jnp.bfloat16
F32 = jnp.float32

DIGITS = {"y": (2, 32), "x": (4, 8), "z2": (2, 4), "w": (4, 1)}


def groups_over(*free):
    fixed = [d for d in DIGITS if d not in free]

    def places(names):
        return [
            sum(v * DIGITS[d][1] for v, d in zip(values, names))
            for values in itertools.product(*[range(DIGITS[d][0]) for d in names])
        ]

    return [[base + step for step in places(free)] for base in places(fixed)]


Q_GROUPS = groups_over("x", "w")
KV_GROUPS = groups_over("x", "z2")
STATE_GROUPS = groups_over("y", "w")

VMEM = pl.BlockSpec(memory_space=pltpu.VMEM)
SMEM = pl.BlockSpec(memory_space=pltpu.SMEM)


def call(kernel, outs, specs, flops, scratch=()):
    return pl.pallas_call(
        kernel,
        out_shape=[jax.ShapeDtypeStruct(s, d) for s, d in outs],
        in_specs=specs,
        out_specs=[VMEM] * len(outs),
        scratch_shapes=list(scratch),
        compiler_params=pltpu.CompilerParams(vmem_limit_bytes=40 * 1024 * 1024),
        cost_estimate=pl.CostEstimate(flops=flops, bytes_accessed=1000, transcendentals=0),
    )


def digits(index):
    return [(index // step) % size for size, step in DIGITS.values()]


def split2(value):
    high = value.astype(BF)
    return high, (value - high.astype(F32)).astype(BF)


def rotate_kernel(attn_ref, cos_ref, sin_ref, q_ref, kv_ref):
    cosine, sine = cos_ref[...], sin_ref[...]
    for g in range(2):
        x = attn_ref[g].astype(F32)
        for h in range(HEADS_DEV):
            part = x[:, h * HEAD : (h + 1) * HEAD]
            turned = (part * cosine + pltpu.roll(part, HEAD // 2, 1) * sine).astype(BF)
            if g == 0:
                for w in range(4):
                    q_ref[h * 4 + w] = turned
            else:
                kv_ref[h, :TOK, :] = turned
    for h in range(HEADS_DEV):
        kv_ref[h, TOK:, :] = attn_ref[2, :, h * HEAD : (h + 1) * HEAD]


def state_kernel(feat_ref, rim_ref, weight_ref, rates_ref, kv_ref, sent_ref, gate_ref, prod_ref):
    groups = []
    for g in range(3):
        x = jnp.concatenate([rim_ref[g], feat_ref[g].astype(F32)], 0)
        total = weight_ref[0, g : g + 1, :] * x[8 : 8 + TOK]
        for o in range(1, FEAT):
            total = total + weight_ref[o, g : g + 1, :] * x[8 - o : 8 - o + TOK]
        groups.append(total)
    gate_ref[...] = groups[0]
    product = (groups[1] * groups[2]).astype(BF).astype(F32)
    prod_ref[...] = product
    back = (TOK - 1 - lax.broadcasted_iota(jnp.int32, (TOK, 128), 0)).astype(F32)
    for part in range(CH // 128):
        lanes = slice(part * 128, (part + 1) * 128)
        u = product[:, lanes]
        rows = [
            jnp.sum(jnp.exp(-rates_ref[n : n + 1, lanes] * back) * u, 0, keepdims=True)
            for n in range(MODES)
        ]
        high, low = split2(jnp.concatenate(rows, 0))
        for peer in range(8):
            sent_ref[peer, 128 + part * 16 : 144 + part * 16, :] = high
            sent_ref[peer, 192 + part * 16 : 208 + part * 16, :] = low
    for x in range(4):
        for z2 in range(2):
            sent_ref[x * 2 + z2, :128, :] = kv_ref[x]


def near_kernel(prod_ref, coeff_ref, rates_ref, skip_ref, out_ref, padded, impulse):
    padded[:TOK, :] = jnp.zeros((TOK, CH), F32)
    padded[TOK:, :] = prod_ref[...]
    ahead = lax.broadcasted_iota(jnp.int32, (TOK, 128), 0).astype(F32)
    for part in range(CH // 128):
        lanes = slice(part * 128, (part + 1) * 128)
        total = jnp.zeros((TOK, 128), F32)
        for n in range(MODES):
            rate = rates_ref[n : n + 1, lanes]
            total = total + coeff_ref[n : n + 1, lanes] * jnp.exp(-rate * ahead)
        impulse[:, lanes] = total
        y = skip_ref[:, lanes] * prod_ref[:, lanes]
        for t in range(TOK):
            y = y + impulse[t : t + 1, lanes] * padded[TOK - t : 2 * TOK - t, lanes]
        out_ref[:, lanes] = y


def message_kernel(place_ref, got_ref, rates_ref, out_ref):
    y, x, z2, w = digits(place_ref[0])
    for part in range(CH // 128):
        lanes = slice(part * 128, (part + 1) * 128)
        decay = rates_ref[:, lanes] * (-float(TOK))
        states = [
            got_ref[i, 128 + part * 16 : 144 + part * 16, :].astype(F32)
            + got_ref[i, 192 + part * 16 : 208 + part * 16, :].astype(F32)
            for i in range(8)
        ]
        for j in range(8):
            target = (j // 4) * 32 + x * 8 + z2 * 4 + j % 4
            total = jnp.zeros((MODES, 128), F32)
            for i in range(8):
                source = y * 32 + (i // 2) * 8 + (i % 2) * 4 + w
                steps = target - source - 1
                keep = jnp.where(steps >= 0, 1.0, 0.0).astype(F32)
                far = jnp.maximum(steps, 0).astype(F32)
                total = total + (jnp.exp(decay * far) * keep) * states[i]
            out_ref[j, :, lanes] = total


def far_kernel(got_ref, coeff_ref, rates_ref, near_ref, gate_ref, gated_ref, square_ref):
    ahead = (lax.broadcasted_iota(jnp.int32, (TOK, 128), 0) + 1).astype(F32)
    squares = jnp.zeros((TOK, 128), F32)
    for part in range(CH // 128):
        lanes = slice(part * 128, (part + 1) * 128)
        state = got_ref[0, :, lanes]
        for j in range(1, 8):
            state = state + got_ref[j, :, lanes]
        y = near_ref[:, lanes]
        for n in range(MODES):
            rate = rates_ref[n : n + 1, lanes]
            y = y + jnp.exp(-rate * ahead) * (coeff_ref[n : n + 1, lanes] * state[n : n + 1, :])
        gated = gate_ref[:, lanes] * y
        gated_ref[:, lanes] = gated
        squares = squares + gated * gated
    total = jnp.broadcast_to(jnp.sum(squares, 1, keepdims=True), (TOK, 128))
    total = jnp.concatenate([total, jnp.zeros((TOK, 128), F32)], 0)
    square_ref[...] = jnp.transpose(total)[:8, :]


def norm_kernel(square_ref, gated_ref, gain_ref, out_ref):
    total = jnp.sum(square_ref[...], 0, keepdims=True)
    total = jnp.transpose(jnp.broadcast_to(total, (128, 128)))[:TOK, :]
    factor = lax.rsqrt(total * (1.0 / DH) + 1e-06)
    for part in range(CH // 128):
        lanes = slice(part * 128, (part + 1) * 128)
        out_ref[:, lanes] = (gated_ref[:, lanes] * factor * gain_ref[:, lanes]).astype(BF)


def attend_kernel(place_ref, q_ref, own_ref, other_ref, out_ref):
    y, _, z2, w = digits(place_ref[0])
    scale = 1.0 / math.sqrt(HEAD)
    wide = 256
    keys = jnp.concatenate(
        [own_ref[:, :TOK, :].reshape(8 * TOK, HEAD), other_ref[:, :TOK, :].reshape(8 * TOK, HEAD)], 0
    )
    values = jnp.concatenate(
        [own_ref[:, TOK:128, :].reshape(8 * TOK, HEAD), other_ref[:, TOK:, :].reshape(8 * TOK, HEAD)], 0
    )
    row = lax.broadcasted_iota(jnp.int32, (16 * TOK, 1), 0)
    block = row // TOK
    key_place = ((block // 2) % 4) * 8 + (block % 2) * 4 + w
    key_pos = key_place * TOK + row % TOK
    far_off = jnp.where(y == 1, -1, 1 << 20)
    key_pos = jnp.where(block < 8, key_pos, far_off)
    for tile in range(16 * TOK // wide):
        blocks = wide // TOK
        query = q_ref[tile * blocks : (tile + 1) * blocks].reshape(wide, HEAD)
        lane = lax.broadcasted_iota(jnp.int32, (1, wide), 1) + tile * wide
        q_block = lane // TOK
        q_pos = ((q_block // 4) * 8 + z2 * 4 + q_block % 4) * TOK + lane % TOK
        scores = lax.dot_general(
            keys, query, (((1,), (1,)), ((), ())), preferred_element_type=F32
        ) * scale
        scores = jnp.where(key_pos <= q_pos, scores, NEG)
        top = jnp.max(scores, 0, keepdims=True)
        weights = jnp.exp(scores - top)
        total = jnp.sum(weights, 0, keepdims=True)
        mixed = lax.dot_general(
            values, weights.astype(BF), (((0,), (0,)), ((), ())), preferred_element_type=F32
        ) / total
        mixed = jnp.transpose(mixed).astype(BF)
        level = top + jnp.log(total)
        high = level.astype(BF).astype(F32)
        rest = level - high
        middle = rest.astype(BF).astype(F32)
        last = rest - middle
        for b in range(blocks):
            place = tile * blocks + b
            out_ref[place, :TOK, :] = mixed[b * TOK : (b + 1) * TOK]
            lanes = slice((b // 2) * 128, (b // 2) * 128 + 128)
            which = lax.broadcasted_iota(jnp.int32, (16, 128), 0)
            stats = jnp.where(
                which == 0,
                high[:, lanes],
                jnp.where(which == 1, middle[:, lanes], jnp.where(which == 2, last[:, lanes], 0.0)),
            )
            out_ref[place, TOK:, :] = stats.astype(BF)


def merge_kernel(place_ref, got_ref, out_ref):
    odd = place_ref[0] % 2
    levels = jnp.concatenate(
        [jnp.sum(got_ref[k, TOK : TOK + 16, :].astype(F32), 0, keepdims=True) for k in range(16)], 0
    )
    levels = jnp.where(odd == 1, pltpu.roll(levels, TOK, 1), levels)
    weights = []
    for h in range(HEADS_DEV):
        part = levels[h * 4 : (h + 1) * 4]
        part = jnp.exp(part - jnp.max(part, 0, keepdims=True))
        weights.append(part / jnp.sum(part, 0, keepdims=True))
    weights = jnp.concatenate(weights + [jnp.zeros((112, 128), F32)], 0)
    weights = jnp.transpose(weights)[:TOK, :]
    for h in range(HEADS_DEV):
        total = jnp.zeros((TOK, HEAD), F32)
        for k in range(4):
            place = h * 4 + k
            total = total + weights[:, place : place + 1] * got_ref[place, :TOK, :].astype(F32)
        out_ref[:, h * HEAD : (h + 1) * HEAD] = total.astype(BF)


def exchange(value, groups):
    return lax.all_to_all(value, "context", 0, 0, axis_index_groups=groups, tiled=True)


def local(features, feat_weight, skip, residues, rates, norm_gain, attn_in):
    index = lax.axis_index("context")
    devices = lax.axis_size("context")
    place = index.astype(jnp.int32)[None]
    features = jnp.transpose(features, (1, 0, 2))
    attn_in = jnp.transpose(attn_in, (1, 0, 2))
    rim = lax.ppermute(
        features[:, TOK - (FEAT - 1) :], "context", [(s, s + 1) for s in range(devices - 1)]
    )

    coeff = residues * jnp.sqrt(-jnp.expm1(-2.0 * rates))
    inverse = jnp.exp(
        jnp.arange(HEAD // 2, dtype=F32) * (-2.0 * math.log(ROPE_BASE) / HEAD)
    )
    positions = (index * TOK + jnp.arange(TOK)).astype(F32)
    angle = positions[:, None] * inverse[None, :]
    cosine, sine = jnp.cos(angle), jnp.sin(angle)
    cosine = jnp.concatenate([cosine, cosine], 1)
    sine = jnp.concatenate([-sine, sine], 1)

    queries, pairs = call(
        rotate_kernel,
        [((16, TOK, HEAD), BF), ((HEADS_DEV, 2 * TOK, HEAD), BF)],
        [VMEM] * 3,
        1000000000,
    )(attn_in, cosine, sine)
    queries = exchange(queries, Q_GROUPS)

    rim = jnp.pad(rim.astype(F32), ((0, 0), (6, 0), (0, 0)))
    sent, gate, product = call(
        state_kernel,
        [((8, 256, HEAD), BF), ((TOK, CH), F32), ((TOK, CH), F32)],
        [VMEM] * 5,
        2000000000,
    )(features, rim, feat_weight, rates, pairs)
    queries, sent = lax.optimization_barrier((queries, sent))
    got = exchange(sent, KV_GROUPS)

    (near,) = call(
        near_kernel,
        [((TOK, CH), F32)],
        [VMEM] * 4,
        2000000000,
        [pltpu.VMEM((2 * TOK, CH), F32), pltpu.VMEM((TOK, CH), F32)],
    )(product, coeff, rates, skip[None, :])

    other = lax.ppermute(
        got[:, :128], "context", [(s, s + devices // 2) for s in range(devices // 2)]
    )
    (messages,) = call(
        message_kernel, [((8, MODES, CH), F32)], [SMEM, VMEM, VMEM], 1000000000
    )(place, got, rates)
    arrived = exchange(messages, STATE_GROUPS)

    gated, squares = call(
        far_kernel,
        [((TOK, CH), F32), ((8, 128), F32)],
        [VMEM] * 5,
        1000000000,
    )(arrived, coeff, rates, near, gate)
    squares = lax.all_to_all(squares, "dp", 0, 0, tiled=True)
    (hyena_out,) = call(norm_kernel, [((TOK, CH), BF)], [VMEM] * 3, 100000000)(
        squares, gated, norm_gain[None, :]
    )

    (partial,) = call(
        attend_kernel,
        [((16, TOK + 16, HEAD), BF)],
        [SMEM, VMEM, VMEM, VMEM],
        4000000000,
    )(place, queries, got, other)
    partial = exchange(partial, Q_GROUPS)
    (attn_out,) = call(merge_kernel, [((TOK, CH), BF)], [SMEM, VMEM], 1000000000)(place, partial)
    return (hyena_out, attn_out)


def solution(mesh):
    return jax.shard_map(
        local,
        mesh=mesh,
        in_specs=(
            P("context", None, "dp"),
            P(None, None, "dp"),
            P("dp"),
            P(None, "dp"),
            P(None, "dp"),
            P("dp"),
            P("context", None, "dp"),
        ),
        out_specs=(P("context", "dp"), P("context", "dp")),
        check_vma=False,
    )
```

```python
import functools
import itertools
import math

import jax
import jax.numpy as jnp
from jax import lax
from jax.experimental import pallas as pl
from jax.experimental.pallas import tpu as pltpu
from jax.sharding import PartitionSpec as P

DH = 4096
HEAD = 128
HEADS_DEV = 4
FEAT = 3
MODES = 16
TOK = 64
CH = 512
ROPE_BASE = 1000000.0
NEG = -1e30
BF = jnp.bfloat16
F32 = jnp.float32

DIGITS = {"y": (2, 32), "x": (4, 8), "z2": (2, 4), "w": (4, 1)}


def groups_over(*free):
    fixed = [d for d in DIGITS if d not in free]

    def places(names):
        return [
            sum(v * DIGITS[d][1] for v, d in zip(values, names))
            for values in itertools.product(*[range(DIGITS[d][0]) for d in names])
        ]

    return [[base + step for step in places(free)] for base in places(fixed)]


Q_GROUPS = groups_over("x", "w")
KV_GROUPS = groups_over("x", "z2")
STATE_GROUPS = groups_over("y", "w")

VMEM = pl.BlockSpec(memory_space=pltpu.VMEM)
SMEM = pl.BlockSpec(memory_space=pltpu.SMEM)


def call(kernel, outs, specs, flops, scratch=()):
    return pl.pallas_call(
        kernel,
        out_shape=[jax.ShapeDtypeStruct(s, d) for s, d in outs],
        in_specs=specs,
        out_specs=[VMEM] * len(outs),
        scratch_shapes=list(scratch),
        compiler_params=pltpu.CompilerParams(vmem_limit_bytes=40 * 1024 * 1024),
        cost_estimate=pl.CostEstimate(flops=flops, bytes_accessed=1000, transcendentals=0),
    )


def digits(index):
    return [(index // step) % size for size, step in DIGITS.values()]


def rotate_kernel(attn_ref, cos_ref, sin_ref, q_ref, kv_ref):
    cosine, sine = cos_ref[...], sin_ref[...]
    for g in range(2):
        x = attn_ref[g].astype(F32)
        for h in range(HEADS_DEV):
            part = x[:, h * HEAD : (h + 1) * HEAD]
            turned = (part * cosine + pltpu.roll(part, HEAD // 2, 1) * sine).astype(BF)
            if g == 0:
                for w in range(4):
                    q_ref[h * 4 + w] = turned
            else:
                kv_ref[h, :TOK, :] = turned
    for h in range(HEADS_DEV):
        kv_ref[h, TOK:, :] = attn_ref[2, :, h * HEAD : (h + 1) * HEAD]


def state_kernel(feat_ref, rim_ref, weight_ref, rates_ref, kv_ref, sent_ref, gate_ref, prod_ref):
    groups = []
    for g in range(3):
        x = jnp.concatenate([rim_ref[g], feat_ref[g].astype(F32)], 0)
        total = weight_ref[0, g : g + 1, :] * x[8 : 8 + TOK]
        for o in range(1, FEAT):
            total = total + weight_ref[o, g : g + 1, :] * x[8 - o : 8 - o + TOK]
        groups.append(total)
    gate_ref[...] = groups[0]
    product = (groups[1] * groups[2]).astype(BF).astype(F32)
    prod_ref[...] = product
    back = (TOK - 1 - lax.broadcasted_iota(jnp.int32, (TOK, 128), 0)).astype(F32)
    for part in range(CH // 128):
        lanes = slice(part * 128, (part + 1) * 128)
        u = product[:, lanes]
        rows = [
            jnp.sum(jnp.exp(-rates_ref[n : n + 1, lanes] * back) * u, 0, keepdims=True)
            for n in range(MODES)
        ]
        state = jnp.concatenate(rows, 0).astype(BF)
        for peer in range(8):
            sent_ref[peer, 128 + part * 16 : 144 + part * 16, :] = state
    for x in range(4):
        for z2 in range(2):
            sent_ref[x * 2 + z2, :128, :] = kv_ref[x]


def near_kernel(prod_ref, coeff_ref, rates_ref, skip_ref, out_ref, padded, impulse):
    padded[:TOK, :] = jnp.zeros((TOK, CH), F32)
    padded[TOK:, :] = prod_ref[...]
    ahead = lax.broadcasted_iota(jnp.int32, (TOK, 128), 0).astype(F32)
    for part in range(CH // 128):
        lanes = slice(part * 128, (part + 1) * 128)
        total = jnp.zeros((TOK, 128), F32)
        for n in range(MODES):
            rate = rates_ref[n : n + 1, lanes]
            total = total + coeff_ref[n : n + 1, lanes] * jnp.exp(-rate * ahead)
        impulse[:, lanes] = total
        y = skip_ref[:, lanes] * prod_ref[:, lanes]
        for t in range(TOK):
            y = y + impulse[t : t + 1, lanes] * padded[TOK - t : 2 * TOK - t, lanes]
        out_ref[:, lanes] = y


def message_kernel(place_ref, got_ref, rates_ref, out_ref):
    y, x, z2, w = digits(place_ref[0])
    for part in range(CH // 128):
        lanes = slice(part * 128, (part + 1) * 128)
        decay = rates_ref[:, lanes] * (-float(TOK))
        states = [
            got_ref[i, 128 + part * 16 : 144 + part * 16, :].astype(F32) for i in range(8)
        ]
        for j in range(8):
            target = (j // 4) * 32 + x * 8 + z2 * 4 + j % 4
            total = jnp.zeros((MODES, 128), F32)
            for i in range(8):
                source = y * 32 + (i // 2) * 8 + (i % 2) * 4 + w
                steps = target - source - 1
                keep = jnp.where(steps >= 0, 1.0, 0.0).astype(F32)
                far = jnp.maximum(steps, 0).astype(F32)
                total = total + (jnp.exp(decay * far) * keep) * states[i]
            out_ref[j, :, lanes] = total.astype(BF)


def far_kernel(got_ref, coeff_ref, rates_ref, near_ref, gate_ref, gated_ref, square_ref):
    ahead = (lax.broadcasted_iota(jnp.int32, (TOK, 128), 0) + 1).astype(F32)
    squares = jnp.zeros((TOK, 128), F32)
    for part in range(CH // 128):
        lanes = slice(part * 128, (part + 1) * 128)
        state = got_ref[0, :, lanes].astype(F32)
        for j in range(1, 8):
            state = state + got_ref[j, :, lanes].astype(F32)
        y = near_ref[:, lanes]
        for n in range(MODES):
            rate = rates_ref[n : n + 1, lanes]
            y = y + jnp.exp(-rate * ahead) * (coeff_ref[n : n + 1, lanes] * state[n : n + 1, :])
        gated = gate_ref[:, lanes] * y
        gated_ref[:, lanes] = gated
        squares = squares + gated * gated
    total = jnp.broadcast_to(jnp.sum(squares, 1, keepdims=True), (TOK, 128))
    total = jnp.concatenate([total, jnp.zeros((TOK, 128), F32)], 0)
    square_ref[...] = jnp.transpose(total)[:8, :]


def norm_kernel(square_ref, gated_ref, gain_ref, out_ref):
    total = jnp.sum(square_ref[...], 0, keepdims=True)
    total = jnp.transpose(jnp.broadcast_to(total, (128, 128)))[:TOK, :]
    factor = lax.rsqrt(total * (1.0 / DH) + 1e-06)
    for part in range(CH // 128):
        lanes = slice(part * 128, (part + 1) * 128)
        out_ref[:, lanes] = (gated_ref[:, lanes] * factor * gain_ref[:, lanes]).astype(BF)


def attend_kernel(place_ref, q_ref, own_ref, other_ref, out_ref):
    y, _, z2, w = digits(place_ref[0])
    scale = 1.0 / math.sqrt(HEAD)
    wide = 256
    keys = jnp.concatenate(
        [own_ref[:, :TOK, :].reshape(8 * TOK, HEAD), other_ref[:, :TOK, :].reshape(8 * TOK, HEAD)], 0
    )
    values = jnp.concatenate(
        [own_ref[:, TOK:128, :].reshape(8 * TOK, HEAD), other_ref[:, TOK:, :].reshape(8 * TOK, HEAD)], 0
    )
    row = lax.broadcasted_iota(jnp.int32, (16 * TOK, 1), 0)
    block = row // TOK
    key_place = ((block // 2) % 4) * 8 + (block % 2) * 4 + w
    key_pos = key_place * TOK + row % TOK
    far_off = jnp.where(y == 1, -1, 1 << 20)
    key_pos = jnp.where(block < 8, key_pos, far_off)
    for tile in range(16 * TOK // wide):
        blocks = wide // TOK
        query = q_ref[tile * blocks : (tile + 1) * blocks].reshape(wide, HEAD)
        lane = lax.broadcasted_iota(jnp.int32, (1, wide), 1) + tile * wide
        q_block = lane // TOK
        q_pos = ((q_block // 4) * 8 + z2 * 4 + q_block % 4) * TOK + lane % TOK
        scores = lax.dot_general(
            keys, query, (((1,), (1,)), ((), ())), preferred_element_type=F32
        ) * scale
        scores = jnp.where(key_pos <= q_pos, scores, NEG)
        top = jnp.max(scores, 0, keepdims=True)
        weights = jnp.exp(scores - top)
        total = jnp.sum(weights, 0, keepdims=True)
        mixed = lax.dot_general(
            values, weights.astype(BF), (((0,), (0,)), ((), ())), preferred_element_type=F32
        ) / total
        mixed = jnp.transpose(mixed).astype(BF)
        level = top + jnp.log(total)
        high = level.astype(BF).astype(F32)
        rest = level - high
        middle = rest.astype(BF).astype(F32)
        last = rest - middle
        for b in range(blocks):
            place = tile * blocks + b
            out_ref[place, :TOK, :] = mixed[b * TOK : (b + 1) * TOK]
            lanes = slice((b // 2) * 128, (b // 2) * 128 + 128)
            which = lax.broadcasted_iota(jnp.int32, (16, 128), 0)
            stats = jnp.where(
                which == 0,
                high[:, lanes],
                jnp.where(which == 1, middle[:, lanes], jnp.where(which == 2, last[:, lanes], 0.0)),
            )
            out_ref[place, TOK:, :] = stats.astype(BF)


def merge_kernel(place_ref, got_ref, out_ref):
    odd = place_ref[0] % 2
    levels = jnp.concatenate(
        [jnp.sum(got_ref[k, TOK : TOK + 16, :].astype(F32), 0, keepdims=True) for k in range(16)], 0
    )
    levels = jnp.where(odd == 1, pltpu.roll(levels, TOK, 1), levels)
    weights = []
    for h in range(HEADS_DEV):
        part = levels[h * 4 : (h + 1) * 4]
        part = jnp.exp(part - jnp.max(part, 0, keepdims=True))
        weights.append(part / jnp.sum(part, 0, keepdims=True))
    weights = jnp.concatenate(weights + [jnp.zeros((112, 128), F32)], 0)
    weights = jnp.transpose(weights)[:TOK, :]
    for h in range(HEADS_DEV):
        total = jnp.zeros((TOK, HEAD), F32)
        for k in range(4):
            place = h * 4 + k
            total = total + weights[:, place : place + 1] * got_ref[place, :TOK, :].astype(F32)
        out_ref[:, h * HEAD : (h + 1) * HEAD] = total.astype(BF)


def exchange(value, groups):
    return lax.all_to_all(value, "context", 0, 0, axis_index_groups=groups, tiled=True)


def local(features, feat_weight, skip, residues, rates, norm_gain, attn_in):
    index = lax.axis_index("context")
    devices = lax.axis_size("context")
    place = index.astype(jnp.int32)[None]
    features = jnp.transpose(features, (1, 0, 2))
    attn_in = jnp.transpose(attn_in, (1, 0, 2))
    rim = lax.ppermute(
        features[:, TOK - (FEAT - 1) :], "context", [(s, s + 1) for s in range(devices - 1)]
    )

    coeff = residues * jnp.sqrt(-jnp.expm1(-2.0 * rates))
    inverse = jnp.exp(
        jnp.arange(HEAD // 2, dtype=F32) * (-2.0 * math.log(ROPE_BASE) / HEAD)
    )
    positions = (index * TOK + jnp.arange(TOK)).astype(F32)
    angle = positions[:, None] * inverse[None, :]
    cosine, sine = jnp.cos(angle), jnp.sin(angle)
    cosine = jnp.concatenate([cosine, cosine], 1)
    sine = jnp.concatenate([-sine, sine], 1)

    queries, pairs = call(
        rotate_kernel,
        [((16, TOK, HEAD), BF), ((HEADS_DEV, 2 * TOK, HEAD), BF)],
        [VMEM] * 3,
        1000000000,
    )(attn_in, cosine, sine)
    queries = exchange(queries, Q_GROUPS)

    rim = jnp.pad(rim.astype(F32), ((0, 0), (6, 0), (0, 0)))
    sent, gate, product = call(
        state_kernel,
        [((8, 192, HEAD), BF), ((TOK, CH), F32), ((TOK, CH), F32)],
        [VMEM] * 5,
        2000000000,
    )(features, rim, feat_weight, rates, pairs)
    queries, sent = lax.optimization_barrier((queries, sent))
    got = exchange(sent, KV_GROUPS)

    other = lax.ppermute(
        got[:, :128], "context", [(s, s + devices // 2) for s in range(devices // 2)]
    )
    (messages,) = call(
        message_kernel, [((8, MODES, CH), BF)], [SMEM, VMEM, VMEM], 1000000000
    )(place, got, rates)
    arrived = exchange(messages, STATE_GROUPS)

    (near,) = call(
        near_kernel,
        [((TOK, CH), F32)],
        [VMEM] * 4,
        2000000000,
        [pltpu.VMEM((2 * TOK, CH), F32), pltpu.VMEM((TOK, CH), F32)],
    )(product, coeff, rates, skip[None, :])
    (partial,) = call(
        attend_kernel,
        [((16, TOK + 16, HEAD), BF)],
        [SMEM, VMEM, VMEM, VMEM],
        30000000000,
    )(place, queries, got, other)
    partial, arrived = lax.optimization_barrier((partial, arrived))
    partial = exchange(partial, Q_GROUPS)
    gated, squares = call(
        far_kernel,
        [((TOK, CH), F32), ((8, 128), F32)],
        [VMEM] * 5,
        1000000000,
    )(arrived, coeff, rates, near, gate)
    squares, partial = lax.optimization_barrier((squares, partial))
    squares = lax.all_to_all(squares, "dp", 0, 0, tiled=True)
    (attn_out,) = call(merge_kernel, [((TOK, CH), BF)], [SMEM, VMEM], 1000000000)(place, partial)
    (hyena_out,) = call(norm_kernel, [((TOK, CH), BF)], [VMEM] * 3, 100000000)(
        squares, gated, norm_gain[None, :]
    )
    return (hyena_out, attn_out)


def solution(mesh):
    return jax.shard_map(
        local,
        mesh=mesh,
        in_specs=(
            P("context", None, "dp"),
            P(None, None, "dp"),
            P("dp"),
            P(None, "dp"),
            P(None, "dp"),
            P("dp"),
            P("context", None, "dp"),
        ),
        out_specs=(P("context", "dp"), P("context", "dp")),
        check_vma=False,
    )
```

```python
import functools
import itertools
import math

import jax
import jax.numpy as jnp
from jax import lax
from jax.experimental import pallas as pl
from jax.experimental.pallas import tpu as pltpu
from jax.sharding import PartitionSpec as P

DH = 4096
HEAD = 128
HEADS_DEV = 4
FEAT = 3
MODES = 16
TOK = 64
CH = 512
ROPE_BASE = 1000000.0
NEG = -1e30
WIDE = 256
BLOCKS = WIDE // TOK
BF = jnp.bfloat16
F32 = jnp.float32

DIGITS = {"y": (2, 32), "x": (4, 8), "z2": (2, 4), "w": (4, 1)}


def groups_over(*free):
    fixed = [d for d in DIGITS if d not in free]

    def places(names):
        return [
            sum(v * DIGITS[d][1] for v, d in zip(values, names))
            for values in itertools.product(*[range(DIGITS[d][0]) for d in names])
        ]

    return [[base + step for step in places(free)] for base in places(fixed)]


Q_GROUPS = groups_over("x", "w")
KV_GROUPS = groups_over("x", "z2")
STATE_GROUPS = groups_over("y", "w")

VMEM = pl.BlockSpec(memory_space=pltpu.VMEM)
SMEM = pl.BlockSpec(memory_space=pltpu.SMEM)


def call(kernel, outs, specs, flops, scratch=()):
    return pl.pallas_call(
        kernel,
        out_shape=[jax.ShapeDtypeStruct(s, d) for s, d in outs],
        in_specs=specs,
        out_specs=[VMEM] * len(outs),
        scratch_shapes=list(scratch),
        compiler_params=pltpu.CompilerParams(vmem_limit_bytes=40 * 1024 * 1024),
        cost_estimate=pl.CostEstimate(flops=flops, bytes_accessed=1000, transcendentals=0),
    )


def digits(index):
    return [(index // step) % size for size, step in DIGITS.values()]


def rotate_kernel(attn_ref, cos_ref, sin_ref, q_ref, kv_ref):
    cosine, sine = cos_ref[...], sin_ref[...]
    for g in range(2):
        x = attn_ref[g].astype(F32)
        for h in range(HEADS_DEV):
            part = x[:, h * HEAD : (h + 1) * HEAD]
            turned = (part * cosine + pltpu.roll(part, HEAD // 2, 1) * sine).astype(BF)
            if g == 0:
                for w in range(4):
                    q_ref[h * 4 + w] = turned
            else:
                kv_ref[h, :TOK, :] = turned
    for h in range(HEADS_DEV):
        kv_ref[h, TOK:, :] = attn_ref[2, :, h * HEAD : (h + 1) * HEAD]


def state_kernel(feat_ref, rim_ref, weight_ref, rates_ref, kv_ref, sent_ref, gate_ref, prod_ref):
    groups = []
    for g in range(3):
        x = jnp.concatenate([rim_ref[g], feat_ref[g].astype(F32)], 0)
        total = weight_ref[0, g : g + 1, :] * x[8 : 8 + TOK]
        for o in range(1, FEAT):
            total = total + weight_ref[o, g : g + 1, :] * x[8 - o : 8 - o + TOK]
        groups.append(total)
    gate_ref[...] = groups[0]
    product = (groups[1] * groups[2]).astype(BF).astype(F32)
    prod_ref[...] = product
    back = (TOK - 1 - lax.broadcasted_iota(jnp.int32, (TOK, 128), 0)).astype(F32)
    for part in range(CH // 128):
        lanes = slice(part * 128, (part + 1) * 128)
        u = product[:, lanes]
        rows = [
            jnp.sum(jnp.exp(-rates_ref[n : n + 1, lanes] * back) * u, 0, keepdims=True)
            for n in range(MODES)
        ]
        state = jnp.concatenate(rows, 0).astype(BF)
        for peer in range(8):
            sent_ref[peer, 128 + part * 16 : 144 + part * 16, :] = state
    for x in range(4):
        for z2 in range(2):
            sent_ref[x * 2 + z2, :128, :] = kv_ref[x]


def near_kernel(prod_ref, coeff_ref, rates_ref, skip_ref, out_ref, padded, impulse):
    padded[:TOK, :] = jnp.zeros((TOK, CH), F32)
    padded[TOK:, :] = prod_ref[...]
    ahead = lax.broadcasted_iota(jnp.int32, (TOK, 128), 0).astype(F32)
    for part in range(CH // 128):
        lanes = slice(part * 128, (part + 1) * 128)
        total = jnp.zeros((TOK, 128), F32)
        for n in range(MODES):
            rate = rates_ref[n : n + 1, lanes]
            total = total + coeff_ref[n : n + 1, lanes] * jnp.exp(-rate * ahead)
        impulse[:, lanes] = total
        y = skip_ref[:, lanes] * prod_ref[:, lanes]
        for t in range(TOK):
            y = y + impulse[t : t + 1, lanes] * padded[TOK - t : 2 * TOK - t, lanes]
        out_ref[:, lanes] = y


def message_kernel(place_ref, got_ref, rates_ref, out_ref):
    y, x, z2, w = digits(place_ref[0])
    for part in range(CH // 128):
        lanes = slice(part * 128, (part + 1) * 128)
        decay = rates_ref[:, lanes] * (-float(TOK))
        states = [
            got_ref[i, 128 + part * 16 : 144 + part * 16, :].astype(F32) for i in range(8)
        ]
        for j in range(8):
            target = (j // 4) * 32 + x * 8 + z2 * 4 + j % 4
            total = jnp.zeros((MODES, 128), F32)
            for i in range(8):
                source = y * 32 + (i // 2) * 8 + (i % 2) * 4 + w
                steps = target - source - 1
                keep = jnp.where(steps >= 0, 1.0, 0.0).astype(F32)
                far = jnp.maximum(steps, 0).astype(F32)
                total = total + (jnp.exp(decay * far) * keep) * states[i]
            out_ref[j, :, lanes] = total.astype(BF)


def far_kernel(got_ref, coeff_ref, rates_ref, near_ref, gate_ref, gain_ref, gained_ref, square_ref):
    ahead = (lax.broadcasted_iota(jnp.int32, (TOK, 128), 0) + 1).astype(F32)
    squares = jnp.zeros((TOK, 128), F32)
    for part in range(CH // 128):
        lanes = slice(part * 128, (part + 1) * 128)
        state = got_ref[0, :, lanes].astype(F32)
        for j in range(1, 8):
            state = state + got_ref[j, :, lanes].astype(F32)
        y = near_ref[:, lanes]
        for n in range(MODES):
            rate = rates_ref[n : n + 1, lanes]
            y = y + jnp.exp(-rate * ahead) * (coeff_ref[n : n + 1, lanes] * state[n : n + 1, :])
        gated = gate_ref[:, lanes] * y
        gained_ref[:, lanes] = gated * gain_ref[:, lanes]
        squares = squares + gated * gated
    total = jnp.broadcast_to(jnp.sum(squares, 1, keepdims=True), (TOK, 128))
    total = jnp.concatenate([total, jnp.zeros((TOK, 128), F32)], 0)
    square_ref[...] = jnp.transpose(total)[:8, :]


def norm_kernel(square_ref, gained_ref, out_ref):
    total = jnp.sum(square_ref[...], 0, keepdims=True)
    total = jnp.transpose(jnp.broadcast_to(total, (128, 128)))[:TOK, :]
    factor = lax.rsqrt(total * (1.0 / DH) + 1e-06)
    for part in range(CH // 128):
        lanes = slice(part * 128, (part + 1) * 128)
        out_ref[:, lanes] = (gained_ref[:, lanes] * factor).astype(BF)


def attend(keys, values, query, mask):
    scores = lax.dot_general(
        keys, query, (((1,), (1,)), ((), ())), preferred_element_type=F32
    ) * (1.0 / math.sqrt(HEAD))
    scores = mask(scores)
    top = jnp.max(scores, 0, keepdims=True)
    weights = jnp.exp(scores - top)
    total = jnp.sum(weights, 0, keepdims=True)
    mixed = lax.dot_general(
        values, weights.astype(BF), (((0,), (0,)), ((), ())), preferred_element_type=F32
    )
    return top, total, mixed


def near_attend_kernel(place_ref, q_ref, own_ref, mixed_ref, stats_ref):
    _, _, z2, w = digits(place_ref[0])
    keys = own_ref[:, :TOK, :].reshape(8 * TOK, HEAD)
    values = own_ref[:, TOK:128, :].reshape(8 * TOK, HEAD)
    row = lax.broadcasted_iota(jnp.int32, (8 * TOK, 1), 0)
    block = row // TOK
    key_pos = ((block // 2) * 8 + (block % 2) * 4 + w) * TOK + row % TOK
    for tile in range(16 * TOK // WIDE):
        query = q_ref[tile * BLOCKS : (tile + 1) * BLOCKS].reshape(WIDE, HEAD)
        lane = lax.broadcasted_iota(jnp.int32, (1, WIDE), 1) + tile * WIDE
        q_block = lane // TOK
        q_pos = ((q_block // 4) * 8 + z2 * 4 + q_block % 4) * TOK + lane % TOK
        top, total, mixed = attend(
            keys, values, query, lambda s: jnp.where(key_pos <= q_pos, s, NEG)
        )
        lanes = slice(tile * WIDE, (tile + 1) * WIDE)
        mixed_ref[:, lanes] = mixed
        stats_ref[0:1, lanes] = top
        stats_ref[1:2, lanes] = total


def far_attend_kernel(place_ref, q_ref, other_ref, mixed_ref, stats_ref, out_ref):
    bias = jnp.where(digits(place_ref[0])[0] == 1, 0.0, NEG).astype(F32)
    keys = other_ref[:, :TOK, :].reshape(8 * TOK, HEAD)
    values = other_ref[:, TOK:, :].reshape(8 * TOK, HEAD)
    which = lax.broadcasted_iota(jnp.int32, (16, 128), 0)
    for tile in range(16 * TOK // WIDE):
        lanes = slice(tile * WIDE, (tile + 1) * WIDE)
        query = q_ref[tile * BLOCKS : (tile + 1) * BLOCKS].reshape(WIDE, HEAD)
        top_b, total_b, mixed_b = attend(keys, values, query, lambda s: s + bias)
        top_a, total_a = stats_ref[0:1, lanes], stats_ref[1:2, lanes]
        top = jnp.maximum(top_a, top_b)
        scale_a, scale_b = jnp.exp(top_a - top), jnp.exp(top_b - top)
        total = total_a * scale_a + total_b * scale_b
        inverse = 1.0 / total
        mixed = mixed_ref[:, lanes] * (scale_a * inverse) + mixed_b * (scale_b * inverse)
        mixed = jnp.transpose(mixed).astype(BF)
        level = top + jnp.log(total)
        high = level.astype(BF).astype(F32)
        rest = level - high
        middle = rest.astype(BF).astype(F32)
        last = rest - middle
        for b in range(BLOCKS):
            place = tile * BLOCKS + b
            out_ref[place, :TOK, :] = mixed[b * TOK : (b + 1) * TOK]
            part = slice((b // 2) * 128, (b // 2) * 128 + 128)
            stats = jnp.where(
                which == 0,
                high[:, part],
                jnp.where(which == 1, middle[:, part], jnp.where(which == 2, last[:, part], 0.0)),
            )
            out_ref[place, TOK:, :] = stats.astype(BF)


def merge_kernel(place_ref, got_ref, out_ref):
    odd = place_ref[0] % 2
    levels = jnp.concatenate(
        [jnp.sum(got_ref[k, TOK : TOK + 16, :].astype(F32), 0, keepdims=True) for k in range(16)], 0
    )
    levels = jnp.where(odd == 1, pltpu.roll(levels, TOK, 1), levels)
    weights = []
    for h in range(HEADS_DEV):
        part = levels[h * 4 : (h + 1) * 4]
        part = jnp.exp(part - jnp.max(part, 0, keepdims=True))
        weights.append(part / jnp.sum(part, 0, keepdims=True))
    weights = jnp.concatenate(weights + [jnp.zeros((112, 128), F32)], 0)
    weights = jnp.transpose(weights)[:TOK, :]
    for h in range(HEADS_DEV):
        total = jnp.zeros((TOK, HEAD), F32)
        for k in range(4):
            place = h * 4 + k
            total = total + weights[:, place : place + 1] * got_ref[place, :TOK, :].astype(F32)
        out_ref[:, h * HEAD : (h + 1) * HEAD] = total.astype(BF)


def exchange(value, groups):
    return lax.all_to_all(value, "context", 0, 0, axis_index_groups=groups, tiled=True)


def local(features, feat_weight, skip, residues, rates, norm_gain, attn_in):
    index = lax.axis_index("context")
    devices = lax.axis_size("context")
    place = index.astype(jnp.int32)[None]
    features = jnp.transpose(features, (1, 0, 2))
    attn_in = jnp.transpose(attn_in, (1, 0, 2))
    rim = lax.ppermute(
        features[:, TOK - (FEAT - 1) :], "context", [(s, s + 1) for s in range(devices - 1)]
    )

    coeff = residues * jnp.sqrt(-jnp.expm1(-2.0 * rates))
    inverse = jnp.exp(
        jnp.arange(HEAD // 2, dtype=F32) * (-2.0 * math.log(ROPE_BASE) / HEAD)
    )
    positions = (index * TOK + jnp.arange(TOK)).astype(F32)
    angle = positions[:, None] * inverse[None, :]
    cosine, sine = jnp.cos(angle), jnp.sin(angle)
    cosine = jnp.concatenate([cosine, cosine], 1)
    sine = jnp.concatenate([-sine, sine], 1)

    queries, pairs = call(
        rotate_kernel,
        [((16, TOK, HEAD), BF), ((HEADS_DEV, 2 * TOK, HEAD), BF)],
        [VMEM] * 3,
        1000000000,
    )(attn_in, cosine, sine)
    queries = exchange(queries, Q_GROUPS)

    rim = jnp.pad(rim.astype(F32), ((0, 0), (6, 0), (0, 0)))
    sent, gate, product = call(
        state_kernel,
        [((8, 192, HEAD), BF), ((TOK, CH), F32), ((TOK, CH), F32)],
        [VMEM] * 5,
        2000000000,
    )(features, rim, feat_weight, rates, pairs)
    queries, sent = lax.optimization_barrier((queries, sent))
    got = exchange(sent, KV_GROUPS)

    (near,) = call(
        near_kernel,
        [((TOK, CH), F32)],
        [VMEM] * 4,
        2000000000,
        [pltpu.VMEM((2 * TOK, CH), F32), pltpu.VMEM((TOK, CH), F32)],
    )(product, coeff, rates, skip[None, :])
    near, got = lax.optimization_barrier((near, got))
    other = lax.ppermute(
        got[:, :128], "context", [(s, s + devices // 2) for s in range(devices // 2)]
    )
    (messages,) = call(
        message_kernel, [((8, MODES, CH), BF)], [SMEM, VMEM, VMEM], 1000000000
    )(place, got, rates)
    arrived = exchange(messages, STATE_GROUPS)

    mixed, stats = call(
        near_attend_kernel,
        [((HEAD, 16 * TOK), F32), ((8, 16 * TOK), F32)],
        [SMEM, VMEM, VMEM],
        2000000000,
    )(place, queries, got)
    gained, squares = call(
        far_kernel,
        [((TOK, CH), F32), ((8, 128), F32)],
        [VMEM] * 6,
        1000000000,
    )(arrived, coeff, rates, near, gate, norm_gain[None, :])
    squares = lax.all_to_all(squares, "dp", 0, 0, tiled=True)
    (partial,) = call(
        far_attend_kernel,
        [((16, TOK + 16, HEAD), BF)],
        [SMEM, VMEM, VMEM, VMEM, VMEM],
        2000000000,
    )(place, queries, other, mixed, stats)
    partial = exchange(partial, Q_GROUPS)
    (hyena_out,) = call(norm_kernel, [((TOK, CH), BF)], [VMEM] * 2, 100000000)(squares, gained)
    (attn_out,) = call(merge_kernel, [((TOK, CH), BF)], [SMEM, VMEM], 1000000000)(place, partial)
    return (hyena_out, attn_out)


def solution(mesh):
    return jax.shard_map(
        local,
        mesh=mesh,
        in_specs=(
            P("context", None, "dp"),
            P(None, None, "dp"),
            P("dp"),
            P(None, "dp"),
            P(None, "dp"),
            P("dp"),
            P("context", None, "dp"),
        ),
        out_specs=(P("context", "dp"), P("context", "dp")),
        check_vma=False,
    )
```

```python
import functools
import itertools
import math

import jax
import jax.numpy as jnp
from jax import lax
from jax.experimental import pallas as pl
from jax.experimental.pallas import tpu as pltpu
from jax.sharding import PartitionSpec as P

DH = 4096
HEAD = 128
HEADS_DEV = 4
FEAT = 3
MODES = 16
TOK = 64
CH = 512
ROPE_BASE = 1000000.0
NEG = -1e30
WIDE = 256
BLOCKS = WIDE // TOK
BF = jnp.bfloat16
F32 = jnp.float32

DIGITS = {"y": (2, 32), "x": (4, 8), "z2": (2, 4), "w": (4, 1)}


def groups_over(*free):
    fixed = [d for d in DIGITS if d not in free]

    def places(names):
        return [
            sum(v * DIGITS[d][1] for v, d in zip(values, names))
            for values in itertools.product(*[range(DIGITS[d][0]) for d in names])
        ]

    return [[base + step for step in places(free)] for base in places(fixed)]


Q_GROUPS = groups_over("x", "w")
KV_GROUPS = groups_over("x", "z2")
STATE_GROUPS = groups_over("y", "w")

VMEM = pl.BlockSpec(memory_space=pltpu.VMEM)
SMEM = pl.BlockSpec(memory_space=pltpu.SMEM)


def call(kernel, outs, specs, flops, scratch=()):
    return pl.pallas_call(
        kernel,
        out_shape=[jax.ShapeDtypeStruct(s, d) for s, d in outs],
        in_specs=specs,
        out_specs=[VMEM] * len(outs),
        scratch_shapes=list(scratch),
        compiler_params=pltpu.CompilerParams(vmem_limit_bytes=16 * 1024 * 1024),
        cost_estimate=pl.CostEstimate(flops=flops, bytes_accessed=1000, transcendentals=0),
    )


def digits(index):
    return [(index // step) % size for size, step in DIGITS.values()]


def expand(rates, weights, start):
    ahead = (lax.broadcasted_iota(jnp.int32, (8, 128), 0) + start).astype(F32)
    bases = [jnp.exp(-rates[n : n + 1, :] * ahead) for n in range(MODES)]
    tiles = []
    for a in range(8):
        scaled = weights * jnp.exp(rates * (-8.0 * a))
        tiles.append(sum(bases[n] * scaled[n : n + 1, :] for n in range(MODES)))
    return tiles


def rotate_kernel(attn_ref, cos_ref, sin_ref, q_ref, kv_ref):
    cosine, sine = cos_ref[...], sin_ref[...]
    for g in range(2):
        x = attn_ref[g].astype(F32)
        for h in range(HEADS_DEV):
            part = x[:, h * HEAD : (h + 1) * HEAD]
            turned = (part * cosine + pltpu.roll(part, HEAD // 2, 1) * sine).astype(BF)
            if g == 0:
                for w in range(4):
                    q_ref[h * 4 + w] = turned
            else:
                kv_ref[h, :TOK, :] = turned
    for h in range(HEADS_DEV):
        kv_ref[h, TOK:, :] = attn_ref[2, :, h * HEAD : (h + 1) * HEAD]


def state_kernel(feat_ref, rim_ref, weight_ref, rates_ref, kv_ref, sent_ref, gate_ref, prod_ref):
    groups = []
    for g in range(3):
        x = jnp.concatenate([rim_ref[g], feat_ref[g].astype(F32)], 0)
        total = weight_ref[0, g : g + 1, :] * x[8 : 8 + TOK]
        for o in range(1, FEAT):
            total = total + weight_ref[o, g : g + 1, :] * x[8 - o : 8 - o + TOK]
        groups.append(total)
    gate_ref[...] = groups[0]
    product = (groups[1] * groups[2]).astype(BF).astype(F32)
    prod_ref[...] = product
    back = (7 - lax.broadcasted_iota(jnp.int32, (8, 128), 0)).astype(F32)
    for part in range(CH // 128):
        lanes = slice(part * 128, (part + 1) * 128)
        step = jnp.exp(-8.0 * rates_ref[:, lanes])
        rows = []
        for n in range(MODES):
            total = product[:8, lanes]
            for a in range(1, 8):
                total = total * step[n : n + 1, :] + product[8 * a : 8 * a + 8, lanes]
            total = total * jnp.exp(-rates_ref[n : n + 1, lanes] * back)
            rows.append(jnp.sum(total, 0, keepdims=True))
        state = jnp.concatenate(rows, 0).astype(BF)
        for peer in range(8):
            sent_ref[peer, 128 + part * 16 : 144 + part * 16, :] = state
    for x in range(4):
        for z2 in range(2):
            sent_ref[x * 2 + z2, :128, :] = kv_ref[x]


def near_kernel(prod_ref, coeff_ref, rates_ref, skip_ref, out_ref, padded, impulse):
    padded[:TOK, :] = jnp.zeros((TOK, CH), F32)
    padded[TOK:, :] = prod_ref[...]
    for part in range(CH // 128):
        lanes = slice(part * 128, (part + 1) * 128)
        rows = expand(rates_ref[:, lanes], coeff_ref[:, lanes], 0)
        for a in range(8):
            impulse[8 * a : 8 * a + 8, lanes] = rows[a]
        y = skip_ref[:, lanes] * prod_ref[:, lanes]
        for t in range(TOK):
            y = y + impulse[t : t + 1, lanes] * padded[TOK - t : 2 * TOK - t, lanes]
        out_ref[:, lanes] = y


def message_kernel(place_ref, got_ref, rates_ref, out_ref):
    y, x, z2, w = digits(place_ref[0])
    gaps = [8 * (x - i // 2) + 4 * (z2 - i % 2) for i in range(8)]
    for part in range(CH // 128):
        lanes = slice(part * 128, (part + 1) * 128)
        decay = rates_ref[:, lanes] * (-float(TOK))

        def faded(steps):
            return jnp.exp(decay * jnp.maximum(steps, 0).astype(F32))

        before = jnp.zeros((MODES, 128), F32)
        whole = jnp.zeros((MODES, 128), F32)
        own = jnp.zeros((MODES, 128), F32)
        for i, gap in enumerate(gaps):
            state = got_ref[i, 128 + part * 16 : 144 + part * 16, :].astype(F32)
            before = before + jnp.where(gap > 0, 1.0, 0.0).astype(F32) * faded(gap - 4) * state
            own = own + jnp.where(gap == 0, 1.0, 0.0).astype(F32) * state
            whole = whole + faded(gap + 28) * state
        for other in range(4):
            reach = faded(other - w + 3)
            same = reach * before + jnp.where(other > w, 1.0, 0.0).astype(F32) * faded(other - w - 1) * own
            cross = reach * whole
            out_ref[other, :, lanes] = jnp.where(y == 0, same, 0.0).astype(BF)
            out_ref[4 + other, :, lanes] = jnp.where(y == 0, cross, same).astype(BF)


def far_kernel(got_ref, coeff_ref, rates_ref, near_ref, gate_ref, gain_ref, gained_ref, square_ref):
    squares = jnp.zeros((TOK, 128), F32)
    for part in range(CH // 128):
        lanes = slice(part * 128, (part + 1) * 128)
        state = got_ref[0, :, lanes].astype(F32)
        for j in range(1, 8):
            state = state + got_ref[j, :, lanes].astype(F32)
        tiles = expand(rates_ref[:, lanes], coeff_ref[:, lanes] * state, 1)
        gated = gate_ref[:, lanes] * (near_ref[:, lanes] + jnp.concatenate(tiles, 0))
        gained_ref[:, lanes] = gated * gain_ref[:, lanes]
        squares = squares + gated * gated
    total = jnp.broadcast_to(jnp.sum(squares, 1, keepdims=True), (TOK, 128))
    total = jnp.concatenate([total, jnp.zeros((TOK, 128), F32)], 0)
    square_ref[...] = jnp.transpose(total)[:8, :]


def norm_kernel(square_ref, gained_ref, out_ref):
    total = jnp.sum(square_ref[...], 0, keepdims=True)
    total = jnp.transpose(jnp.broadcast_to(total, (128, 128)))[:TOK, :]
    factor = lax.rsqrt(total * (1.0 / DH) + 1e-06)
    for part in range(CH // 128):
        lanes = slice(part * 128, (part + 1) * 128)
        out_ref[:, lanes] = (gained_ref[:, lanes] * factor).astype(BF)


def attend(keys, values, query, mask):
    scores = lax.dot_general(
        keys, query, (((1,), (1,)), ((), ())), preferred_element_type=F32
    ) * (1.0 / math.sqrt(HEAD))
    scores = mask(scores)
    top = jnp.max(scores, 0, keepdims=True)
    weights = jnp.exp(scores - top)
    total = jnp.sum(weights, 0, keepdims=True)
    mixed = lax.dot_general(
        values, weights.astype(BF), (((0,), (0,)), ((), ())), preferred_element_type=F32
    )
    return top, total, mixed


def near_attend_kernel(place_ref, q_ref, own_ref, mixed_ref, stats_ref):
    _, _, z2, w = digits(place_ref[0])
    keys = own_ref[:, :TOK, :].reshape(8 * TOK, HEAD)
    values = own_ref[:, TOK:128, :].reshape(8 * TOK, HEAD)
    row = lax.broadcasted_iota(jnp.int32, (8 * TOK, 1), 0)
    block = row // TOK
    key_pos = ((block // 2) * 8 + (block % 2) * 4 + w) * TOK + row % TOK
    for tile in range(16 * TOK // WIDE):
        query = q_ref[tile * BLOCKS : (tile + 1) * BLOCKS].reshape(WIDE, HEAD)
        lane = lax.broadcasted_iota(jnp.int32, (1, WIDE), 1) + tile * WIDE
        q_block = lane // TOK
        q_pos = ((q_block // 4) * 8 + z2 * 4 + q_block % 4) * TOK + lane % TOK
        top, total, mixed = attend(
            keys, values, query, lambda s: jnp.where(key_pos <= q_pos, s, NEG)
        )
        lanes = slice(tile * WIDE, (tile + 1) * WIDE)
        mixed_ref[:, lanes] = mixed
        stats_ref[0:1, lanes] = top
        stats_ref[1:2, lanes] = total


def far_attend_kernel(place_ref, q_ref, other_ref, mixed_ref, stats_ref, out_ref):
    bias = jnp.where(digits(place_ref[0])[0] == 1, 0.0, NEG).astype(F32)
    keys = other_ref[:, :TOK, :].reshape(8 * TOK, HEAD)
    values = other_ref[:, TOK:, :].reshape(8 * TOK, HEAD)
    which = lax.broadcasted_iota(jnp.int32, (16, 128), 0)
    for tile in range(16 * TOK // WIDE):
        lanes = slice(tile * WIDE, (tile + 1) * WIDE)
        query = q_ref[tile * BLOCKS : (tile + 1) * BLOCKS].reshape(WIDE, HEAD)
        top_b, total_b, mixed_b = attend(keys, values, query, lambda s: s + bias)
        top_a, total_a = stats_ref[0:1, lanes], stats_ref[1:2, lanes]
        top = jnp.maximum(top_a, top_b)
        scale_a, scale_b = jnp.exp(top_a - top), jnp.exp(top_b - top)
        total = total_a * scale_a + total_b * scale_b
        inverse = 1.0 / total
        mixed = mixed_ref[:, lanes] * (scale_a * inverse) + mixed_b * (scale_b * inverse)
        mixed = jnp.transpose(mixed).astype(BF)
        level = top + jnp.log(total)
        high = level.astype(BF).astype(F32)
        rest = level - high
        middle = rest.astype(BF).astype(F32)
        last = rest - middle
        for b in range(BLOCKS):
            place = tile * BLOCKS + b
            out_ref[place, :TOK, :] = mixed[b * TOK : (b + 1) * TOK]
            part = slice((b // 2) * 128, (b // 2) * 128 + 128)
            stats = jnp.where(
                which == 0,
                high[:, part],
                jnp.where(which == 1, middle[:, part], jnp.where(which == 2, last[:, part], 0.0)),
            )
            out_ref[place, TOK:, :] = stats.astype(BF)


def merge_kernel(place_ref, got_ref, out_ref):
    odd = place_ref[0] % 2
    levels = jnp.sum(got_ref[:, TOK:, :].astype(F32), 1)
    levels = jnp.where(odd == 1, pltpu.roll(levels, TOK, 1), levels)
    weights = []
    for h in range(HEADS_DEV):
        part = levels[h * 4 : (h + 1) * 4]
        part = jnp.exp(part - jnp.max(part, 0, keepdims=True))
        weights.append(part / jnp.sum(part, 0, keepdims=True))
    weights = jnp.concatenate(weights + [jnp.zeros((112, 128), F32)], 0)
    weights = jnp.transpose(weights)[:TOK, :]
    for h in range(HEADS_DEV):
        total = jnp.zeros((TOK, HEAD), F32)
        for k in range(4):
            place = h * 4 + k
            total = total + weights[:, place : place + 1] * got_ref[place, :TOK, :].astype(F32)
        out_ref[:, h * HEAD : (h + 1) * HEAD] = total.astype(BF)


def exchange(value, groups):
    return lax.all_to_all(value, "context", 0, 0, axis_index_groups=groups, tiled=True)


def local(features, feat_weight, skip, residues, rates, norm_gain, attn_in):
    index = lax.axis_index("context")
    devices = lax.axis_size("context")
    place = index.astype(jnp.int32)[None]
    features = jnp.transpose(features, (1, 0, 2))
    attn_in = jnp.transpose(attn_in, (1, 0, 2))
    rim = lax.ppermute(
        features[:, TOK - (FEAT - 1) :], "context", [(s, s + 1) for s in range(devices - 1)]
    )

    coeff = residues * jnp.sqrt(-jnp.expm1(-2.0 * rates))
    inverse = jnp.exp(
        jnp.arange(HEAD // 2, dtype=F32) * (-2.0 * math.log(ROPE_BASE) / HEAD)
    )
    positions = (index * TOK + jnp.arange(TOK)).astype(F32)
    angle = positions[:, None] * inverse[None, :]
    cosine, sine = jnp.cos(angle), jnp.sin(angle)
    cosine = jnp.concatenate([cosine, cosine], 1)
    sine = jnp.concatenate([-sine, sine], 1)

    queries, pairs = call(
        rotate_kernel,
        [((16, TOK, HEAD), BF), ((HEADS_DEV, 2 * TOK, HEAD), BF)],
        [VMEM] * 3,
        1000000000,
    )(attn_in, cosine, sine)
    queries = exchange(queries, Q_GROUPS)

    rim = jnp.pad(rim.astype(F32), ((0, 0), (6, 0), (0, 0)))
    sent, gate, product = call(
        state_kernel,
        [((8, 192, HEAD), BF), ((TOK, CH), F32), ((TOK, CH), F32)],
        [VMEM] * 5,
        20000000000,
    )(features, rim, feat_weight, rates, pairs)
    queries, sent, coeff = lax.optimization_barrier((queries, sent, coeff))
    got = exchange(sent, KV_GROUPS)

    product, got = lax.optimization_barrier((product, got))
    (near,) = call(
        near_kernel,
        [((TOK, CH), F32)],
        [VMEM] * 4,
        2000000000,
        [pltpu.VMEM((2 * TOK, CH), F32), pltpu.VMEM((TOK, CH), F32)],
    )(product, coeff, rates, skip[None, :])
    other = lax.ppermute(
        got[:, :128], "context", [(s, s + devices // 2) for s in range(devices // 2)]
    )
    (messages,) = call(
        message_kernel, [((8, MODES, CH), BF)], [SMEM, VMEM, VMEM], 1000000000
    )(place, got, rates)
    arrived = exchange(messages, STATE_GROUPS)

    mixed, stats = call(
        near_attend_kernel,
        [((HEAD, 16 * TOK), F32), ((8, 16 * TOK), F32)],
        [SMEM, VMEM, VMEM],
        200000000,
    )(place, queries, got)
    gained, squares = call(
        far_kernel,
        [((TOK, CH), F32), ((8, 128), F32)],
        [VMEM] * 6,
        1000000000,
    )(arrived, coeff, rates, near, gate, norm_gain[None, :])
    squares = lax.all_to_all(squares, "dp", 0, 0, tiled=True)
    (partial,) = call(
        far_attend_kernel,
        [((16, TOK + 16, HEAD), BF)],
        [SMEM, VMEM, VMEM, VMEM, VMEM],
        20000000000,
    )(place, queries, other, mixed, stats)
    partial = exchange(partial, Q_GROUPS)
    (hyena_out,) = call(norm_kernel, [((TOK, CH), BF)], [VMEM] * 2, 100000000)(squares, gained)
    (attn_out,) = call(merge_kernel, [((TOK, CH), BF)], [SMEM, VMEM], 1000000000)(place, partial)
    return (hyena_out, attn_out)


def solution(mesh):
    return jax.shard_map(
        local,
        mesh=mesh,
        in_specs=(
            P("context", None, "dp"),
            P(None, None, "dp"),
            P("dp"),
            P(None, "dp"),
            P(None, "dp"),
            P("dp"),
            P("context", None, "dp"),
        ),
        out_specs=(P("context", "dp"), P("context", "dp")),
        check_vma=False,
    )
```

```python
import functools
import itertools
import math

import jax
import jax.numpy as jnp
from jax import lax
from jax.experimental import pallas as pl
from jax.experimental.pallas import tpu as pltpu
from jax.sharding import PartitionSpec as P

DH = 4096
HEAD = 128
HEADS_DEV = 4
FEAT = 3
MODES = 16
TOK = 64
CH = 512
ROPE_BASE = 1000000.0
NEG = -1e30
WIDE = 256
BLOCKS = WIDE // TOK
BF = jnp.bfloat16
F32 = jnp.float32

DIGITS = {"y": (2, 32), "x": (4, 8), "z2": (2, 4), "w": (4, 1)}


def groups_over(*free):
    fixed = [d for d in DIGITS if d not in free]

    def places(names):
        return [
            sum(v * DIGITS[d][1] for v, d in zip(values, names))
            for values in itertools.product(*[range(DIGITS[d][0]) for d in names])
        ]

    return [[base + step for step in places(free)] for base in places(fixed)]


Q_GROUPS = groups_over("x", "w")
KV_GROUPS = groups_over("x", "z2")

VMEM = pl.BlockSpec(memory_space=pltpu.VMEM)
SMEM = pl.BlockSpec(memory_space=pltpu.SMEM)


def call(kernel, outs, specs, flops, scratch=()):
    return pl.pallas_call(
        kernel,
        out_shape=[jax.ShapeDtypeStruct(s, d) for s, d in outs],
        in_specs=specs,
        out_specs=[VMEM] * len(outs),
        scratch_shapes=list(scratch),
        compiler_params=pltpu.CompilerParams(vmem_limit_bytes=16 * 1024 * 1024),
        cost_estimate=pl.CostEstimate(flops=flops, bytes_accessed=1000, transcendentals=0),
    )


def digits(index):
    return [(index // step) % size for size, step in DIGITS.values()]


def expand(rates, weights, start):
    ahead = (lax.broadcasted_iota(jnp.int32, (8, 128), 0) + start).astype(F32)
    bases = [jnp.exp(-rates[n : n + 1, :] * ahead) for n in range(MODES)]
    tiles = []
    for a in range(8):
        scaled = weights * jnp.exp(rates * (-8.0 * a))
        tiles.append(sum(bases[n] * scaled[n : n + 1, :] for n in range(MODES)))
    return tiles


def rotate_kernel(attn_ref, cos_ref, sin_ref, q_ref, kv_ref):
    cosine, sine = cos_ref[...], sin_ref[...]
    for g in range(2):
        x = attn_ref[g].astype(F32)
        for h in range(HEADS_DEV):
            part = x[:, h * HEAD : (h + 1) * HEAD]
            turned = (part * cosine + pltpu.roll(part, HEAD // 2, 1) * sine).astype(BF)
            if g == 0:
                for w in range(4):
                    q_ref[h * 4 + w] = turned
            else:
                kv_ref[h, :TOK, :] = turned
    for h in range(HEADS_DEV):
        kv_ref[h, TOK:, :] = attn_ref[2, :, h * HEAD : (h + 1) * HEAD]


def state_kernel(feat_ref, rim_ref, weight_ref, rates_ref, kv_ref, sent_ref, gate_ref, prod_ref):
    groups = []
    for g in range(3):
        x = jnp.concatenate([rim_ref[g], feat_ref[g].astype(F32)], 0)
        total = weight_ref[0, g : g + 1, :] * x[8 : 8 + TOK]
        for o in range(1, FEAT):
            total = total + weight_ref[o, g : g + 1, :] * x[8 - o : 8 - o + TOK]
        groups.append(total)
    gate_ref[...] = groups[0]
    product = (groups[1] * groups[2]).astype(BF).astype(F32)
    prod_ref[...] = product
    back = (7 - lax.broadcasted_iota(jnp.int32, (8, 128), 0)).astype(F32)
    for part in range(CH // 128):
        lanes = slice(part * 128, (part + 1) * 128)
        step = jnp.exp(-8.0 * rates_ref[:, lanes])
        rows = []
        for n in range(MODES):
            total = product[:8, lanes]
            for a in range(1, 8):
                total = total * step[n : n + 1, :] + product[8 * a : 8 * a + 8, lanes]
            total = total * jnp.exp(-rates_ref[n : n + 1, lanes] * back)
            rows.append(jnp.sum(total, 0, keepdims=True))
        state = jnp.concatenate(rows, 0).astype(BF)
        for peer in range(8):
            sent_ref[peer, 128 + part * 16 : 144 + part * 16, :] = state
    for x in range(4):
        for z2 in range(2):
            sent_ref[x * 2 + z2, :128, :] = kv_ref[x]


def near_kernel(prod_ref, coeff_ref, rates_ref, skip_ref, out_ref, padded, impulse):
    padded[:TOK, :] = jnp.zeros((TOK, CH), F32)
    padded[TOK:, :] = prod_ref[...]
    for part in range(CH // 128):
        lanes = slice(part * 128, (part + 1) * 128)
        rows = expand(rates_ref[:, lanes], coeff_ref[:, lanes], 0)
        for a in range(8):
            impulse[8 * a : 8 * a + 8, lanes] = rows[a]
        y = skip_ref[:, lanes] * prod_ref[:, lanes]
        for t in range(TOK):
            y = y + impulse[t : t + 1, lanes] * padded[TOK - t : 2 * TOK - t, lanes]
        out_ref[:, lanes] = y


def write_messages(index, own_ref, other_ref, rates_ref, out_ref):
    y, x, z2, w = digits(index)
    rows = pl.ds(pl.multiple_of(128 + x * 16, 16), 16)
    decay = rates_ref[x] * (-float(TOK))
    second = jnp.where(y == 1, 1.0, 0.0).astype(F32)

    def faded(steps):
        return jnp.exp(decay * jnp.maximum(steps, 0).astype(F32))

    def when(condition):
        return jnp.where(condition, 1.0, 0.0).astype(F32)

    own_states = [own_ref[i, rows, :].astype(F32) for i in range(8)]
    other_states = [other_ref[i, rows, :].astype(F32) * second for i in range(8)]
    reach = [faded(wt - w + 3) for wt in range(4)]
    step = [faded(wt - w - 1) * when(wt > w) for wt in range(4)]
    for xt in range(4):
        before = jnp.zeros((MODES, 128), F32)
        own = jnp.zeros((MODES, 128), F32)
        for i in range(8):
            gap = 8 * (xt - i // 2) + 4 * (z2 - i % 2)
            before = before + when(gap > 0) * faded(gap - 4) * own_states[i]
            before = before + faded(gap + 28) * other_states[i]
            own = own + when(gap == 0) * own_states[i]
        for wt in range(4):
            out_ref[xt * 4 + wt, 80:96, :] = (reach[wt] * before + step[wt] * own).astype(BF)


def far_kernel(got_ref, coeff_ref, rates_ref, near_ref, gate_ref, gain_ref, gained_ref, square_ref):
    squares = jnp.zeros((TOK, 128), F32)
    for part in range(CH // 128):
        lanes = slice(part * 128, (part + 1) * 128)
        state = got_ref[part * 4, 80:96, :].astype(F32)
        for j in range(1, 4):
            state = state + got_ref[part * 4 + j, 80:96, :].astype(F32)
        tiles = expand(rates_ref[:, lanes], coeff_ref[:, lanes] * state, 1)
        gated = gate_ref[:, lanes] * (near_ref[:, lanes] + jnp.concatenate(tiles, 0))
        gained_ref[:, lanes] = gated * gain_ref[:, lanes]
        squares = squares + gated * gated
    total = jnp.broadcast_to(jnp.sum(squares, 1, keepdims=True), (TOK, 128))
    total = jnp.concatenate([total, jnp.zeros((TOK, 128), F32)], 0)
    square_ref[...] = jnp.transpose(total)[:8, :]


def norm_kernel(square_ref, gained_ref, out_ref):
    total = jnp.sum(square_ref[...], 0, keepdims=True)
    total = jnp.transpose(jnp.broadcast_to(total, (128, 128)))[:TOK, :]
    factor = lax.rsqrt(total * (1.0 / DH) + 1e-06)
    for part in range(CH // 128):
        lanes = slice(part * 128, (part + 1) * 128)
        out_ref[:, lanes] = (gained_ref[:, lanes] * factor).astype(BF)


def attend(keys, values, query, mask):
    scores = lax.dot_general(
        keys, query, (((1,), (1,)), ((), ())), preferred_element_type=F32
    ) * (1.0 / math.sqrt(HEAD))
    scores = mask(scores)
    top = jnp.max(scores, 0, keepdims=True)
    weights = jnp.exp(scores - top)
    total = jnp.sum(weights, 0, keepdims=True)
    mixed = lax.dot_general(
        values, weights.astype(BF), (((0,), (0,)), ((), ())), preferred_element_type=F32
    )
    return top, total, mixed


def near_attend_kernel(place_ref, q_ref, own_ref, mixed_ref, stats_ref):
    _, _, z2, w = digits(place_ref[0])
    keys = own_ref[:, :TOK, :].reshape(8 * TOK, HEAD)
    values = own_ref[:, TOK:128, :].reshape(8 * TOK, HEAD)
    row = lax.broadcasted_iota(jnp.int32, (8 * TOK, 1), 0)
    block = row // TOK
    key_pos = ((block // 2) * 8 + (block % 2) * 4 + w) * TOK + row % TOK
    for tile in range(16 * TOK // WIDE):
        query = q_ref[tile * BLOCKS : (tile + 1) * BLOCKS].reshape(WIDE, HEAD)
        lane = lax.broadcasted_iota(jnp.int32, (1, WIDE), 1) + tile * WIDE
        q_block = lane // TOK
        q_pos = ((q_block // 4) * 8 + z2 * 4 + q_block % 4) * TOK + lane % TOK
        top, total, mixed = attend(
            keys, values, query, lambda s: jnp.where(key_pos <= q_pos, s, NEG)
        )
        lanes = slice(tile * WIDE, (tile + 1) * WIDE)
        mixed_ref[:, lanes] = mixed
        stats_ref[0:1, lanes] = top
        stats_ref[1:2, lanes] = total


def far_attend_kernel(
    place_ref, q_ref, own_ref, other_ref, mixed_ref, stats_ref, rates_ref, out_ref
):
    bias = jnp.where(digits(place_ref[0])[0] == 1, 0.0, NEG).astype(F32)
    keys = other_ref[:, :TOK, :].reshape(8 * TOK, HEAD)
    values = other_ref[:, TOK:128, :].reshape(8 * TOK, HEAD)
    write_messages(place_ref[0], own_ref, other_ref, rates_ref, out_ref)
    which = lax.broadcasted_iota(jnp.int32, (16, 128), 0)
    for tile in range(16 * TOK // WIDE):
        lanes = slice(tile * WIDE, (tile + 1) * WIDE)
        query = q_ref[tile * BLOCKS : (tile + 1) * BLOCKS].reshape(WIDE, HEAD)
        top_b, total_b, mixed_b = attend(keys, values, query, lambda s: s + bias)
        top_a, total_a = stats_ref[0:1, lanes], stats_ref[1:2, lanes]
        top = jnp.maximum(top_a, top_b)
        scale_a, scale_b = jnp.exp(top_a - top), jnp.exp(top_b - top)
        total = total_a * scale_a + total_b * scale_b
        inverse = 1.0 / total
        mixed = mixed_ref[:, lanes] * (scale_a * inverse) + mixed_b * (scale_b * inverse)
        mixed = jnp.transpose(mixed).astype(BF)
        level = top + jnp.log(total)
        high = level.astype(BF).astype(F32)
        rest = level - high
        middle = rest.astype(BF).astype(F32)
        last = rest - middle
        for b in range(BLOCKS):
            place = tile * BLOCKS + b
            out_ref[place, :TOK, :] = mixed[b * TOK : (b + 1) * TOK]
            part = slice((b // 2) * 128, (b // 2) * 128 + 128)
            stats = jnp.where(
                which == 0,
                high[:, part],
                jnp.where(which == 1, middle[:, part], jnp.where(which == 2, last[:, part], 0.0)),
            )
            out_ref[place, TOK:80, :] = stats.astype(BF)


def merge_kernel(place_ref, got_ref, out_ref):
    odd = place_ref[0] % 2
    levels = jnp.sum(got_ref[:, TOK:80, :].astype(F32), 1)
    levels = jnp.where(odd == 1, pltpu.roll(levels, TOK, 1), levels)
    weights = []
    for h in range(HEADS_DEV):
        part = levels[h * 4 : (h + 1) * 4]
        part = jnp.exp(part - jnp.max(part, 0, keepdims=True))
        weights.append(part / jnp.sum(part, 0, keepdims=True))
    weights = jnp.concatenate(weights + [jnp.zeros((112, 128), F32)], 0)
    weights = jnp.transpose(weights)[:TOK, :]
    for h in range(HEADS_DEV):
        total = jnp.zeros((TOK, HEAD), F32)
        for k in range(4):
            place = h * 4 + k
            total = total + weights[:, place : place + 1] * got_ref[place, :TOK, :].astype(F32)
        out_ref[:, h * HEAD : (h + 1) * HEAD] = total.astype(BF)


def exchange(value, groups):
    return lax.all_to_all(value, "context", 0, 0, axis_index_groups=groups, tiled=True)


def local(features, feat_weight, skip, residues, rates, norm_gain, attn_in):
    index = lax.axis_index("context")
    devices = lax.axis_size("context")
    place = index.astype(jnp.int32)[None]
    features = jnp.transpose(features, (1, 0, 2))
    attn_in = jnp.transpose(attn_in, (1, 0, 2))
    rim = lax.ppermute(
        features[:, TOK - (FEAT - 1) :], "context", [(s, s + 1) for s in range(devices - 1)]
    )

    coeff = residues * jnp.sqrt(-jnp.expm1(-2.0 * rates))
    inverse = jnp.exp(
        jnp.arange(HEAD // 2, dtype=F32) * (-2.0 * math.log(ROPE_BASE) / HEAD)
    )
    positions = (index * TOK + jnp.arange(TOK)).astype(F32)
    angle = positions[:, None] * inverse[None, :]
    cosine, sine = jnp.cos(angle), jnp.sin(angle)
    cosine = jnp.concatenate([cosine, cosine], 1)
    sine = jnp.concatenate([-sine, sine], 1)

    queries, pairs = call(
        rotate_kernel,
        [((16, TOK, HEAD), BF), ((HEADS_DEV, 2 * TOK, HEAD), BF)],
        [VMEM] * 3,
        1000000000,
    )(attn_in, cosine, sine)
    queries = exchange(queries, Q_GROUPS)

    rim = jnp.pad(rim.astype(F32), ((0, 0), (6, 0), (0, 0)))
    sent, gate, product = call(
        state_kernel,
        [((8, 192, HEAD), BF), ((TOK, CH), F32), ((TOK, CH), F32)],
        [VMEM] * 5,
        20000000000,
    )(features, rim, feat_weight, rates, pairs)
    quarters = jnp.transpose(rates.reshape(MODES, CH // 128, 128), (1, 0, 2))
    queries, sent, coeff, quarters, skip, gain = lax.optimization_barrier(
        (queries, sent, coeff, quarters, skip[None, :], norm_gain[None, :])
    )
    got = exchange(sent, KV_GROUPS)
    product, got = lax.optimization_barrier((product, got))

    other = lax.ppermute(got, "context", [(s, s + devices // 2) for s in range(devices // 2)])
    mixed, stats = call(
        near_attend_kernel,
        [((HEAD, 16 * TOK), F32), ((8, 16 * TOK), F32)],
        [SMEM, VMEM, VMEM],
        200000000,
    )(place, queries, got)
    (near,) = call(
        near_kernel,
        [((TOK, CH), F32)],
        [VMEM] * 4,
        200000000,
        [pltpu.VMEM((2 * TOK, CH), F32), pltpu.VMEM((TOK, CH), F32)],
    )(product, coeff, rates, skip)
    near, other = lax.optimization_barrier((near, other))
    (partial,) = call(
        far_attend_kernel,
        [((16, TOK + 32, HEAD), BF)],
        [SMEM] + [VMEM] * 6,
        20000000000,
    )(place, queries, got, other, mixed, stats, quarters)
    partial = exchange(partial, Q_GROUPS)

    gained, squares = call(
        far_kernel,
        [((TOK, CH), F32), ((8, 128), F32)],
        [VMEM] * 6,
        1000000000,
    )(partial, coeff, rates, near, gate, gain)
    squares = lax.all_to_all(squares, "dp", 0, 0, tiled=True)
    (attn_out,) = call(merge_kernel, [((TOK, CH), BF)], [SMEM, VMEM], 1000000000)(place, partial)
    (hyena_out,) = call(norm_kernel, [((TOK, CH), BF)], [VMEM] * 2, 100000000)(squares, gained)
    return (hyena_out, attn_out)


def solution(mesh):
    return jax.shard_map(
        local,
        mesh=mesh,
        in_specs=(
            P("context", None, "dp"),
            P(None, None, "dp"),
            P("dp"),
            P(None, "dp"),
            P(None, "dp"),
            P("dp"),
            P("context", None, "dp"),
        ),
        out_specs=(P("context", "dp"), P("context", "dp")),
        check_vma=False,
    )
```

```python
import functools
import itertools
import math

import jax
import jax.numpy as jnp
from jax import lax
from jax.experimental import pallas as pl
from jax.experimental.pallas import tpu as pltpu
from jax.sharding import PartitionSpec as P

DH = 4096
HEAD = 128
HEADS_DEV = 4
FEAT = 3
MODES = 16
TOK = 64
CH = 512
ROPE_BASE = 1000000.0
NEG = -1e30
PACK = 2 * TOK + MODES
WIDE = 256
BLOCKS = WIDE // TOK
BF = jnp.bfloat16
F32 = jnp.float32

DIGITS = {"y": (2, 32), "x": (4, 8), "v": (4, 2), "u": (2, 1)}


def groups_over(*free):
    fixed = [d for d in DIGITS if d not in free]

    def places(names):
        return [
            sum(v * DIGITS[d][1] for v, d in zip(values, names))
            for values in itertools.product(*[range(DIGITS[d][0]) for d in names])
        ]

    return [[base + step for step in places(free)] for base in places(fixed)]


Q_GROUPS = groups_over("x", "v")
KV_GROUPS = groups_over("x", "u")

VMEM = pl.BlockSpec(memory_space=pltpu.VMEM)
SMEM = pl.BlockSpec(memory_space=pltpu.SMEM)


def call(kernel, outs, specs, flops, scratch=()):
    return pl.pallas_call(
        kernel,
        out_shape=[jax.ShapeDtypeStruct(s, d) for s, d in outs],
        in_specs=specs,
        out_specs=[VMEM] * len(outs),
        scratch_shapes=list(scratch),
        compiler_params=pltpu.CompilerParams(vmem_limit_bytes=16 * 1024 * 1024),
        cost_estimate=pl.CostEstimate(flops=flops, bytes_accessed=1000, transcendentals=0),
    )


def digits(index):
    return [(index // step) % size for size, step in DIGITS.values()]


def expand(rates, weights, start):
    ahead = (lax.broadcasted_iota(jnp.int32, (8, 128), 0) + start).astype(F32)
    bases = [jnp.exp(-rates[n : n + 1, :] * ahead) for n in range(MODES)]
    tiles = []
    for a in range(8):
        scaled = weights * jnp.exp(rates * (-8.0 * a))
        tiles.append(sum(bases[n] * scaled[n : n + 1, :] for n in range(MODES)))
    return tiles


def rotate_kernel(attn_ref, cos_ref, sin_ref, q_ref, kv_ref):
    cosine, sine = cos_ref[...], sin_ref[...]
    for g in range(2):
        x = attn_ref[g].astype(F32)
        for h in range(HEADS_DEV):
            part = x[:, h * HEAD : (h + 1) * HEAD]
            turned = (part * cosine + pltpu.roll(part, HEAD // 2, 1) * sine).astype(BF)
            if g == 0:
                for w in range(4):
                    q_ref[h * 4 + w] = turned
            else:
                kv_ref[h, :TOK, :] = turned
    for h in range(HEADS_DEV):
        kv_ref[h, TOK:, :] = attn_ref[2, :, h * HEAD : (h + 1) * HEAD]


def state_kernel(feat_ref, rim_ref, weight_ref, rates_ref, kv_ref, sent_ref, gate_ref, prod_ref):
    groups = []
    for g in range(3):
        x = jnp.concatenate([rim_ref[g], feat_ref[g].astype(F32)], 0)
        total = weight_ref[0, g : g + 1, :] * x[8 : 8 + TOK]
        for o in range(1, FEAT):
            total = total + weight_ref[o, g : g + 1, :] * x[8 - o : 8 - o + TOK]
        groups.append(total)
    gate_ref[...] = groups[0]
    product = (groups[1] * groups[2]).astype(BF).astype(F32)
    prod_ref[...] = product
    back = (7 - lax.broadcasted_iota(jnp.int32, (8, 128), 0)).astype(F32)
    for part in range(CH // 128):
        lanes = slice(part * 128, (part + 1) * 128)
        step = jnp.exp(-8.0 * rates_ref[:, lanes])
        rows = []
        for n in range(MODES):
            total = product[:8, lanes]
            for a in range(1, 8):
                total = total * step[n : n + 1, :] + product[8 * a : 8 * a + 8, lanes]
            total = total * jnp.exp(-rates_ref[n : n + 1, lanes] * back)
            rows.append(jnp.sum(total, 0, keepdims=True))
        sent_ref[part, : 2 * TOK, :] = kv_ref[part]
        sent_ref[part, 2 * TOK :, :] = jnp.concatenate(rows, 0).astype(BF)


def join_kernel(own_ref, other_ref, out_ref):
    for peer in range(8):
        out_ref[peer, :PACK, :] = own_ref[peer // 2]
        out_ref[peer, PACK:, :] = other_ref[peer // 2]


def near_kernel(prod_ref, coeff_ref, rates_ref, skip_ref, out_ref, padded, impulse):
    padded[:TOK, :] = jnp.zeros((TOK, CH), F32)
    padded[TOK:, :] = prod_ref[...]
    for part in range(CH // 128):
        lanes = slice(part * 128, (part + 1) * 128)
        rows = expand(rates_ref[:, lanes], coeff_ref[:, lanes], 0)
        for a in range(8):
            impulse[8 * a : 8 * a + 8, lanes] = rows[a]
        y = skip_ref[:, lanes] * prod_ref[:, lanes]
        for t in range(TOK):
            y = y + impulse[t : t + 1, lanes] * padded[TOK - t : 2 * TOK - t, lanes]
        out_ref[:, lanes] = y


def write_messages(index, got_ref, rates_ref, out_ref):
    y, x, v, u = digits(index)
    decay = rates_ref[x] * (-float(TOK))
    second = jnp.where(y == 1, 1.0, 0.0).astype(F32)

    def faded(steps):
        return jnp.exp(decay * jnp.maximum(steps, 0).astype(F32))

    own_states = [got_ref[i, 2 * TOK : PACK, :].astype(F32) for i in range(8)]
    other_states = [got_ref[i, PACK + 2 * TOK :, :].astype(F32) * second for i in range(8)]
    reach = [faded(2 * (vt - v) + 6) for vt in range(4)]
    near_steps = [[2 * (vt - v) + u - us - 1 for us in range(2)] for vt in range(4)]
    close = [
        [faded(steps) * jnp.where(steps >= 0, 1.0, 0.0).astype(F32) for steps in pair]
        for pair in near_steps
    ]
    before = {(dx, us): faded(8 * dx - 7 + u - us) for dx in range(1, 4) for us in range(2)}
    across = {(dx, us): faded(8 * dx + 25 + u - us) for dx in range(-3, 4) for us in range(2)}
    for xt in range(4):
        total = jnp.zeros((MODES, 128), F32)
        for xs in range(4):
            for us in range(2):
                total = total + across[xt - xs, us] * other_states[xs * 2 + us]
                if xs < xt:
                    total = total + before[xt - xs, us] * own_states[xs * 2 + us]
        for vt in range(4):
            state = reach[vt] * total
            for us in range(2):
                state = state + close[vt][us] * own_states[xt * 2 + us]
            out_ref[xt * 4 + vt, 80:96, :] = state.astype(BF)


def far_kernel(got_ref, coeff_ref, rates_ref, near_ref, gate_ref, gain_ref, gained_ref, square_ref):
    squares = jnp.zeros((TOK, 128), F32)
    for part in range(CH // 128):
        lanes = slice(part * 128, (part + 1) * 128)
        state = got_ref[part * 4, 80:96, :].astype(F32)
        for j in range(1, 4):
            state = state + got_ref[part * 4 + j, 80:96, :].astype(F32)
        tiles = expand(rates_ref[:, lanes], coeff_ref[:, lanes] * state, 1)
        gated = gate_ref[:, lanes] * (near_ref[:, lanes] + jnp.concatenate(tiles, 0))
        gained_ref[:, lanes] = gated * gain_ref[:, lanes]
        squares = squares + gated * gated
    total = jnp.broadcast_to(jnp.sum(squares, 1, keepdims=True), (TOK, 128))
    total = jnp.concatenate([total, jnp.zeros((TOK, 128), F32)], 0)
    square_ref[...] = jnp.transpose(total)[:8, :]


def norm_kernel(square_ref, gained_ref, out_ref):
    total = jnp.sum(square_ref[...], 0, keepdims=True)
    total = jnp.transpose(jnp.broadcast_to(total, (128, 128)))[:TOK, :]
    factor = lax.rsqrt(total * (1.0 / DH) + 1e-06)
    for part in range(CH // 128):
        lanes = slice(part * 128, (part + 1) * 128)
        out_ref[:, lanes] = (gained_ref[:, lanes] * factor).astype(BF)


def attend_kernel(place_ref, q_ref, got_ref, rates_ref, out_ref):
    y, _, v, u = digits(place_ref[0])
    write_messages(place_ref[0], got_ref, rates_ref, out_ref)
    keys = jnp.concatenate(
        [got_ref[:, first : first + TOK, :].reshape(8 * TOK, HEAD) for first in (0, PACK)], 0
    )
    values = jnp.concatenate(
        [got_ref[:, first + TOK : first + 2 * TOK, :].reshape(8 * TOK, HEAD) for first in (0, PACK)], 0
    )
    row = lax.broadcasted_iota(jnp.int32, (16 * TOK, 1), 0)
    block = row // TOK
    key_pos = (((block // 2) % 4) * 8 + 2 * v + block % 2) * TOK + row % TOK
    key_pos = jnp.where(block < 8, key_pos, jnp.where(y == 1, -1, 1 << 20))
    which = lax.broadcasted_iota(jnp.int32, (16, 128), 0)
    for tile in range(16 * TOK // WIDE):
        query = q_ref[tile * BLOCKS : (tile + 1) * BLOCKS].reshape(WIDE, HEAD)
        lane = lax.broadcasted_iota(jnp.int32, (1, WIDE), 1) + tile * WIDE
        q_block = lane // TOK
        q_pos = ((q_block // 4) * 8 + 2 * (q_block % 4) + u) * TOK + lane % TOK
        scores = lax.dot_general(
            keys, query, (((1,), (1,)), ((), ())), preferred_element_type=F32
        ) * (1.0 / math.sqrt(HEAD))
        scores = jnp.where(key_pos <= q_pos, scores, NEG)
        top = jnp.max(scores, 0, keepdims=True)
        weights = jnp.exp(scores - top)
        total = jnp.sum(weights, 0, keepdims=True)
        mixed = lax.dot_general(
            values, weights.astype(BF), (((0,), (0,)), ((), ())), preferred_element_type=F32
        )
        mixed = jnp.transpose(mixed * (1.0 / total)).astype(BF)
        level = top + jnp.log(total)
        high = level.astype(BF).astype(F32)
        rest = level - high
        middle = rest.astype(BF).astype(F32)
        last = rest - middle
        for b in range(BLOCKS):
            place = tile * BLOCKS + b
            out_ref[place, :TOK, :] = mixed[b * TOK : (b + 1) * TOK]
            part = slice((b // 2) * 128, (b // 2) * 128 + 128)
            stats = jnp.where(
                which == 0,
                high[:, part],
                jnp.where(which == 1, middle[:, part], jnp.where(which == 2, last[:, part], 0.0)),
            )
            out_ref[place, TOK:80, :] = stats.astype(BF)


def merge_kernel(place_ref, got_ref, out_ref):
    odd = digits(place_ref[0])[2] % 2
    levels = jnp.sum(got_ref[:, TOK:80, :].astype(F32), 1)
    levels = jnp.where(odd == 1, pltpu.roll(levels, TOK, 1), levels)
    weights = []
    for h in range(HEADS_DEV):
        part = levels[h * 4 : (h + 1) * 4]
        part = jnp.exp(part - jnp.max(part, 0, keepdims=True))
        weights.append(part / jnp.sum(part, 0, keepdims=True))
    weights = jnp.concatenate(weights + [jnp.zeros((112, 128), F32)], 0)
    weights = jnp.transpose(weights)[:TOK, :]
    for h in range(HEADS_DEV):
        total = jnp.zeros((TOK, HEAD), F32)
        for k in range(4):
            place = h * 4 + k
            total = total + weights[:, place : place + 1] * got_ref[place, :TOK, :].astype(F32)
        out_ref[:, h * HEAD : (h + 1) * HEAD] = total.astype(BF)


def exchange(value, groups):
    return lax.all_to_all(value, "context", 0, 0, axis_index_groups=groups, tiled=True)


def local(features, feat_weight, skip, residues, rates, norm_gain, attn_in):
    index = lax.axis_index("context")
    devices = lax.axis_size("context")
    place = index.astype(jnp.int32)[None]
    features = jnp.transpose(features, (1, 0, 2))
    attn_in = jnp.transpose(attn_in, (1, 0, 2))
    rim = lax.ppermute(
        features[:, TOK - (FEAT - 1) :], "context", [(s, s + 1) for s in range(devices - 1)]
    )

    coeff = residues * jnp.sqrt(-jnp.expm1(-2.0 * rates))
    inverse = jnp.exp(
        jnp.arange(HEAD // 2, dtype=F32) * (-2.0 * math.log(ROPE_BASE) / HEAD)
    )
    positions = (index * TOK + jnp.arange(TOK)).astype(F32)
    angle = positions[:, None] * inverse[None, :]
    cosine, sine = jnp.cos(angle), jnp.sin(angle)
    cosine = jnp.concatenate([cosine, cosine], 1)
    sine = jnp.concatenate([-sine, sine], 1)

    queries, pairs = call(
        rotate_kernel,
        [((16, TOK, HEAD), BF), ((HEADS_DEV, 2 * TOK, HEAD), BF)],
        [VMEM] * 3,
        1000000000,
    )(attn_in, cosine, sine)
    queries = exchange(queries, Q_GROUPS)

    rim = jnp.pad(rim.astype(F32), ((0, 0), (6, 0), (0, 0)))
    sent, gate, product = call(
        state_kernel,
        [((HEADS_DEV, PACK, HEAD), BF), ((TOK, CH), F32), ((TOK, CH), F32)],
        [VMEM] * 5,
        20000000000,
    )(features, rim, feat_weight, rates, pairs)
    other = lax.ppermute(sent, "context", [(s, s + devices // 2) for s in range(devices // 2)])
    (near,) = call(
        near_kernel,
        [((TOK, CH), F32)],
        [VMEM] * 4,
        200000000,
        [pltpu.VMEM((2 * TOK, CH), F32), pltpu.VMEM((TOK, CH), F32)],
    )(product, coeff, rates, skip[None, :])
    quarters = jnp.transpose(rates.reshape(MODES, CH // 128, 128), (1, 0, 2))
    (both,) = call(join_kernel, [((8, 2 * PACK, HEAD), BF)], [VMEM] * 2, 500000000)(sent, other)
    queries, both, coeff, quarters, near, gain = lax.optimization_barrier(
        (queries, both, coeff, quarters, near, norm_gain[None, :])
    )
    got = exchange(both, KV_GROUPS)
    (partial,) = call(
        attend_kernel,
        [((16, TOK + 32, HEAD), BF)],
        [SMEM] + [VMEM] * 3,
        4000000000,
    )(place, queries, got, quarters)
    partial = exchange(partial, Q_GROUPS)

    gained, squares = call(
        far_kernel,
        [((TOK, CH), F32), ((8, 128), F32)],
        [VMEM] * 6,
        1000000000,
    )(partial, coeff, rates, near, gate, gain)
    squares = lax.all_to_all(squares, "dp", 0, 0, tiled=True)
    (attn_out,) = call(merge_kernel, [((TOK, CH), BF)], [SMEM, VMEM], 1000000000)(place, partial)
    (hyena_out,) = call(norm_kernel, [((TOK, CH), BF)], [VMEM] * 2, 100000000)(squares, gained)
    return (hyena_out, attn_out)


def solution(mesh):
    return jax.shard_map(
        local,
        mesh=mesh,
        in_specs=(
            P("context", None, "dp"),
            P(None, None, "dp"),
            P("dp"),
            P(None, "dp"),
            P(None, "dp"),
            P("dp"),
            P("context", None, "dp"),
        ),
        out_specs=(P("context", "dp"), P("context", "dp")),
        check_vma=False,
    )
```

```python
import functools
import itertools
import math

import jax
import jax.numpy as jnp
from jax import lax
from jax.experimental import pallas as pl
from jax.experimental.pallas import tpu as pltpu
from jax.sharding import PartitionSpec as P

DH = 4096
HEAD = 128
HEADS_DEV = 4
FEAT = 3
MODES = 16
TOK = 64
CH = 512
ROPE_BASE = 1000000.0
NEG = -1e30
PACK = 2 * TOK + MODES
WIDE = 256
BLOCKS = WIDE // TOK
BF = jnp.bfloat16
F32 = jnp.float32

DIGITS = {"y": (2, 32), "x": (4, 8), "v": (4, 2), "u": (2, 1)}


def groups_over(*free):
    fixed = [d for d in DIGITS if d not in free]

    def places(names):
        return [
            sum(v * DIGITS[d][1] for v, d in zip(values, names))
            for values in itertools.product(*[range(DIGITS[d][0]) for d in names])
        ]

    return [[base + step for step in places(free)] for base in places(fixed)]


Q_GROUPS = groups_over("x", "v")
KV_GROUPS = groups_over("x", "u")

VMEM = pl.BlockSpec(memory_space=pltpu.VMEM)
SMEM = pl.BlockSpec(memory_space=pltpu.SMEM)


def call(kernel, outs, specs, flops, scratch=()):
    return pl.pallas_call(
        kernel,
        out_shape=[jax.ShapeDtypeStruct(s, d) for s, d in outs],
        in_specs=specs,
        out_specs=[VMEM] * len(outs),
        scratch_shapes=list(scratch),
        compiler_params=pltpu.CompilerParams(vmem_limit_bytes=16 * 1024 * 1024),
        cost_estimate=pl.CostEstimate(flops=flops, bytes_accessed=1000, transcendentals=0),
    )


def digits(index):
    return [(index // step) % size for size, step in DIGITS.values()]


def expand(rates, weights, start):
    ahead = (lax.broadcasted_iota(jnp.int32, (8, 128), 0) + start).astype(F32)
    bases = [jnp.exp(-rates[n : n + 1, :] * ahead) for n in range(MODES)]
    tiles = []
    for a in range(8):
        scaled = weights * jnp.exp(rates * (-8.0 * a))
        tiles.append(sum(bases[n] * scaled[n : n + 1, :] for n in range(MODES)))
    return tiles


def rotate_kernel(attn_ref, cos_ref, sin_ref, q_ref, kv_ref):
    cosine, sine = cos_ref[...], sin_ref[...]
    for g in range(2):
        x = attn_ref[g].astype(F32)
        for h in range(HEADS_DEV):
            part = x[:, h * HEAD : (h + 1) * HEAD]
            turned = (part * cosine + pltpu.roll(part, HEAD // 2, 1) * sine).astype(BF)
            if g == 0:
                for w in range(4):
                    q_ref[h * 4 + w] = turned
            else:
                kv_ref[h, :TOK, :] = turned
    for h in range(HEADS_DEV):
        kv_ref[h, TOK:, :] = attn_ref[2, :, h * HEAD : (h + 1) * HEAD]


def state_kernel(feat_ref, rim_ref, weight_ref, rates_ref, kv_ref, sent_ref, gate_ref, prod_ref):
    groups = []
    for g in range(3):
        x = jnp.concatenate([rim_ref[g], feat_ref[g].astype(F32)], 0)
        total = weight_ref[0, g : g + 1, :] * x[8 : 8 + TOK]
        for o in range(1, FEAT):
            total = total + weight_ref[o, g : g + 1, :] * x[8 - o : 8 - o + TOK]
        groups.append(total)
    gate_ref[...] = groups[0]
    product = (groups[1] * groups[2]).astype(BF).astype(F32)
    prod_ref[...] = product
    back = (7 - lax.broadcasted_iota(jnp.int32, (8, 128), 0)).astype(F32)
    for part in range(CH // 128):
        lanes = slice(part * 128, (part + 1) * 128)
        step = jnp.exp(-8.0 * rates_ref[:, lanes])
        rows = []
        for n in range(MODES):
            total = product[:8, lanes]
            for a in range(1, 8):
                total = total * step[n : n + 1, :] + product[8 * a : 8 * a + 8, lanes]
            total = total * jnp.exp(-rates_ref[n : n + 1, lanes] * back)
            rows.append(jnp.sum(total, 0, keepdims=True))
        sent_ref[part, : 2 * TOK, :] = kv_ref[part]
        sent_ref[part, 2 * TOK :, :] = jnp.concatenate(rows, 0).astype(BF)


def join_kernel(own_ref, other_ref, out_ref):
    for peer in range(8):
        out_ref[peer, :PACK, :] = own_ref[peer // 2]
        out_ref[peer, PACK:, :] = other_ref[peer // 2]


def near_kernel(prod_ref, coeff_ref, rates_ref, skip_ref, out_ref, padded, impulse):
    padded[:TOK, :] = jnp.zeros((TOK, CH), F32)
    padded[TOK:, :] = prod_ref[...]
    for part in range(CH // 128):
        lanes = slice(part * 128, (part + 1) * 128)
        rows = expand(rates_ref[:, lanes], coeff_ref[:, lanes], 0)
        for a in range(8):
            impulse[8 * a : 8 * a + 8, lanes] = rows[a]
        y = skip_ref[:, lanes] * prod_ref[:, lanes]
        for t in range(TOK):
            y = y + impulse[t : t + 1, lanes] * padded[TOK - t : 2 * TOK - t, lanes]
        out_ref[:, lanes] = y


def write_messages(index, got_ref, rates_ref, out_ref):
    y, x, v, u = digits(index)
    decay = rates_ref[x] * (-float(TOK))
    second = jnp.where(y == 1, 1.0, 0.0).astype(F32)

    def faded(steps):
        return jnp.exp(decay * jnp.maximum(steps, 0).astype(F32))

    own_states = [got_ref[i, 2 * TOK : PACK, :].astype(F32) for i in range(8)]
    other_states = [got_ref[i, PACK + 2 * TOK :, :].astype(F32) * second for i in range(8)]
    reach = [faded(2 * (vt - v) + 6) for vt in range(4)]
    near_steps = [[2 * (vt - v) + u - us - 1 for us in range(2)] for vt in range(4)]
    close = [
        [faded(steps) * jnp.where(steps >= 0, 1.0, 0.0).astype(F32) for steps in pair]
        for pair in near_steps
    ]
    before = {(dx, us): faded(8 * dx - 7 + u - us) for dx in range(1, 4) for us in range(2)}
    across = {(dx, us): faded(8 * dx + 25 + u - us) for dx in range(-3, 4) for us in range(2)}
    for xt in range(4):
        total = jnp.zeros((MODES, 128), F32)
        for xs in range(4):
            for us in range(2):
                total = total + across[xt - xs, us] * other_states[xs * 2 + us]
                if xs < xt:
                    total = total + before[xt - xs, us] * own_states[xs * 2 + us]
        for vt in range(4):
            state = reach[vt] * total
            for us in range(2):
                state = state + close[vt][us] * own_states[xt * 2 + us]
            out_ref[xt * 4 + vt, 80:96, :] = state.astype(BF)


def norm_kernel(square_ref, gained_ref, out_ref):
    total = jnp.sum(square_ref[...], 0, keepdims=True)
    total = jnp.transpose(jnp.broadcast_to(total, (128, 128)))[:TOK, :]
    factor = lax.rsqrt(total * (1.0 / DH) + 1e-06)
    for part in range(CH // 128):
        lanes = slice(part * 128, (part + 1) * 128)
        out_ref[:, lanes] = (gained_ref[:, lanes] * factor).astype(BF)


def attend(keys, values, query, mask):
    scores = lax.dot_general(
        keys, query, (((1,), (1,)), ((), ())), preferred_element_type=F32
    ) * (math.log2(math.e) / math.sqrt(HEAD))
    scores = mask(scores)
    top = jnp.max(scores, 0, keepdims=True)
    weights = jnp.exp2(scores - top)
    total = jnp.sum(weights, 0, keepdims=True)
    mixed = lax.dot_general(
        values, weights.astype(BF), (((0,), (0,)), ((), ())), preferred_element_type=F32
    )
    return top, total, mixed


def attend_kernel(place_ref, q_ref, got_ref, rates_ref, out_ref):
    y, _, v, u = digits(place_ref[0])
    write_messages(place_ref[0], got_ref, rates_ref, out_ref)

    def half(first):
        keys = got_ref[:, first : first + TOK, :].reshape(8 * TOK, HEAD)
        return keys, got_ref[:, first + TOK : first + 2 * TOK, :].reshape(8 * TOK, HEAD)

    own, other = half(0), half(PACK)
    row = lax.broadcasted_iota(jnp.int32, (8 * TOK, 1), 0)
    block = row // TOK
    key_pos = ((block // 2) * 8 + 2 * v + block % 2) * TOK + row % TOK
    which = lax.broadcasted_iota(jnp.int32, (16, 128), 0)

    def query_of(tile):
        return q_ref[tile * BLOCKS : (tile + 1) * BLOCKS].reshape(WIDE, HEAD)

    def own_part(tile):
        lane = lax.broadcasted_iota(jnp.int32, (1, WIDE), 1) + tile * WIDE
        q_block = lane // TOK
        q_pos = ((q_block // 4) * 8 + 2 * (q_block % 4) + u) * TOK + lane % TOK
        return attend(*own, query_of(tile), lambda s: jnp.where(key_pos <= q_pos, s, NEG))

    def write(tile, top, total, mixed):
        mixed = jnp.transpose(mixed).astype(BF)
        level = top + jnp.log2(total)
        high = level.astype(BF).astype(F32)
        rest = level - high
        middle = rest.astype(BF).astype(F32)
        last = rest - middle
        for b in range(BLOCKS):
            place = tile * BLOCKS + b
            out_ref[place, :TOK, :] = mixed[b * TOK : (b + 1) * TOK]
            part = slice((b // 2) * 128, (b // 2) * 128 + 128)
            stats = jnp.where(
                which == 0,
                high[:, part],
                jnp.where(which == 1, middle[:, part], jnp.where(which == 2, last[:, part], 0.0)),
            )
            out_ref[place, TOK:80, :] = stats.astype(BF)

    @pl.when(y == 0)
    def _():
        for tile in range(16 * TOK // WIDE):
            top, total, mixed = own_part(tile)
            write(tile, top, total, mixed * (1.0 / total))

    @pl.when(y == 1)
    def _():
        for tile in range(16 * TOK // WIDE):
            top_a, total_a, mixed_a = own_part(tile)
            top_b, total_b, mixed_b = attend(*other, query_of(tile), lambda s: s)
            top = jnp.maximum(top_a, top_b)
            scale_a, scale_b = jnp.exp2(top_a - top), jnp.exp2(top_b - top)
            total = total_a * scale_a + total_b * scale_b
            inverse = 1.0 / total
            write(tile, top, total, mixed_a * (scale_a * inverse) + mixed_b * (scale_b * inverse))


def merge(index, got_ref, out_ref):
    odd = digits(index)[2] % 2
    levels = jnp.sum(got_ref[:, TOK:80, :].astype(F32), 1)
    levels = jnp.where(odd == 1, pltpu.roll(levels, TOK, 1), levels)
    weights = []
    for h in range(HEADS_DEV):
        part = levels[h * 4 : (h + 1) * 4]
        part = jnp.exp2(part - jnp.max(part, 0, keepdims=True))
        weights.append(part / jnp.sum(part, 0, keepdims=True))
    weights = jnp.concatenate(weights + [jnp.zeros((112, 128), F32)], 0)
    weights = jnp.transpose(weights)[:TOK, :]
    for h in range(HEADS_DEV):
        total = jnp.zeros((TOK, HEAD), F32)
        for k in range(4):
            place = h * 4 + k
            total = total + weights[:, place : place + 1] * got_ref[place, :TOK, :].astype(F32)
        out_ref[:, h * HEAD : (h + 1) * HEAD] = total.astype(BF)


def tail_kernel(
    place_ref, got_ref, coeff_ref, rates_ref, near_ref, gate_ref, gain_ref, gained_ref, square_ref, out_ref
):
    squares = jnp.zeros((TOK, 128), F32)
    for part in range(CH // 128):
        lanes = slice(part * 128, (part + 1) * 128)
        state = got_ref[part * 4, 80:96, :].astype(F32)
        for j in range(1, 4):
            state = state + got_ref[part * 4 + j, 80:96, :].astype(F32)
        tiles = expand(rates_ref[:, lanes], coeff_ref[:, lanes] * state, 1)
        gated = gate_ref[:, lanes] * (near_ref[:, lanes] + jnp.concatenate(tiles, 0))
        gained_ref[:, lanes] = gated * gain_ref[:, lanes]
        squares = squares + gated * gated
    total = jnp.broadcast_to(jnp.sum(squares, 1, keepdims=True), (TOK, 128))
    total = jnp.concatenate([total, jnp.zeros((TOK, 128), F32)], 0)
    square_ref[...] = jnp.transpose(total)[:8, :]
    merge(place_ref[0], got_ref, out_ref)


def exchange(value, groups):
    return lax.all_to_all(value, "context", 0, 0, axis_index_groups=groups, tiled=True)


def local(features, feat_weight, skip, residues, rates, norm_gain, attn_in):
    index = lax.axis_index("context")
    devices = lax.axis_size("context")
    place = index.astype(jnp.int32)[None]
    features = jnp.transpose(features, (1, 0, 2))
    attn_in = jnp.transpose(attn_in, (1, 0, 2))
    rim = lax.ppermute(
        features[:, TOK - (FEAT - 1) :], "context", [(s, s + 1) for s in range(devices - 1)]
    )

    coeff = residues * jnp.sqrt(-jnp.expm1(-2.0 * rates))
    inverse = jnp.exp(
        jnp.arange(HEAD // 2, dtype=F32) * (-2.0 * math.log(ROPE_BASE) / HEAD)
    )
    positions = (index * TOK + jnp.arange(TOK)).astype(F32)
    angle = positions[:, None] * inverse[None, :]
    cosine, sine = jnp.cos(angle), jnp.sin(angle)
    cosine = jnp.concatenate([cosine, cosine], 1)
    sine = jnp.concatenate([-sine, sine], 1)

    queries, pairs = call(
        rotate_kernel,
        [((16, TOK, HEAD), BF), ((HEADS_DEV, 2 * TOK, HEAD), BF)],
        [VMEM] * 3,
        1000000000,
    )(attn_in, cosine, sine)
    queries = exchange(queries, Q_GROUPS)

    rim = jnp.pad(rim.astype(F32), ((0, 0), (6, 0), (0, 0)))
    sent, gate, product = call(
        state_kernel,
        [((HEADS_DEV, PACK, HEAD), BF), ((TOK, CH), F32), ((TOK, CH), F32)],
        [VMEM] * 5,
        20000000000,
    )(features, rim, feat_weight, rates, pairs)
    other = lax.ppermute(sent, "context", [(s, s + devices // 2) for s in range(devices // 2)])
    (near,) = call(
        near_kernel,
        [((TOK, CH), F32)],
        [VMEM] * 4,
        200000000,
        [pltpu.VMEM((2 * TOK, CH), F32), pltpu.VMEM((TOK, CH), F32)],
    )(product, coeff, rates, skip[None, :])
    quarters = jnp.transpose(rates.reshape(MODES, CH // 128, 128), (1, 0, 2))
    (both,) = call(join_kernel, [((8, 2 * PACK, HEAD), BF)], [VMEM] * 2, 500000000)(sent, other)
    queries, both, coeff, quarters, near, gain = lax.optimization_barrier(
        (queries, both, coeff, quarters, near, norm_gain[None, :])
    )
    got = exchange(both, KV_GROUPS)
    (partial,) = call(
        attend_kernel,
        [((16, TOK + 32, HEAD), BF)],
        [SMEM] + [VMEM] * 3,
        4000000000,
    )(place, queries, got, quarters)
    partial = exchange(partial, Q_GROUPS)

    gained, squares, attn_out = call(
        tail_kernel,
        [((TOK, CH), F32), ((8, 128), F32), ((TOK, CH), BF)],
        [SMEM] + [VMEM] * 6,
        1000000000,
    )(place, partial, coeff, rates, near, gate, gain)
    squares = lax.all_to_all(squares, "dp", 0, 0, tiled=True)
    (hyena_out,) = call(norm_kernel, [((TOK, CH), BF)], [VMEM] * 2, 100000000)(squares, gained)
    return (hyena_out, attn_out)


def solution(mesh):
    return jax.shard_map(
        local,
        mesh=mesh,
        in_specs=(
            P("context", None, "dp"),
            P(None, None, "dp"),
            P("dp"),
            P(None, "dp"),
            P(None, "dp"),
            P("dp"),
            P("context", None, "dp"),
        ),
        out_specs=(P("context", "dp"), P("context", "dp")),
        check_vma=False,
    )
```

```python
import functools
import itertools
import math

import jax
import jax.numpy as jnp
from jax import lax
from jax.experimental import pallas as pl
from jax.experimental.pallas import tpu as pltpu
from jax.sharding import PartitionSpec as P

DH = 4096
HEAD = 128
HEADS_DEV = 4
FEAT = 3
MODES = 16
TOK = 64
CH = 512
ROPE_BASE = 1000000.0
NEG = -1e30
PACK = 2 * TOK + MODES
WIDE = 256
BLOCKS = WIDE // TOK
BF = jnp.bfloat16
F32 = jnp.float32

DIGITS = {"y": (2, 32), "x": (4, 8), "v": (4, 2), "u": (2, 1)}


def groups_over(*free):
    fixed = [d for d in DIGITS if d not in free]

    def places(names):
        return [
            sum(v * DIGITS[d][1] for v, d in zip(values, names))
            for values in itertools.product(*[range(DIGITS[d][0]) for d in names])
        ]

    return [[base + step for step in places(free)] for base in places(fixed)]


Q_GROUPS = groups_over("x", "v")
KV_GROUPS = groups_over("x", "u")

VMEM = pl.BlockSpec(memory_space=pltpu.VMEM)
SMEM = pl.BlockSpec(memory_space=pltpu.SMEM)


def call(kernel, outs, specs, flops, scratch=()):
    return pl.pallas_call(
        kernel,
        out_shape=[jax.ShapeDtypeStruct(s, d) for s, d in outs],
        in_specs=specs,
        out_specs=[VMEM] * len(outs),
        scratch_shapes=list(scratch),
        compiler_params=pltpu.CompilerParams(vmem_limit_bytes=16 * 1024 * 1024),
        cost_estimate=pl.CostEstimate(flops=flops, bytes_accessed=1000, transcendentals=0),
    )


def digits(index):
    return [(index // step) % size for size, step in DIGITS.values()]


def expand(rates, weights, start):
    ahead = (lax.broadcasted_iota(jnp.int32, (8, 128), 0) + start).astype(F32)
    bases = [jnp.exp(-rates[n : n + 1, :] * ahead) for n in range(MODES)]
    tiles = []
    for a in range(8):
        scaled = weights * jnp.exp(rates * (-8.0 * a))
        tiles.append(sum(bases[n] * scaled[n : n + 1, :] for n in range(MODES)))
    return tiles


def rotate_kernel(attn_ref, cos_ref, sin_ref, q_ref, kv_ref):
    cosine, sine = cos_ref[...], sin_ref[...]
    for g in range(2):
        x = attn_ref[g].astype(F32)
        for h in range(HEADS_DEV):
            part = x[:, h * HEAD : (h + 1) * HEAD]
            turned = (part * cosine + pltpu.roll(part, HEAD // 2, 1) * sine).astype(BF)
            if g == 0:
                for w in range(4):
                    q_ref[h * 4 + w] = turned
            else:
                kv_ref[h, :TOK, :] = turned
    for h in range(HEADS_DEV):
        kv_ref[h, TOK:, :] = attn_ref[2, :, h * HEAD : (h + 1) * HEAD]


def state_kernel(feat_ref, rim_ref, weight_ref, rates_ref, kv_ref, sent_ref, gate_ref, prod_ref):
    groups = []
    for g in range(3):
        x = jnp.concatenate([rim_ref[g], feat_ref[g].astype(F32)], 0)
        total = weight_ref[0, g : g + 1, :] * x[8 : 8 + TOK]
        for o in range(1, FEAT):
            total = total + weight_ref[o, g : g + 1, :] * x[8 - o : 8 - o + TOK]
        groups.append(total)
    gate_ref[...] = groups[0]
    product = (groups[1] * groups[2]).astype(BF).astype(F32)
    prod_ref[...] = product
    back = (7 - lax.broadcasted_iota(jnp.int32, (8, 128), 0)).astype(F32)
    for part in range(CH // 128):
        lanes = slice(part * 128, (part + 1) * 128)
        step = jnp.exp(-8.0 * rates_ref[:, lanes])
        rows = []
        for n in range(MODES):
            total = product[:8, lanes]
            for a in range(1, 8):
                total = total * step[n : n + 1, :] + product[8 * a : 8 * a + 8, lanes]
            total = total * jnp.exp(-rates_ref[n : n + 1, lanes] * back)
            rows.append(jnp.sum(total, 0, keepdims=True))
        sent_ref[part, : 2 * TOK, :] = kv_ref[part]
        sent_ref[part, 2 * TOK :, :] = jnp.concatenate(rows, 0).astype(BF)


def join_kernel(own_ref, other_ref, out_ref):
    for peer in range(8):
        out_ref[peer, :PACK, :] = own_ref[peer // 2]
        out_ref[peer, PACK:, :] = other_ref[peer // 2]


def near_kernel(prod_ref, coeff_ref, rates_ref, skip_ref, out_ref, padded, impulse):
    padded[:TOK, :] = jnp.zeros((TOK, CH), F32)
    padded[TOK:, :] = prod_ref[...]
    for part in range(CH // 128):
        lanes = slice(part * 128, (part + 1) * 128)
        rows = expand(rates_ref[:, lanes], coeff_ref[:, lanes], 0)
        for a in range(8):
            impulse[8 * a : 8 * a + 8, lanes] = rows[a]
        y = skip_ref[:, lanes] * prod_ref[:, lanes]
        for t in range(TOK):
            y = y + impulse[t : t + 1, lanes] * padded[TOK - t : 2 * TOK - t, lanes]
        out_ref[:, lanes] = y


def write_messages(index, got_ref, rates_ref, out_ref):
    y, x, v, u = digits(index)
    decay = rates_ref[x] * (-float(TOK))
    second = jnp.where(y == 1, 1.0, 0.0).astype(F32)

    def faded(steps):
        return jnp.exp(decay * jnp.maximum(steps, 0).astype(F32))

    own_states = [got_ref[i, 2 * TOK : PACK, :].astype(F32) for i in range(8)]
    other_states = [got_ref[i, PACK + 2 * TOK :, :].astype(F32) * second for i in range(8)]
    reach = [faded(2 * (vt - v) + 6) for vt in range(4)]
    near_steps = [[2 * (vt - v) + u - us - 1 for us in range(2)] for vt in range(4)]
    close = [
        [faded(steps) * jnp.where(steps >= 0, 1.0, 0.0).astype(F32) for steps in pair]
        for pair in near_steps
    ]
    before = {(dx, us): faded(8 * dx - 7 + u - us) for dx in range(1, 4) for us in range(2)}
    across = {(dx, us): faded(8 * dx + 25 + u - us) for dx in range(-3, 4) for us in range(2)}
    for xt in range(4):
        total = jnp.zeros((MODES, 128), F32)
        for xs in range(4):
            for us in range(2):
                total = total + across[xt - xs, us] * other_states[xs * 2 + us]
                if xs < xt:
                    total = total + before[xt - xs, us] * own_states[xs * 2 + us]
        for vt in range(4):
            state = reach[vt] * total
            for us in range(2):
                state = state + close[vt][us] * own_states[xt * 2 + us]
            out_ref[xt * 4 + vt, 80:96, :] = state.astype(BF)


def norm_kernel(square_ref, gained_ref, out_ref):
    total = jnp.sum(square_ref[...], 0, keepdims=True)
    total = jnp.transpose(jnp.broadcast_to(total, (128, 128)))[:TOK, :]
    factor = lax.rsqrt(total * (1.0 / DH) + 1e-06)
    for part in range(CH // 128):
        lanes = slice(part * 128, (part + 1) * 128)
        out_ref[:, lanes] = (gained_ref[:, lanes] * factor).astype(BF)


def attend(keys, values, query, mask):
    scores = lax.dot_general(
        keys, query, (((1,), (1,)), ((), ())), preferred_element_type=F32
    ) * (math.log2(math.e) / math.sqrt(HEAD))
    scores = mask(scores)
    top = jnp.max(scores, 0, keepdims=True)
    weights = jnp.exp2(scores - top)
    total = jnp.sum(weights, 0, keepdims=True)
    mixed = lax.dot_general(
        values, weights.astype(BF), (((0,), (0,)), ((), ())), preferred_element_type=F32
    )
    return top, total, mixed


def attend_kernel(place_ref, q_ref, got_ref, rates_ref, out_ref):
    y, _, v, u = digits(place_ref[0])
    write_messages(place_ref[0], got_ref, rates_ref, out_ref)

    def half(first):
        keys = got_ref[:, first : first + TOK, :].reshape(8 * TOK, HEAD)
        return keys, got_ref[:, first + TOK : first + 2 * TOK, :].reshape(8 * TOK, HEAD)

    own, other = half(0), half(PACK)
    row = lax.broadcasted_iota(jnp.int32, (8 * TOK, 1), 0)
    block = row // TOK
    key_pos = ((block // 2) * 8 + 2 * v + block % 2) * TOK + row % TOK
    which = lax.broadcasted_iota(jnp.int32, (16, 128), 0)

    def query_of(tile):
        return q_ref[tile * BLOCKS : (tile + 1) * BLOCKS].reshape(WIDE, HEAD)

    def own_part(tile):
        lane = lax.broadcasted_iota(jnp.int32, (1, WIDE), 1) + tile * WIDE
        q_block = lane // TOK
        q_pos = ((q_block // 4) * 8 + 2 * (q_block % 4) + u) * TOK + lane % TOK
        return attend(*own, query_of(tile), lambda s: jnp.where(key_pos <= q_pos, s, NEG))

    def write(tile, top, total, mixed):
        mixed = jnp.transpose(mixed).astype(BF)
        level = top + jnp.log2(total)
        high = level.astype(BF).astype(F32)
        rest = level - high
        middle = rest.astype(BF).astype(F32)
        last = rest - middle
        for b in range(BLOCKS):
            place = tile * BLOCKS + b
            out_ref[place, :TOK, :] = mixed[b * TOK : (b + 1) * TOK]
            part = slice((b // 2) * 128, (b // 2) * 128 + 128)
            stats = jnp.where(
                which == 0,
                high[:, part],
                jnp.where(which == 1, middle[:, part], jnp.where(which == 2, last[:, part], 0.0)),
            )
            out_ref[place, TOK:80, :] = stats.astype(BF)

    @pl.when(y == 0)
    def _():
        for tile in range(16 * TOK // WIDE):
            top, total, mixed = own_part(tile)
            write(tile, top, total, mixed * (1.0 / total))

    @pl.when(y == 1)
    def _():
        for tile in range(16 * TOK // WIDE):
            top_a, total_a, mixed_a = own_part(tile)
            top_b, total_b, mixed_b = attend(*other, query_of(tile), lambda s: s)
            top = jnp.maximum(top_a, top_b)
            scale_a, scale_b = jnp.exp2(top_a - top), jnp.exp2(top_b - top)
            total = total_a * scale_a + total_b * scale_b
            inverse = 1.0 / total
            write(tile, top, total, mixed_a * (scale_a * inverse) + mixed_b * (scale_b * inverse))


def merge(index, got_ref, out_ref):
    odd = digits(index)[2] % 2
    levels = jnp.sum(got_ref[:, TOK:80, :].astype(F32), 1)
    levels = jnp.where(odd == 1, pltpu.roll(levels, TOK, 1), levels)
    weights = []
    for h in range(HEADS_DEV):
        part = levels[h * 4 : (h + 1) * 4]
        part = jnp.exp2(part - jnp.max(part, 0, keepdims=True))
        weights.append(part / jnp.sum(part, 0, keepdims=True))
    weights = jnp.concatenate(weights + [jnp.zeros((112, 128), F32)], 0)
    weights = jnp.transpose(weights)[:TOK, :]
    for h in range(HEADS_DEV):
        total = jnp.zeros((TOK, HEAD), F32)
        for k in range(4):
            place = h * 4 + k
            total = total + weights[:, place : place + 1] * got_ref[place, :TOK, :].astype(F32)
        out_ref[:, h * HEAD : (h + 1) * HEAD] = total.astype(BF)


def tail_kernel(
    place_ref, got_ref, coeff_ref, rates_ref, near_ref, gate_ref, gain_ref, gained_ref, square_ref, out_ref
):
    squares = jnp.zeros((TOK, 128), F32)
    for part in range(CH // 128):
        lanes = slice(part * 128, (part + 1) * 128)
        state = got_ref[part * 4, 80:96, :].astype(F32)
        for j in range(1, 4):
            state = state + got_ref[part * 4 + j, 80:96, :].astype(F32)
        tiles = expand(rates_ref[:, lanes], coeff_ref[:, lanes] * state, 1)
        gated = gate_ref[:, lanes] * (near_ref[:, lanes] + jnp.concatenate(tiles, 0))
        gained_ref[:, lanes] = gated * gain_ref[:, lanes]
        squares = squares + gated * gated
    total = jnp.broadcast_to(jnp.sum(squares, 1, keepdims=True), (TOK, 128))
    total = jnp.concatenate([total, jnp.zeros((TOK, 128), F32)], 0)
    square_ref[...] = jnp.transpose(total)[:8, :]
    merge(place_ref[0], got_ref, out_ref)


def exchange(value, groups):
    return lax.all_to_all(value, "context", 0, 0, axis_index_groups=groups, tiled=True)


def local(features, feat_weight, skip, residues, rates, norm_gain, attn_in):
    index = lax.axis_index("context")
    devices = lax.axis_size("context")
    place = index.astype(jnp.int32)[None]
    features = jnp.transpose(features, (1, 0, 2))
    attn_in = jnp.transpose(attn_in, (1, 0, 2))
    rim = lax.ppermute(
        features[:, TOK - (FEAT - 1) :], "context", [(s, s + 1) for s in range(devices - 1)]
    )

    coeff = residues * jnp.sqrt(-jnp.expm1(-2.0 * rates))
    inverse = jnp.exp(
        jnp.arange(HEAD // 2, dtype=F32) * (-2.0 * math.log(ROPE_BASE) / HEAD)
    )
    positions = (index * TOK + jnp.arange(TOK)).astype(F32)
    angle = positions[:, None] * inverse[None, :]
    cosine, sine = jnp.cos(angle), jnp.sin(angle)
    cosine = jnp.concatenate([cosine, cosine], 1)
    sine = jnp.concatenate([-sine, sine], 1)

    queries, pairs = call(
        rotate_kernel,
        [((16, TOK, HEAD), BF), ((HEADS_DEV, 2 * TOK, HEAD), BF)],
        [VMEM] * 3,
        1000000000,
    )(attn_in, cosine, sine)
    rim = jnp.pad(rim.astype(F32), ((0, 0), (6, 0), (0, 0)))
    sent, gate, product = call(
        state_kernel,
        [((HEADS_DEV, PACK, HEAD), BF), ((TOK, CH), F32), ((TOK, CH), F32)],
        [VMEM] * 5,
        20000000000,
    )(features, rim, feat_weight, rates, pairs)
    sent, queries = lax.optimization_barrier((sent, queries))
    queries = exchange(queries, Q_GROUPS)
    other = lax.ppermute(sent, "context", [(s, s + devices // 2) for s in range(devices // 2)])
    (near,) = call(
        near_kernel,
        [((TOK, CH), F32)],
        [VMEM] * 4,
        200000000,
        [pltpu.VMEM((2 * TOK, CH), F32), pltpu.VMEM((TOK, CH), F32)],
    )(product, coeff, rates, skip[None, :])
    quarters = jnp.transpose(rates.reshape(MODES, CH // 128, 128), (1, 0, 2))
    (both,) = call(join_kernel, [((8, 2 * PACK, HEAD), BF)], [VMEM] * 2, 50000000000)(sent, other)
    queries, both, coeff, quarters, near, gain = lax.optimization_barrier(
        (queries, both, coeff, quarters, near, norm_gain[None, :])
    )
    got = exchange(both, KV_GROUPS)
    (partial,) = call(
        attend_kernel,
        [((16, TOK + 32, HEAD), BF)],
        [SMEM] + [VMEM] * 3,
        4000000000,
    )(place, queries, got, quarters)
    partial = exchange(partial, Q_GROUPS)

    gained, squares, attn_out = call(
        tail_kernel,
        [((TOK, CH), F32), ((8, 128), F32), ((TOK, CH), BF)],
        [SMEM] + [VMEM] * 6,
        1000000000,
    )(place, partial, coeff, rates, near, gate, gain)
    squares = lax.all_to_all(squares, "dp", 0, 0, tiled=True)
    (hyena_out,) = call(norm_kernel, [((TOK, CH), BF)], [VMEM] * 2, 100000000)(squares, gained)
    return (hyena_out, attn_out)


def solution(mesh):
    return jax.shard_map(
        local,
        mesh=mesh,
        in_specs=(
            P("context", None, "dp"),
            P(None, None, "dp"),
            P("dp"),
            P(None, "dp"),
            P(None, "dp"),
            P("dp"),
            P("context", None, "dp"),
        ),
        out_specs=(P("context", "dp"), P("context", "dp")),
        check_vma=False,
    )
```

```python
import functools
import itertools
import math

import jax
import jax.numpy as jnp
from jax import lax
from jax.experimental import pallas as pl
from jax.experimental.pallas import tpu as pltpu
from jax.sharding import PartitionSpec as P

DH = 4096
HEAD = 128
HEADS_DEV = 4
FEAT = 3
MODES = 16
TOK = 64
CH = 512
ROPE_BASE = 1000000.0
NEG = -1e30
PACK = 2 * TOK + MODES
WIDE = 256
BLOCKS = WIDE // TOK
BF = jnp.bfloat16
F32 = jnp.float32

DIGITS = {"y": (2, 32), "x": (4, 8), "v": (4, 2), "u": (2, 1)}


def groups_over(*free):
    fixed = [d for d in DIGITS if d not in free]

    def places(names):
        return [
            sum(v * DIGITS[d][1] for v, d in zip(values, names))
            for values in itertools.product(*[range(DIGITS[d][0]) for d in names])
        ]

    return [[base + step for step in places(free)] for base in places(fixed)]


Q_GROUPS = groups_over("x", "v")
KV_GROUPS = groups_over("x", "u")

VMEM = pl.BlockSpec(memory_space=pltpu.VMEM)
SMEM = pl.BlockSpec(memory_space=pltpu.SMEM)


def call(kernel, outs, specs, flops, scratch=()):
    return pl.pallas_call(
        kernel,
        out_shape=[jax.ShapeDtypeStruct(s, d) for s, d in outs],
        in_specs=specs,
        out_specs=[VMEM] * len(outs),
        scratch_shapes=list(scratch),
        compiler_params=pltpu.CompilerParams(vmem_limit_bytes=16 * 1024 * 1024),
        cost_estimate=pl.CostEstimate(flops=flops, bytes_accessed=1000, transcendentals=0),
    )


def digits(index):
    return [(index // step) % size for size, step in DIGITS.values()]


def expand(rates, weights, start):
    ahead = (lax.broadcasted_iota(jnp.int32, (8, 128), 0) + start).astype(F32)
    bases = [jnp.exp(-rates[n : n + 1, :] * ahead) for n in range(MODES)]
    tiles = []
    for a in range(8):
        scaled = weights * jnp.exp(rates * (-8.0 * a))
        tiles.append(sum(bases[n] * scaled[n : n + 1, :] for n in range(MODES)))
    return tiles


def rotated(x, cosine, sine):
    x = x.astype(F32)
    return (x * cosine + pltpu.roll(x, HEAD // 2, 1) * sine).astype(BF)


def pair_kernel(attn_ref, cos_ref, sin_ref, kv_ref):
    cosine, sine = cos_ref[...], sin_ref[...]
    for h in range(HEADS_DEV):
        lanes = slice(h * HEAD, (h + 1) * HEAD)
        kv_ref[h, :TOK, :] = rotated(attn_ref[1, :, lanes], cosine, sine)
        kv_ref[h, TOK:, :] = attn_ref[2, :, lanes]


def query_kernel(attn_ref, cos_ref, sin_ref, q_ref):
    cosine, sine = cos_ref[...], sin_ref[...]
    for h in range(HEADS_DEV):
        turned = rotated(attn_ref[0, :, h * HEAD : (h + 1) * HEAD], cosine, sine)
        for v in range(4):
            q_ref[h * 4 + v] = turned


def state_kernel(feat_ref, rim_ref, weight_ref, rates_ref, state_ref, gate_ref, prod_ref):
    groups = []
    for g in range(3):
        x = jnp.concatenate([rim_ref[g], feat_ref[g].astype(F32)], 0)
        total = weight_ref[0, g : g + 1, :] * x[8 : 8 + TOK]
        for o in range(1, FEAT):
            total = total + weight_ref[o, g : g + 1, :] * x[8 - o : 8 - o + TOK]
        groups.append(total)
    gate_ref[...] = groups[0]
    product = (groups[1] * groups[2]).astype(BF).astype(F32)
    prod_ref[...] = product
    back = (7 - lax.broadcasted_iota(jnp.int32, (8, 128), 0)).astype(F32)
    for part in range(CH // 128):
        lanes = slice(part * 128, (part + 1) * 128)
        step = jnp.exp(-8.0 * rates_ref[:, lanes])
        rows = []
        for n in range(MODES):
            total = product[:8, lanes]
            for a in range(1, 8):
                total = total * step[n : n + 1, :] + product[8 * a : 8 * a + 8, lanes]
            total = total * jnp.exp(-rates_ref[n : n + 1, lanes] * back)
            rows.append(jnp.sum(total, 0, keepdims=True))
        state_ref[part] = jnp.concatenate(rows, 0).astype(BF)


def join_kernel(pair_ref, state_ref, far_pair_ref, far_state_ref, out_ref):
    for peer in range(8):
        head = peer // 2
        out_ref[peer, : 2 * TOK, :] = pair_ref[head]
        out_ref[peer, 2 * TOK : PACK, :] = state_ref[head]
        out_ref[peer, PACK : PACK + 2 * TOK, :] = far_pair_ref[head]
        out_ref[peer, PACK + 2 * TOK :, :] = far_state_ref[head]


def near_kernel(prod_ref, coeff_ref, rates_ref, skip_ref, out_ref, padded, impulse):
    padded[:TOK, :] = jnp.zeros((TOK, CH), F32)
    padded[TOK:, :] = prod_ref[...]
    for part in range(CH // 128):
        lanes = slice(part * 128, (part + 1) * 128)
        rows = expand(rates_ref[:, lanes], coeff_ref[:, lanes], 0)
        for a in range(8):
            impulse[8 * a : 8 * a + 8, lanes] = rows[a]
        y = skip_ref[:, lanes] * prod_ref[:, lanes]
        for t in range(TOK):
            y = y + impulse[t : t + 1, lanes] * padded[TOK - t : 2 * TOK - t, lanes]
        out_ref[:, lanes] = y


def write_messages(index, got_ref, rates_ref, out_ref):
    y, x, v, u = digits(index)
    decay = rates_ref[x] * (-float(TOK))
    second = jnp.where(y == 1, 1.0, 0.0).astype(F32)

    def faded(steps):
        return jnp.exp(decay * jnp.maximum(steps, 0).astype(F32))

    own_states = [got_ref[i, 2 * TOK : PACK, :].astype(F32) for i in range(8)]
    other_states = [got_ref[i, PACK + 2 * TOK :, :].astype(F32) * second for i in range(8)]
    reach = [faded(2 * (vt - v) + 6) for vt in range(4)]
    near_steps = [[2 * (vt - v) + u - us - 1 for us in range(2)] for vt in range(4)]
    close = [
        [faded(steps) * jnp.where(steps >= 0, 1.0, 0.0).astype(F32) for steps in pair]
        for pair in near_steps
    ]
    before = {(dx, us): faded(8 * dx - 7 + u - us) for dx in range(1, 4) for us in range(2)}
    across = {(dx, us): faded(8 * dx + 25 + u - us) for dx in range(-3, 4) for us in range(2)}
    for xt in range(4):
        total = jnp.zeros((MODES, 128), F32)
        for xs in range(4):
            for us in range(2):
                total = total + across[xt - xs, us] * other_states[xs * 2 + us]
                if xs < xt:
                    total = total + before[xt - xs, us] * own_states[xs * 2 + us]
        for vt in range(4):
            state = reach[vt] * total
            for us in range(2):
                state = state + close[vt][us] * own_states[xt * 2 + us]
            out_ref[xt * 4 + vt, 80:96, :] = state.astype(BF)


def norm_kernel(square_ref, gained_ref, out_ref):
    total = jnp.sum(square_ref[...], 0, keepdims=True)
    total = jnp.transpose(jnp.broadcast_to(total, (128, 128)))[:TOK, :]
    factor = lax.rsqrt(total * (1.0 / DH) + 1e-06)
    for part in range(CH // 128):
        lanes = slice(part * 128, (part + 1) * 128)
        out_ref[:, lanes] = (gained_ref[:, lanes] * factor).astype(BF)


def attend(keys, values, query, mask):
    scores = lax.dot_general(
        keys, query, (((1,), (1,)), ((), ())), preferred_element_type=F32
    ) * (math.log2(math.e) / math.sqrt(HEAD))
    scores = mask(scores)
    top = jnp.max(scores, 0, keepdims=True)
    weights = jnp.exp2(scores - top)
    total = jnp.sum(weights, 0, keepdims=True)
    mixed = lax.dot_general(
        values, weights.astype(BF), (((0,), (0,)), ((), ())), preferred_element_type=F32
    )
    return top, total, mixed


def attend_kernel(place_ref, q_ref, got_ref, rates_ref, out_ref):
    y, _, v, u = digits(place_ref[0])
    write_messages(place_ref[0], got_ref, rates_ref, out_ref)

    def half(first):
        keys = got_ref[:, first : first + TOK, :].reshape(8 * TOK, HEAD)
        return keys, got_ref[:, first + TOK : first + 2 * TOK, :].reshape(8 * TOK, HEAD)

    own, other = half(0), half(PACK)
    row = lax.broadcasted_iota(jnp.int32, (8 * TOK, 1), 0)
    block = row // TOK
    key_pos = ((block // 2) * 8 + 2 * v + block % 2) * TOK + row % TOK
    which = lax.broadcasted_iota(jnp.int32, (16, 128), 0)

    def query_of(tile):
        return q_ref[tile * BLOCKS : (tile + 1) * BLOCKS].reshape(WIDE, HEAD)

    def own_part(tile):
        lane = lax.broadcasted_iota(jnp.int32, (1, WIDE), 1) + tile * WIDE
        q_block = lane // TOK
        q_pos = ((q_block // 4) * 8 + 2 * (q_block % 4) + u) * TOK + lane % TOK
        return attend(*own, query_of(tile), lambda s: jnp.where(key_pos <= q_pos, s, NEG))

    def write(tile, top, total, mixed):
        mixed = jnp.transpose(mixed).astype(BF)
        level = top + jnp.log2(total)
        high = level.astype(BF).astype(F32)
        rest = level - high
        middle = rest.astype(BF).astype(F32)
        last = rest - middle
        for b in range(BLOCKS):
            place = tile * BLOCKS + b
            out_ref[place, :TOK, :] = mixed[b * TOK : (b + 1) * TOK]
            part = slice((b // 2) * 128, (b // 2) * 128 + 128)
            stats = jnp.where(
                which == 0,
                high[:, part],
                jnp.where(which == 1, middle[:, part], jnp.where(which == 2, last[:, part], 0.0)),
            )
            out_ref[place, TOK:80, :] = stats.astype(BF)

    @pl.when(y == 0)
    def _():
        for tile in range(16 * TOK // WIDE):
            top, total, mixed = own_part(tile)
            write(tile, top, total, mixed * (1.0 / total))

    @pl.when(y == 1)
    def _():
        for tile in range(16 * TOK // WIDE):
            top_a, total_a, mixed_a = own_part(tile)
            top_b, total_b, mixed_b = attend(*other, query_of(tile), lambda s: s)
            top = jnp.maximum(top_a, top_b)
            scale_a, scale_b = jnp.exp2(top_a - top), jnp.exp2(top_b - top)
            total = total_a * scale_a + total_b * scale_b
            inverse = 1.0 / total
            write(tile, top, total, mixed_a * (scale_a * inverse) + mixed_b * (scale_b * inverse))


def merge(index, got_ref, out_ref):
    odd = digits(index)[2] % 2
    levels = jnp.sum(got_ref[:, TOK:80, :].astype(F32), 1)
    levels = jnp.where(odd == 1, pltpu.roll(levels, TOK, 1), levels)
    weights = []
    for h in range(HEADS_DEV):
        part = levels[h * 4 : (h + 1) * 4]
        part = jnp.exp2(part - jnp.max(part, 0, keepdims=True))
        weights.append(part / jnp.sum(part, 0, keepdims=True))
    weights = jnp.concatenate(weights + [jnp.zeros((112, 128), F32)], 0)
    weights = jnp.transpose(weights)[:TOK, :]
    for h in range(HEADS_DEV):
        total = jnp.zeros((TOK, HEAD), F32)
        for k in range(4):
            place = h * 4 + k
            total = total + weights[:, place : place + 1] * got_ref[place, :TOK, :].astype(F32)
        out_ref[:, h * HEAD : (h + 1) * HEAD] = total.astype(BF)


def tail_kernel(
    place_ref, got_ref, coeff_ref, rates_ref, near_ref, gate_ref, gain_ref, gained_ref, square_ref, out_ref
):
    squares = jnp.zeros((TOK, 128), F32)
    for part in range(CH // 128):
        lanes = slice(part * 128, (part + 1) * 128)
        state = got_ref[part * 4, 80:96, :].astype(F32)
        for j in range(1, 4):
            state = state + got_ref[part * 4 + j, 80:96, :].astype(F32)
        tiles = expand(rates_ref[:, lanes], coeff_ref[:, lanes] * state, 1)
        gated = gate_ref[:, lanes] * (near_ref[:, lanes] + jnp.concatenate(tiles, 0))
        gained_ref[:, lanes] = gated * gain_ref[:, lanes]
        squares = squares + gated * gated
    total = jnp.broadcast_to(jnp.sum(squares, 1, keepdims=True), (TOK, 128))
    total = jnp.concatenate([total, jnp.zeros((TOK, 128), F32)], 0)
    square_ref[...] = jnp.transpose(total)[:8, :]
    merge(place_ref[0], got_ref, out_ref)


def exchange(value, groups):
    return lax.all_to_all(value, "context", 0, 0, axis_index_groups=groups, tiled=True)


def local(features, feat_weight, skip, residues, rates, norm_gain, attn_in):
    index = lax.axis_index("context")
    devices = lax.axis_size("context")
    place = index.astype(jnp.int32)[None]
    features = jnp.transpose(features, (1, 0, 2))
    attn_in = jnp.transpose(attn_in, (1, 0, 2))
    rim = lax.ppermute(
        features[:, TOK - (FEAT - 1) :], "context", [(s, s + 1) for s in range(devices - 1)]
    )

    coeff = residues * jnp.sqrt(-jnp.expm1(-2.0 * rates))
    inverse = jnp.exp(
        jnp.arange(HEAD // 2, dtype=F32) * (-2.0 * math.log(ROPE_BASE) / HEAD)
    )
    positions = (index * TOK + jnp.arange(TOK)).astype(F32)
    angle = positions[:, None] * inverse[None, :]
    cosine, sine = jnp.cos(angle), jnp.sin(angle)
    cosine = jnp.concatenate([cosine, cosine], 1)
    sine = jnp.concatenate([-sine, sine], 1)

    (pairs,) = call(
        pair_kernel, [((HEADS_DEV, 2 * TOK, HEAD), BF)], [VMEM] * 3, 1000000000
    )(attn_in, cosine, sine)
    pairs, cosine = lax.optimization_barrier((pairs, cosine))
    (queries,) = call(
        query_kernel, [((16, TOK, HEAD), BF)], [VMEM] * 3, 20000000000
    )(attn_in, cosine, sine)
    over_y = [(s, s + devices // 2) for s in range(devices // 2)]
    far_pairs = lax.ppermute(pairs, "context", over_y)
    queries = exchange(queries, Q_GROUPS)

    rim = jnp.pad(rim.astype(F32), ((0, 0), (6, 0), (0, 0)))
    states, gate, product = call(
        state_kernel,
        [((HEADS_DEV, MODES, HEAD), BF), ((TOK, CH), F32), ((TOK, CH), F32)],
        [VMEM] * 4,
        1000000,
    )(features, rim, feat_weight, rates)
    far_states = lax.ppermute(states, "context", over_y)
    (near,) = call(
        near_kernel,
        [((TOK, CH), F32)],
        [VMEM] * 4,
        1000000,
        [pltpu.VMEM((2 * TOK, CH), F32), pltpu.VMEM((TOK, CH), F32)],
    )(product, coeff, rates, skip[None, :])
    quarters = jnp.transpose(rates.reshape(MODES, CH // 128, 128), (1, 0, 2))
    (both,) = call(join_kernel, [((8, 2 * PACK, HEAD), BF)], [VMEM] * 4, 50000000000)(
        pairs, states, far_pairs, far_states
    )
    queries, both, coeff, quarters, near, gain = lax.optimization_barrier(
        (queries, both, coeff, quarters, near, norm_gain[None, :])
    )
    got = exchange(both, KV_GROUPS)
    (partial,) = call(
        attend_kernel,
        [((16, TOK + 32, HEAD), BF)],
        [SMEM] + [VMEM] * 3,
        4000000000,
    )(place, queries, got, quarters)
    partial = exchange(partial, Q_GROUPS)

    gained, squares, attn_out = call(
        tail_kernel,
        [((TOK, CH), F32), ((8, 128), F32), ((TOK, CH), BF)],
        [SMEM] + [VMEM] * 6,
        1000000000,
    )(place, partial, coeff, rates, near, gate, gain)
    squares = lax.all_to_all(squares, "dp", 0, 0, tiled=True)
    (hyena_out,) = call(norm_kernel, [((TOK, CH), BF)], [VMEM] * 2, 100000000)(squares, gained)
    return (hyena_out, attn_out)


def solution(mesh):
    return jax.shard_map(
        local,
        mesh=mesh,
        in_specs=(
            P("context", None, "dp"),
            P(None, None, "dp"),
            P("dp"),
            P(None, "dp"),
            P(None, "dp"),
            P("dp"),
            P("context", None, "dp"),
        ),
        out_specs=(P("context", "dp"), P("context", "dp")),
        check_vma=False,
    )
```

```python
import functools
import itertools
import math

import jax
import jax.numpy as jnp
from jax import lax
from jax.experimental import pallas as pl
from jax.experimental.pallas import tpu as pltpu
from jax.sharding import PartitionSpec as P

DH = 4096
HEAD = 128
HEADS_DEV = 4
FEAT = 3
MODES = 16
TOK = 64
CH = 512
ROPE_BASE = 1000000.0
NEG = -1e30
PACK = 2 * TOK + MODES
WIDE = 256
BLOCKS = WIDE // TOK
BF = jnp.bfloat16
F32 = jnp.float32

DIGITS = {"y": (2, 32), "x": (4, 8), "v": (4, 2), "u": (2, 1)}


def groups_over(*free):
    fixed = [d for d in DIGITS if d not in free]

    def places(names):
        return [
            sum(v * DIGITS[d][1] for v, d in zip(values, names))
            for values in itertools.product(*[range(DIGITS[d][0]) for d in names])
        ]

    return [[base + step for step in places(free)] for base in places(fixed)]


Q_GROUPS = groups_over("x", "v")
KV_GROUPS = groups_over("x", "u")

VMEM = pl.BlockSpec(memory_space=pltpu.VMEM)
SMEM = pl.BlockSpec(memory_space=pltpu.SMEM)


def call(kernel, outs, specs, flops, scratch=()):
    return pl.pallas_call(
        kernel,
        out_shape=[jax.ShapeDtypeStruct(s, d) for s, d in outs],
        in_specs=specs,
        out_specs=[VMEM] * len(outs),
        scratch_shapes=list(scratch),
        compiler_params=pltpu.CompilerParams(vmem_limit_bytes=16 * 1024 * 1024),
        cost_estimate=pl.CostEstimate(flops=flops, bytes_accessed=1000, transcendentals=0),
    )


def digits(index):
    return [(index // step) % size for size, step in DIGITS.values()]


def expand(rates, weights, start):
    ahead = (lax.broadcasted_iota(jnp.int32, (8, 128), 0) + start).astype(F32)
    bases = [jnp.exp(-rates[n : n + 1, :] * ahead) for n in range(MODES)]
    tiles = []
    for a in range(8):
        scaled = weights * jnp.exp(rates * (-8.0 * a))
        tiles.append(sum(bases[n] * scaled[n : n + 1, :] for n in range(MODES)))
    return tiles


def rotate_kernel(attn_ref, cos_ref, sin_ref, q_ref, kv_ref):
    cosine, sine = cos_ref[...], sin_ref[...]
    for g in range(2):
        x = attn_ref[g].astype(F32)
        for h in range(HEADS_DEV):
            part = x[:, h * HEAD : (h + 1) * HEAD]
            turned = (part * cosine + pltpu.roll(part, HEAD // 2, 1) * sine).astype(BF)
            if g == 0:
                for w in range(4):
                    q_ref[h * 4 + w] = turned
            else:
                kv_ref[h, :TOK, :] = turned
    for h in range(HEADS_DEV):
        kv_ref[h, TOK:, :] = attn_ref[2, :, h * HEAD : (h + 1) * HEAD]


def state_kernel(feat_ref, rim_ref, weight_ref, rates_ref, state_ref, gate_ref, prod_ref):
    groups = []
    for g in range(3):
        x = jnp.concatenate([rim_ref[g], feat_ref[g].astype(F32)], 0)
        total = weight_ref[0, g : g + 1, :] * x[8 : 8 + TOK]
        for o in range(1, FEAT):
            total = total + weight_ref[o, g : g + 1, :] * x[8 - o : 8 - o + TOK]
        groups.append(total)
    gate_ref[...] = groups[0]
    product = (groups[1] * groups[2]).astype(BF).astype(F32)
    prod_ref[...] = product
    back = (7 - lax.broadcasted_iota(jnp.int32, (8, 128), 0)).astype(F32)
    for part in range(CH // 128):
        lanes = slice(part * 128, (part + 1) * 128)
        step = jnp.exp(-8.0 * rates_ref[:, lanes])
        rows = []
        for n in range(MODES):
            total = product[:8, lanes]
            for a in range(1, 8):
                total = total * step[n : n + 1, :] + product[8 * a : 8 * a + 8, lanes]
            total = total * jnp.exp(-rates_ref[n : n + 1, lanes] * back)
            rows.append(jnp.sum(total, 0, keepdims=True))
        state_ref[part] = jnp.concatenate(rows, 0).astype(BF)


def join_kernel(pair_ref, state_ref, far_pair_ref, far_state_ref, out_ref):
    for peer in range(8):
        head = peer // 2
        out_ref[peer, : 2 * TOK, :] = pair_ref[head]
        out_ref[peer, 2 * TOK : PACK, :] = state_ref[head]
        out_ref[peer, PACK : PACK + 2 * TOK, :] = far_pair_ref[head]
        out_ref[peer, PACK + 2 * TOK :, :] = far_state_ref[head]


def near_kernel(prod_ref, coeff_ref, rates_ref, skip_ref, out_ref, padded, impulse):
    padded[:TOK, :] = jnp.zeros((TOK, CH), F32)
    padded[TOK:, :] = prod_ref[...]
    for part in range(CH // 128):
        lanes = slice(part * 128, (part + 1) * 128)
        rows = expand(rates_ref[:, lanes], coeff_ref[:, lanes], 0)
        for a in range(8):
            impulse[8 * a : 8 * a + 8, lanes] = rows[a]
        y = skip_ref[:, lanes] * prod_ref[:, lanes]
        for t in range(TOK):
            y = y + impulse[t : t + 1, lanes] * padded[TOK - t : 2 * TOK - t, lanes]
        out_ref[:, lanes] = y


def write_messages(index, got_ref, rates_ref, out_ref):
    y, x, v, u = digits(index)
    decay = rates_ref[x] * (-float(TOK))
    second = jnp.where(y == 1, 1.0, 0.0).astype(F32)

    def faded(steps):
        return jnp.exp(decay * jnp.maximum(steps, 0).astype(F32))

    own_states = [got_ref[i, 2 * TOK : PACK, :].astype(F32) for i in range(8)]
    other_states = [got_ref[i, PACK + 2 * TOK :, :].astype(F32) * second for i in range(8)]
    reach = [faded(2 * (vt - v) + 6) for vt in range(4)]
    near_steps = [[2 * (vt - v) + u - us - 1 for us in range(2)] for vt in range(4)]
    close = [
        [faded(steps) * jnp.where(steps >= 0, 1.0, 0.0).astype(F32) for steps in pair]
        for pair in near_steps
    ]
    before = {(dx, us): faded(8 * dx - 7 + u - us) for dx in range(1, 4) for us in range(2)}
    across = {(dx, us): faded(8 * dx + 25 + u - us) for dx in range(-3, 4) for us in range(2)}
    for xt in range(4):
        total = jnp.zeros((MODES, 128), F32)
        for xs in range(4):
            for us in range(2):
                total = total + across[xt - xs, us] * other_states[xs * 2 + us]
                if xs < xt:
                    total = total + before[xt - xs, us] * own_states[xs * 2 + us]
        for vt in range(4):
            state = reach[vt] * total
            for us in range(2):
                state = state + close[vt][us] * own_states[xt * 2 + us]
            out_ref[xt * 4 + vt, 80:96, :] = state.astype(BF)


def norm_kernel(square_ref, gained_ref, out_ref):
    total = jnp.sum(square_ref[...], 0, keepdims=True)
    total = jnp.transpose(jnp.broadcast_to(total, (128, 128)))[:TOK, :]
    factor = lax.rsqrt(total * (1.0 / DH) + 1e-06)
    for part in range(CH // 128):
        lanes = slice(part * 128, (part + 1) * 128)
        out_ref[:, lanes] = (gained_ref[:, lanes] * factor).astype(BF)


def attend(keys, values, query, mask):
    scores = lax.dot_general(
        keys, query, (((1,), (1,)), ((), ())), preferred_element_type=F32
    ) * (math.log2(math.e) / math.sqrt(HEAD))
    scores = mask(scores)
    top = jnp.max(scores, 0, keepdims=True)
    weights = jnp.exp2(scores - top)
    total = jnp.sum(weights, 0, keepdims=True)
    mixed = lax.dot_general(
        values, weights.astype(BF), (((0,), (0,)), ((), ())), preferred_element_type=F32
    )
    return top, total, mixed


def attend_kernel(place_ref, q_ref, got_ref, rates_ref, out_ref):
    y, _, v, u = digits(place_ref[0])
    write_messages(place_ref[0], got_ref, rates_ref, out_ref)

    def half(first):
        keys = got_ref[:, first : first + TOK, :].reshape(8 * TOK, HEAD)
        return keys, got_ref[:, first + TOK : first + 2 * TOK, :].reshape(8 * TOK, HEAD)

    own, other = half(0), half(PACK)
    row = lax.broadcasted_iota(jnp.int32, (8 * TOK, 1), 0)
    block = row // TOK
    key_pos = ((block // 2) * 8 + 2 * v + block % 2) * TOK + row % TOK
    which = lax.broadcasted_iota(jnp.int32, (16, 128), 0)

    def query_of(tile):
        return q_ref[tile * BLOCKS : (tile + 1) * BLOCKS].reshape(WIDE, HEAD)

    def own_part(tile):
        lane = lax.broadcasted_iota(jnp.int32, (1, WIDE), 1) + tile * WIDE
        q_block = lane // TOK
        q_pos = ((q_block // 4) * 8 + 2 * (q_block % 4) + u) * TOK + lane % TOK
        return attend(*own, query_of(tile), lambda s: jnp.where(key_pos <= q_pos, s, NEG))

    def write(tile, top, total, mixed):
        mixed = jnp.transpose(mixed).astype(BF)
        level = top + jnp.log2(total)
        high = level.astype(BF).astype(F32)
        rest = level - high
        middle = rest.astype(BF).astype(F32)
        last = rest - middle
        for b in range(BLOCKS):
            place = tile * BLOCKS + b
            out_ref[place, :TOK, :] = mixed[b * TOK : (b + 1) * TOK]
            part = slice((b // 2) * 128, (b // 2) * 128 + 128)
            stats = jnp.where(
                which == 0,
                high[:, part],
                jnp.where(which == 1, middle[:, part], jnp.where(which == 2, last[:, part], 0.0)),
            )
            out_ref[place, TOK:80, :] = stats.astype(BF)

    @pl.when(y == 0)
    def _():
        for tile in range(16 * TOK // WIDE):
            top, total, mixed = own_part(tile)
            write(tile, top, total, mixed * (1.0 / total))

    @pl.when(y == 1)
    def _():
        for tile in range(16 * TOK // WIDE):
            top_a, total_a, mixed_a = own_part(tile)
            top_b, total_b, mixed_b = attend(*other, query_of(tile), lambda s: s)
            top = jnp.maximum(top_a, top_b)
            scale_a, scale_b = jnp.exp2(top_a - top), jnp.exp2(top_b - top)
            total = total_a * scale_a + total_b * scale_b
            inverse = 1.0 / total
            write(tile, top, total, mixed_a * (scale_a * inverse) + mixed_b * (scale_b * inverse))


def merge(index, got_ref, out_ref):
    odd = digits(index)[2] % 2
    levels = jnp.sum(got_ref[:, TOK:80, :].astype(F32), 1)
    levels = jnp.where(odd == 1, pltpu.roll(levels, TOK, 1), levels)
    weights = []
    for h in range(HEADS_DEV):
        part = levels[h * 4 : (h + 1) * 4]
        part = jnp.exp2(part - jnp.max(part, 0, keepdims=True))
        weights.append(part / jnp.sum(part, 0, keepdims=True))
    weights = jnp.concatenate(weights + [jnp.zeros((112, 128), F32)], 0)
    weights = jnp.transpose(weights)[:TOK, :]
    for h in range(HEADS_DEV):
        total = jnp.zeros((TOK, HEAD), F32)
        for k in range(4):
            place = h * 4 + k
            total = total + weights[:, place : place + 1] * got_ref[place, :TOK, :].astype(F32)
        out_ref[:, h * HEAD : (h + 1) * HEAD] = total.astype(BF)


def tail_kernel(
    place_ref, got_ref, coeff_ref, rates_ref, near_ref, gate_ref, gain_ref, gained_ref, square_ref, out_ref
):
    squares = jnp.zeros((TOK, 128), F32)
    for part in range(CH // 128):
        lanes = slice(part * 128, (part + 1) * 128)
        state = got_ref[part * 4, 80:96, :].astype(F32)
        for j in range(1, 4):
            state = state + got_ref[part * 4 + j, 80:96, :].astype(F32)
        tiles = expand(rates_ref[:, lanes], coeff_ref[:, lanes] * state, 1)
        gated = gate_ref[:, lanes] * (near_ref[:, lanes] + jnp.concatenate(tiles, 0))
        gained_ref[:, lanes] = gated * gain_ref[:, lanes]
        squares = squares + gated * gated
    total = jnp.broadcast_to(jnp.sum(squares, 1, keepdims=True), (TOK, 128))
    total = jnp.concatenate([total, jnp.zeros((TOK, 128), F32)], 0)
    square_ref[...] = jnp.transpose(total)[:8, :]
    merge(place_ref[0], got_ref, out_ref)


def exchange(value, groups):
    return lax.all_to_all(value, "context", 0, 0, axis_index_groups=groups, tiled=True)


def local(features, feat_weight, skip, residues, rates, norm_gain, attn_in):
    index = lax.axis_index("context")
    devices = lax.axis_size("context")
    place = index.astype(jnp.int32)[None]
    features = jnp.transpose(features, (1, 0, 2))
    attn_in = jnp.transpose(attn_in, (1, 0, 2))
    rim = lax.ppermute(
        features[:, TOK - (FEAT - 1) :], "context", [(s, s + 1) for s in range(devices - 1)]
    )

    coeff = residues * jnp.sqrt(-jnp.expm1(-2.0 * rates))
    inverse = jnp.exp(
        jnp.arange(HEAD // 2, dtype=F32) * (-2.0 * math.log(ROPE_BASE) / HEAD)
    )
    positions = (index * TOK + jnp.arange(TOK)).astype(F32)
    angle = positions[:, None] * inverse[None, :]
    cosine, sine = jnp.cos(angle), jnp.sin(angle)
    cosine = jnp.concatenate([cosine, cosine], 1)
    sine = jnp.concatenate([-sine, sine], 1)

    queries, pairs = call(
        rotate_kernel,
        [((16, TOK, HEAD), BF), ((HEADS_DEV, 2 * TOK, HEAD), BF)],
        [VMEM] * 3,
        1000000000,
    )(attn_in, cosine, sine)
    over_y = [(s, s + devices // 2) for s in range(devices // 2)]
    far_pairs = lax.ppermute(pairs, "context", over_y)
    queries = exchange(queries, Q_GROUPS)

    rim = jnp.pad(rim.astype(F32), ((0, 0), (6, 0), (0, 0)))
    states, gate, product = call(
        state_kernel,
        [((HEADS_DEV, MODES, HEAD), BF), ((TOK, CH), F32), ((TOK, CH), F32)],
        [VMEM] * 4,
        1000000,
    )(features, rim, feat_weight, rates)
    far_states = lax.ppermute(states, "context", over_y)
    (near,) = call(
        near_kernel,
        [((TOK, CH), F32)],
        [VMEM] * 4,
        1000000,
        [pltpu.VMEM((2 * TOK, CH), F32), pltpu.VMEM((TOK, CH), F32)],
    )(product, coeff, rates, skip[None, :])
    quarters = jnp.transpose(rates.reshape(MODES, CH // 128, 128), (1, 0, 2))
    (both,) = call(join_kernel, [((8, 2 * PACK, HEAD), BF)], [VMEM] * 4, 50000000000)(
        pairs, states, far_pairs, far_states
    )
    queries, both, coeff, quarters, near, gain = lax.optimization_barrier(
        (queries, both, coeff, quarters, near, norm_gain[None, :])
    )
    got = exchange(both, KV_GROUPS)
    (partial,) = call(
        attend_kernel,
        [((16, TOK + 32, HEAD), BF)],
        [SMEM] + [VMEM] * 3,
        4000000000,
    )(place, queries, got, quarters)
    partial = exchange(partial, Q_GROUPS)

    gained, squares, attn_out = call(
        tail_kernel,
        [((TOK, CH), F32), ((8, 128), F32), ((TOK, CH), BF)],
        [SMEM] + [VMEM] * 6,
        1000000000,
    )(place, partial, coeff, rates, near, gate, gain)
    squares = lax.all_to_all(squares, "dp", 0, 0, tiled=True)
    (hyena_out,) = call(norm_kernel, [((TOK, CH), BF)], [VMEM] * 2, 100000000)(squares, gained)
    return (hyena_out, attn_out)


def solution(mesh):
    return jax.shard_map(
        local,
        mesh=mesh,
        in_specs=(
            P("context", None, "dp"),
            P(None, None, "dp"),
            P("dp"),
            P(None, "dp"),
            P(None, "dp"),
            P("dp"),
            P("context", None, "dp"),
        ),
        out_specs=(P("context", "dp"), P("context", "dp")),
        check_vma=False,
    )
```

```python
import functools
import itertools
import math

import jax
import jax.numpy as jnp
from jax import lax
from jax.experimental import pallas as pl
from jax.experimental.pallas import tpu as pltpu
from jax.sharding import PartitionSpec as P

DH = 4096
HEAD = 128
HEADS_DEV = 4
FEAT = 3
MODES = 16
TOK = 64
CH = 512
ROPE_BASE = 1000000.0
NEG = -1e30
PACK = 2 * TOK + MODES
WIDE = 512
BLOCKS = WIDE // TOK
BF = jnp.bfloat16
F32 = jnp.float32

DIGITS = {"y": (2, 32), "x": (4, 8), "v": (4, 2), "u": (2, 1)}


def groups_over(*free):
    fixed = [d for d in DIGITS if d not in free]

    def places(names):
        return [
            sum(v * DIGITS[d][1] for v, d in zip(values, names))
            for values in itertools.product(*[range(DIGITS[d][0]) for d in names])
        ]

    return [[base + step for step in places(free)] for base in places(fixed)]


Q_GROUPS = groups_over("x", "v")
KV_GROUPS = groups_over("x", "u")

VMEM = pl.BlockSpec(memory_space=pltpu.VMEM)
SMEM = pl.BlockSpec(memory_space=pltpu.SMEM)


def call(kernel, outs, specs, flops, scratch=()):
    return pl.pallas_call(
        kernel,
        out_shape=[jax.ShapeDtypeStruct(s, d) for s, d in outs],
        in_specs=specs,
        out_specs=[VMEM] * len(outs),
        scratch_shapes=list(scratch),
        compiler_params=pltpu.CompilerParams(vmem_limit_bytes=16 * 1024 * 1024),
        cost_estimate=pl.CostEstimate(flops=flops, bytes_accessed=1000, transcendentals=0),
    )


def digits(index):
    return [(index // step) % size for size, step in DIGITS.values()]


def expand(rates, weights, start):
    ahead = (lax.broadcasted_iota(jnp.int32, (8, 128), 0) + start).astype(F32)
    bases = [jnp.exp(-rates[n : n + 1, :] * ahead) for n in range(MODES)]
    tiles = []
    for a in range(8):
        scaled = weights * jnp.exp(rates * (-8.0 * a))
        tiles.append(sum(bases[n] * scaled[n : n + 1, :] for n in range(MODES)))
    return tiles


def rotate_kernel(attn_ref, cos_ref, sin_ref, q_ref, kv_ref):
    cosine, sine = cos_ref[...], sin_ref[...]
    for g in range(2):
        x = attn_ref[g].astype(F32)
        for h in range(HEADS_DEV):
            part = x[:, h * HEAD : (h + 1) * HEAD]
            turned = (part * cosine + pltpu.roll(part, HEAD // 2, 1) * sine).astype(BF)
            if g == 0:
                for w in range(4):
                    q_ref[h * 4 + w] = turned
            else:
                kv_ref[h, :TOK, :] = turned
    for h in range(HEADS_DEV):
        kv_ref[h, TOK:, :] = attn_ref[2, :, h * HEAD : (h + 1) * HEAD]


def state_kernel(feat_ref, rim_ref, weight_ref, rates_ref, state_ref, gate_ref, prod_ref):
    groups = []
    for g in range(3):
        x = jnp.concatenate([rim_ref[g], feat_ref[g].astype(F32)], 0)
        total = weight_ref[0, g : g + 1, :] * x[8 : 8 + TOK]
        for o in range(1, FEAT):
            total = total + weight_ref[o, g : g + 1, :] * x[8 - o : 8 - o + TOK]
        groups.append(total)
    gate_ref[...] = groups[0]
    product = (groups[1] * groups[2]).astype(BF).astype(F32)
    prod_ref[...] = product
    back = (7 - lax.broadcasted_iota(jnp.int32, (8, 128), 0)).astype(F32)
    for part in range(CH // 128):
        lanes = slice(part * 128, (part + 1) * 128)
        step = jnp.exp(-8.0 * rates_ref[:, lanes])
        rows = []
        for n in range(MODES):
            total = product[:8, lanes]
            for a in range(1, 8):
                total = total * step[n : n + 1, :] + product[8 * a : 8 * a + 8, lanes]
            total = total * jnp.exp(-rates_ref[n : n + 1, lanes] * back)
            rows.append(jnp.sum(total, 0, keepdims=True))
        state_ref[part] = jnp.concatenate(rows, 0).astype(BF)


def join_kernel(pair_ref, state_ref, far_pair_ref, far_state_ref, out_ref):
    for peer in range(8):
        head = peer // 2
        out_ref[peer, : 2 * TOK, :] = pair_ref[head]
        out_ref[peer, 2 * TOK : PACK, :] = state_ref[head]
        out_ref[peer, PACK : PACK + 2 * TOK, :] = far_pair_ref[head]
        out_ref[peer, PACK + 2 * TOK :, :] = far_state_ref[head]


def near_kernel(prod_ref, coeff_ref, rates_ref, skip_ref, out_ref, padded, impulse):
    padded[:TOK, :] = jnp.zeros((TOK, CH), F32)
    padded[TOK:, :] = prod_ref[...]
    for part in range(CH // 128):
        lanes = slice(part * 128, (part + 1) * 128)
        rows = expand(rates_ref[:, lanes], coeff_ref[:, lanes], 0)
        for a in range(8):
            impulse[8 * a : 8 * a + 8, lanes] = rows[a]
        y = skip_ref[:, lanes] * prod_ref[:, lanes]
        for t in range(TOK):
            y = y + impulse[t : t + 1, lanes] * padded[TOK - t : 2 * TOK - t, lanes]
        out_ref[:, lanes] = y


def write_messages(index, got_ref, rates_ref, out_ref):
    y, x, v, u = digits(index)
    decay = rates_ref[x] * (-float(TOK))
    second = jnp.where(y == 1, 1.0, 0.0).astype(F32)

    def faded(steps):
        return jnp.exp(decay * jnp.maximum(steps, 0).astype(F32))

    own_states = [got_ref[i, 2 * TOK : PACK, :].astype(F32) for i in range(8)]
    other_states = [got_ref[i, PACK + 2 * TOK :, :].astype(F32) * second for i in range(8)]
    reach = [faded(2 * (vt - v) + 6) for vt in range(4)]
    near_steps = [[2 * (vt - v) + u - us - 1 for us in range(2)] for vt in range(4)]
    close = [
        [faded(steps) * jnp.where(steps >= 0, 1.0, 0.0).astype(F32) for steps in pair]
        for pair in near_steps
    ]
    before = {(dx, us): faded(8 * dx - 7 + u - us) for dx in range(1, 4) for us in range(2)}
    across = {(dx, us): faded(8 * dx + 25 + u - us) for dx in range(-3, 4) for us in range(2)}
    for xt in range(4):
        total = jnp.zeros((MODES, 128), F32)
        for xs in range(4):
            for us in range(2):
                total = total + across[xt - xs, us] * other_states[xs * 2 + us]
                if xs < xt:
                    total = total + before[xt - xs, us] * own_states[xs * 2 + us]
        for vt in range(4):
            state = reach[vt] * total
            for us in range(2):
                state = state + close[vt][us] * own_states[xt * 2 + us]
            out_ref[xt * 4 + vt, 80:96, :] = state.astype(BF)


def norm_kernel(square_ref, gained_ref, out_ref):
    total = jnp.sum(square_ref[...], 0, keepdims=True)
    total = jnp.transpose(jnp.broadcast_to(total, (128, 128)))[:TOK, :]
    factor = lax.rsqrt(total * (1.0 / DH) + 1e-06)
    for part in range(CH // 128):
        lanes = slice(part * 128, (part + 1) * 128)
        out_ref[:, lanes] = (gained_ref[:, lanes] * factor).astype(BF)


def attend(keys, values, query, mask):
    scores = lax.dot_general(
        query, keys, (((1,), (1,)), ((), ())), preferred_element_type=F32
    ) * (math.log2(math.e) / math.sqrt(HEAD))
    scores = mask(scores)
    top = jnp.max(scores, 1, keepdims=True)
    weights = jnp.exp2(scores - top)
    total = jnp.sum(weights, 1, keepdims=True)
    mixed = lax.dot_general(
        weights.astype(BF), values, (((1,), (0,)), ((), ())), preferred_element_type=F32
    )
    return top, total, mixed


def attend_kernel(place_ref, q_ref, got_ref, rates_ref, out_ref):
    y, _, v, u = digits(place_ref[0])
    write_messages(place_ref[0], got_ref, rates_ref, out_ref)

    def half(first):
        keys = got_ref[:, first : first + TOK, :].reshape(8 * TOK, HEAD)
        return keys, got_ref[:, first + TOK : first + 2 * TOK, :].reshape(8 * TOK, HEAD)

    own, other = half(0), half(PACK)
    lane = lax.broadcasted_iota(jnp.int32, (1, 8 * TOK), 1)
    block = lane // TOK
    key_pos = ((block // 2) * 8 + 2 * v + block % 2) * TOK + lane % TOK
    which = lax.broadcasted_iota(jnp.int32, (16, 128), 0)

    def query_of(tile):
        return q_ref[tile * BLOCKS : (tile + 1) * BLOCKS].reshape(WIDE, HEAD)

    def own_part(tile):
        row = lax.broadcasted_iota(jnp.int32, (WIDE, 1), 0) + tile * WIDE
        q_block = row // TOK
        q_pos = ((q_block // 4) * 8 + 2 * (q_block % 4) + u) * TOK + row % TOK
        return attend(*own, query_of(tile), lambda s: jnp.where(key_pos <= q_pos, s, NEG))

    def write(tile, top, total, mixed):
        mixed = mixed.astype(BF).reshape(BLOCKS, TOK, HEAD)
        out_ref[tile * BLOCKS : (tile + 1) * BLOCKS, :TOK, :] = mixed
        level = jnp.broadcast_to(top + jnp.log2(total), (WIDE, 128))
        for pair in range(WIDE // 128):
            row = jnp.transpose(level[pair * 128 : (pair + 1) * 128])[:1, :]
            high = row.astype(BF).astype(F32)
            rest = row - high
            middle = rest.astype(BF).astype(F32)
            last = rest - middle
            stats = jnp.where(
                which == 0,
                high,
                jnp.where(which == 1, middle, jnp.where(which == 2, last, 0.0)),
            ).astype(BF)
            for b in range(2):
                out_ref[tile * BLOCKS + 2 * pair + b, TOK:80, :] = stats

    @pl.when(y == 0)
    def _():
        for tile in range(16 * TOK // WIDE):
            top, total, mixed = own_part(tile)
            write(tile, top, total, mixed * (1.0 / total))

    @pl.when(y == 1)
    def _():
        for tile in range(16 * TOK // WIDE):
            top_a, total_a, mixed_a = own_part(tile)
            top_b, total_b, mixed_b = attend(*other, query_of(tile), lambda s: s)
            top = jnp.maximum(top_a, top_b)
            scale_a, scale_b = jnp.exp2(top_a - top), jnp.exp2(top_b - top)
            total = total_a * scale_a + total_b * scale_b
            inverse = 1.0 / total
            write(tile, top, total, mixed_a * (scale_a * inverse) + mixed_b * (scale_b * inverse))


def merge(index, got_ref, out_ref):
    odd = digits(index)[2] % 2
    levels = jnp.sum(got_ref[:, TOK:80, :].astype(F32), 1)
    levels = jnp.where(odd == 1, pltpu.roll(levels, TOK, 1), levels)
    weights = []
    for h in range(HEADS_DEV):
        part = levels[h * 4 : (h + 1) * 4]
        part = jnp.exp2(part - jnp.max(part, 0, keepdims=True))
        weights.append(part / jnp.sum(part, 0, keepdims=True))
    weights = jnp.concatenate(weights + [jnp.zeros((112, 128), F32)], 0)
    weights = jnp.transpose(weights)[:TOK, :]
    for h in range(HEADS_DEV):
        total = jnp.zeros((TOK, HEAD), F32)
        for k in range(4):
            place = h * 4 + k
            total = total + weights[:, place : place + 1] * got_ref[place, :TOK, :].astype(F32)
        out_ref[:, h * HEAD : (h + 1) * HEAD] = total.astype(BF)


def tail_kernel(
    place_ref, got_ref, coeff_ref, rates_ref, near_ref, gate_ref, gain_ref, gained_ref, square_ref, out_ref
):
    squares = jnp.zeros((TOK, 128), F32)
    for part in range(CH // 128):
        lanes = slice(part * 128, (part + 1) * 128)
        state = got_ref[part * 4, 80:96, :].astype(F32)
        for j in range(1, 4):
            state = state + got_ref[part * 4 + j, 80:96, :].astype(F32)
        tiles = expand(rates_ref[:, lanes], coeff_ref[:, lanes] * state, 1)
        gated = gate_ref[:, lanes] * (near_ref[:, lanes] + jnp.concatenate(tiles, 0))
        gained_ref[:, lanes] = gated * gain_ref[:, lanes]
        squares = squares + gated * gated
    total = jnp.broadcast_to(jnp.sum(squares, 1, keepdims=True), (TOK, 128))
    total = jnp.concatenate([total, jnp.zeros((TOK, 128), F32)], 0)
    square_ref[...] = jnp.transpose(total)[:8, :]
    merge(place_ref[0], got_ref, out_ref)


def exchange(value, groups):
    return lax.all_to_all(value, "context", 0, 0, axis_index_groups=groups, tiled=True)


def local(features, feat_weight, skip, residues, rates, norm_gain, attn_in):
    index = lax.axis_index("context")
    devices = lax.axis_size("context")
    place = index.astype(jnp.int32)[None]
    features = jnp.transpose(features, (1, 0, 2))
    attn_in = jnp.transpose(attn_in, (1, 0, 2))
    rim = lax.ppermute(
        features[:, TOK - (FEAT - 1) :], "context", [(s, s + 1) for s in range(devices - 1)]
    )

    coeff = residues * jnp.sqrt(-jnp.expm1(-2.0 * rates))
    inverse = jnp.exp(
        jnp.arange(HEAD // 2, dtype=F32) * (-2.0 * math.log(ROPE_BASE) / HEAD)
    )
    positions = (index * TOK + jnp.arange(TOK)).astype(F32)
    angle = positions[:, None] * inverse[None, :]
    cosine, sine = jnp.cos(angle), jnp.sin(angle)
    cosine = jnp.concatenate([cosine, cosine], 1)
    sine = jnp.concatenate([-sine, sine], 1)

    queries, pairs = call(
        rotate_kernel,
        [((16, TOK, HEAD), BF), ((HEADS_DEV, 2 * TOK, HEAD), BF)],
        [VMEM] * 3,
        1000000000,
    )(attn_in, cosine, sine)
    over_y = [(s, s + devices // 2) for s in range(devices // 2)]
    far_pairs = lax.ppermute(pairs, "context", over_y)
    queries = exchange(queries, Q_GROUPS)

    rim = jnp.pad(rim.astype(F32), ((0, 0), (6, 0), (0, 0)))
    states, gate, product = call(
        state_kernel,
        [((HEADS_DEV, MODES, HEAD), BF), ((TOK, CH), F32), ((TOK, CH), F32)],
        [VMEM] * 4,
        1000000,
    )(features, rim, feat_weight, rates)
    far_states = lax.ppermute(states, "context", over_y)
    (near,) = call(
        near_kernel,
        [((TOK, CH), F32)],
        [VMEM] * 4,
        1000000,
        [pltpu.VMEM((2 * TOK, CH), F32), pltpu.VMEM((TOK, CH), F32)],
    )(product, coeff, rates, skip[None, :])
    quarters = jnp.transpose(rates.reshape(MODES, CH // 128, 128), (1, 0, 2))
    (both,) = call(join_kernel, [((8, 2 * PACK, HEAD), BF)], [VMEM] * 4, 50000000000)(
        pairs, states, far_pairs, far_states
    )
    queries, both, coeff, quarters, near, gain = lax.optimization_barrier(
        (queries, both, coeff, quarters, near, norm_gain[None, :])
    )
    got = exchange(both, KV_GROUPS)
    (partial,) = call(
        attend_kernel,
        [((16, TOK + 32, HEAD), BF)],
        [SMEM] + [VMEM] * 3,
        4000000000,
    )(place, queries, got, quarters)
    partial = exchange(partial, Q_GROUPS)

    gained, squares, attn_out = call(
        tail_kernel,
        [((TOK, CH), F32), ((8, 128), F32), ((TOK, CH), BF)],
        [SMEM] + [VMEM] * 6,
        1000000000,
    )(place, partial, coeff, rates, near, gate, gain)
    squares = lax.all_to_all(squares, "dp", 0, 0, tiled=True)
    (hyena_out,) = call(norm_kernel, [((TOK, CH), BF)], [VMEM] * 2, 100000000)(squares, gained)
    return (hyena_out, attn_out)


def solution(mesh):
    return jax.shard_map(
        local,
        mesh=mesh,
        in_specs=(
            P("context", None, "dp"),
            P(None, None, "dp"),
            P("dp"),
            P(None, "dp"),
            P(None, "dp"),
            P("dp"),
            P("context", None, "dp"),
        ),
        out_specs=(P("context", "dp"), P("context", "dp")),
        check_vma=False,
    )
```

```python
import functools
import itertools
import math

import jax
import jax.numpy as jnp
from jax import lax
from jax.experimental import pallas as pl
from jax.experimental.pallas import tpu as pltpu
from jax.sharding import PartitionSpec as P

DH = 4096
HEAD = 128
HEADS_DEV = 4
FEAT = 3
MODES = 16
TOK = 64
CH = 512
ROPE_BASE = 1000000.0
NEG = -1e30
PACK = 2 * TOK + MODES
WIDE = 512
BLOCKS = WIDE // TOK
BF = jnp.bfloat16
F32 = jnp.float32

DIGITS = {"y": (2, 32), "s": (2, 16), "r": (2, 8), "v": (4, 2), "u": (2, 1)}


def groups_over(*free):
    fixed = [d for d in DIGITS if d not in free]

    def places(names):
        return [
            sum(v * DIGITS[d][1] for v, d in zip(values, names))
            for values in itertools.product(*[range(DIGITS[d][0]) for d in names])
        ]

    return [[base + step for step in places(free)] for base in places(fixed)]


Q_GROUPS = groups_over("r", "v", "u")
KV_GROUPS = groups_over("s", "r", "u")

VMEM = pl.BlockSpec(memory_space=pltpu.VMEM)
SMEM = pl.BlockSpec(memory_space=pltpu.SMEM)


def call(kernel, outs, specs, flops, scratch=()):
    return pl.pallas_call(
        kernel,
        out_shape=[jax.ShapeDtypeStruct(s, d) for s, d in outs],
        in_specs=specs,
        out_specs=[VMEM] * len(outs),
        scratch_shapes=list(scratch),
        compiler_params=pltpu.CompilerParams(vmem_limit_bytes=16 * 1024 * 1024),
        cost_estimate=pl.CostEstimate(flops=flops, bytes_accessed=1000, transcendentals=0),
    )


def digits(index):
    return [(index // step) % size for size, step in DIGITS.values()]


def member(head, v):
    return (head // 2) * 8 + v * 2 + head % 2


def expand(rates, weights, start):
    ahead = (lax.broadcasted_iota(jnp.int32, (8, 128), 0) + start).astype(F32)
    bases = [jnp.exp(-rates[n : n + 1, :] * ahead) for n in range(MODES)]
    tiles = []
    for a in range(8):
        scaled = weights * jnp.exp(rates * (-8.0 * a))
        tiles.append(sum(bases[n] * scaled[n : n + 1, :] for n in range(MODES)))
    return tiles


def rotate_kernel(attn_ref, cos_ref, sin_ref, q_ref, kv_ref):
    cosine, sine = cos_ref[...], sin_ref[...]
    for g in range(2):
        x = attn_ref[g].astype(F32)
        for h in range(HEADS_DEV):
            part = x[:, h * HEAD : (h + 1) * HEAD]
            turned = (part * cosine + pltpu.roll(part, HEAD // 2, 1) * sine).astype(BF)
            if g == 0:
                for v in range(4):
                    q_ref[member(h, v)] = turned
            else:
                kv_ref[h, :TOK, :] = turned
    for h in range(HEADS_DEV):
        kv_ref[h, TOK:, :] = attn_ref[2, :, h * HEAD : (h + 1) * HEAD]


def state_kernel(feat_ref, rim_ref, weight_ref, rates_ref, state_ref, gate_ref, prod_ref):
    groups = []
    for g in range(3):
        x = jnp.concatenate([rim_ref[g], feat_ref[g].astype(F32)], 0)
        total = weight_ref[0, g : g + 1, :] * x[8 : 8 + TOK]
        for o in range(1, FEAT):
            total = total + weight_ref[o, g : g + 1, :] * x[8 - o : 8 - o + TOK]
        groups.append(total)
    gate_ref[...] = groups[0]
    product = (groups[1] * groups[2]).astype(BF).astype(F32)
    prod_ref[...] = product
    back = (7 - lax.broadcasted_iota(jnp.int32, (8, 128), 0)).astype(F32)
    for part in range(CH // 128):
        lanes = slice(part * 128, (part + 1) * 128)
        step = jnp.exp(-8.0 * rates_ref[:, lanes])
        rows = []
        for n in range(MODES):
            total = product[:8, lanes]
            for a in range(1, 8):
                total = total * step[n : n + 1, :] + product[8 * a : 8 * a + 8, lanes]
            total = total * jnp.exp(-rates_ref[n : n + 1, lanes] * back)
            rows.append(jnp.sum(total, 0, keepdims=True))
        state_ref[part] = jnp.concatenate(rows, 0).astype(BF)


def join_kernel(pair_ref, state_ref, far_pair_ref, far_state_ref, out_ref):
    for peer in range(8):
        head = peer % 4
        out_ref[peer, : 2 * TOK, :] = pair_ref[head]
        out_ref[peer, 2 * TOK : PACK, :] = state_ref[head]
        out_ref[peer, PACK : PACK + 2 * TOK, :] = far_pair_ref[head]
        out_ref[peer, PACK + 2 * TOK :, :] = far_state_ref[head]


def near_kernel(prod_ref, coeff_ref, rates_ref, skip_ref, out_ref, padded, impulse):
    padded[:TOK, :] = jnp.zeros((TOK, CH), F32)
    padded[TOK:, :] = prod_ref[...]
    for part in range(CH // 128):
        lanes = slice(part * 128, (part + 1) * 128)
        rows = expand(rates_ref[:, lanes], coeff_ref[:, lanes], 0)
        for a in range(8):
            impulse[8 * a : 8 * a + 8, lanes] = rows[a]
        y = skip_ref[:, lanes] * prod_ref[:, lanes]
        for t in range(TOK):
            y = y + impulse[t : t + 1, lanes] * padded[TOK - t : 2 * TOK - t, lanes]
        out_ref[:, lanes] = y


def write_messages(index, got_ref, rates_ref, out_ref):
    y, s, r, v, u = digits(index)
    decay = rates_ref[2 * r + u] * (-float(TOK))

    def faded(steps):
        return jnp.exp(decay * jnp.maximum(steps, 0).astype(F32))

    def when(condition):
        return jnp.where(condition, 1.0, 0.0).astype(F32)

    second = when(y == 1)
    own_states = [got_ref[i, 2 * TOK : PACK, :].astype(F32) for i in range(8)]
    other_states = [got_ref[i, PACK + 2 * TOK :, :].astype(F32) * second for i in range(8)]
    reach, close = {}, {}
    for vt in range(4):
        for du in (-1, 0, 1):
            steps = 2 * (vt - v) + du - 1
            reach[vt, du] = faded(steps + 8)
            close[vt, du] = faded(steps) * when(steps >= 0)
    for rt in range(2):
        before = [jnp.zeros((MODES, 128), F32) for _ in range(2)]
        level = [jnp.zeros((MODES, 128), F32) for _ in range(2)]
        for pair in range(4):
            gap = 16 * (s - pair // 2) + 8 * (rt - pair % 2)
            earlier = faded(gap - 8) * when(gap > 0)
            across = faded(gap + 24)
            for us in range(2):
                i = pair * 2 + us
                before[us] = before[us] + earlier * own_states[i] + across * other_states[i]
                level[us] = level[us] + when(gap == 0) * own_states[i]
        for vt in range(4):
            for ut in range(2):
                state = jnp.zeros((MODES, 128), F32)
                for us in range(2):
                    state = state + reach[vt, ut - us] * before[us] + close[vt, ut - us] * level[us]
                out_ref[rt * 8 + vt * 2 + ut, 80:96, :] = state.astype(BF)


def norm_kernel(square_ref, gained_ref, out_ref):
    total = jnp.sum(square_ref[...], 0, keepdims=True)
    total = jnp.transpose(jnp.broadcast_to(total, (128, 128)))[:TOK, :]
    factor = lax.rsqrt(total * (1.0 / DH) + 1e-06)
    for part in range(CH // 128):
        lanes = slice(part * 128, (part + 1) * 128)
        out_ref[:, lanes] = (gained_ref[:, lanes] * factor).astype(BF)


def attend(keys, values, query, mask):
    scores = lax.dot_general(
        query, keys, (((1,), (1,)), ((), ())), preferred_element_type=F32
    ) * (math.log2(math.e) / math.sqrt(HEAD))
    scores = mask(scores)
    top = jnp.max(scores, 1, keepdims=True)
    weights = jnp.exp2(scores - top)
    total = jnp.sum(weights, 1, keepdims=True)
    mixed = lax.dot_general(
        weights.astype(BF), values, (((1,), (0,)), ((), ())), preferred_element_type=F32
    )
    return top, total, mixed


def attend_kernel(place_ref, q_ref, got_ref, rates_ref, out_ref):
    y, s, _, v, _ = digits(place_ref[0])
    write_messages(place_ref[0], got_ref, rates_ref, out_ref)

    def half(first):
        keys = got_ref[:, first : first + TOK, :].reshape(8 * TOK, HEAD)
        return keys, got_ref[:, first + TOK : first + 2 * TOK, :].reshape(8 * TOK, HEAD)

    own, other = half(0), half(PACK)
    lane = lax.broadcasted_iota(jnp.int32, (1, 8 * TOK), 1)
    block = lane // TOK
    key_pos = ((block // 4) * 16 + ((block // 2) % 2) * 8 + 2 * v + block % 2) * TOK + lane % TOK
    which = lax.broadcasted_iota(jnp.int32, (16, 128), 0)

    def query_of(tile):
        return q_ref[tile * BLOCKS : (tile + 1) * BLOCKS].reshape(WIDE, HEAD)

    def own_part(tile):
        row = lax.broadcasted_iota(jnp.int32, (WIDE, 1), 0) + tile * WIDE
        q_pos = s * (16 * TOK) + row
        return attend(*own, query_of(tile), lambda t: jnp.where(key_pos <= q_pos, t, NEG))

    def write(tile, top, total, mixed):
        mixed = mixed.astype(BF).reshape(BLOCKS, TOK, HEAD)
        out_ref[tile * BLOCKS : (tile + 1) * BLOCKS, :TOK, :] = mixed
        level = jnp.broadcast_to(top + jnp.log2(total), (WIDE, 128))
        for pair in range(WIDE // 128):
            row = jnp.transpose(level[pair * 128 : (pair + 1) * 128])[:1, :]
            high = row.astype(BF).astype(F32)
            rest = row - high
            middle = rest.astype(BF).astype(F32)
            last = rest - middle
            stats = jnp.where(
                which == 0,
                high,
                jnp.where(which == 1, middle, jnp.where(which == 2, last, 0.0)),
            ).astype(BF)
            for b in range(2):
                out_ref[tile * BLOCKS + 2 * pair + b, TOK:80, :] = stats

    @pl.when(y == 0)
    def _():
        for tile in range(16 * TOK // WIDE):
            top, total, mixed = own_part(tile)
            write(tile, top, total, mixed * (1.0 / total))

    @pl.when(y == 1)
    def _():
        for tile in range(16 * TOK // WIDE):
            top_a, total_a, mixed_a = own_part(tile)
            top_b, total_b, mixed_b = attend(*other, query_of(tile), lambda t: t)
            top = jnp.maximum(top_a, top_b)
            scale_a, scale_b = jnp.exp2(top_a - top), jnp.exp2(top_b - top)
            total = total_a * scale_a + total_b * scale_b
            inverse = 1.0 / total
            write(tile, top, total, mixed_a * (scale_a * inverse) + mixed_b * (scale_b * inverse))


def merge(index, got_ref, out_ref):
    odd = index % 2
    levels = jnp.sum(got_ref[:, TOK:80, :].astype(F32), 1)
    levels = jnp.where(odd == 1, pltpu.roll(levels, TOK, 1), levels)
    weights = []
    for h in range(HEADS_DEV):
        part = jnp.concatenate([levels[member(h, k) : member(h, k) + 1] for k in range(4)], 0)
        part = jnp.exp2(part - jnp.max(part, 0, keepdims=True))
        weights.append(part / jnp.sum(part, 0, keepdims=True))
    weights = jnp.concatenate(weights + [jnp.zeros((112, 128), F32)], 0)
    weights = jnp.transpose(weights)[:TOK, :]
    for h in range(HEADS_DEV):
        total = jnp.zeros((TOK, HEAD), F32)
        for k in range(4):
            place = h * 4 + k
            got = got_ref[member(h, k), :TOK, :].astype(F32)
            total = total + weights[:, place : place + 1] * got
        out_ref[:, h * HEAD : (h + 1) * HEAD] = total.astype(BF)


def tail_kernel(
    place_ref, got_ref, coeff_ref, rates_ref, near_ref, gate_ref, gain_ref, gained_ref, square_ref, out_ref
):
    squares = jnp.zeros((TOK, 128), F32)
    for part in range(CH // 128):
        lanes = slice(part * 128, (part + 1) * 128)
        state = got_ref[member(part, 0), 80:96, :].astype(F32)
        for v in range(1, 4):
            state = state + got_ref[member(part, v), 80:96, :].astype(F32)
        tiles = expand(rates_ref[:, lanes], coeff_ref[:, lanes] * state, 1)
        gated = gate_ref[:, lanes] * (near_ref[:, lanes] + jnp.concatenate(tiles, 0))
        gained_ref[:, lanes] = gated * gain_ref[:, lanes]
        squares = squares + gated * gated
    total = jnp.broadcast_to(jnp.sum(squares, 1, keepdims=True), (TOK, 128))
    total = jnp.concatenate([total, jnp.zeros((TOK, 128), F32)], 0)
    square_ref[...] = jnp.transpose(total)[:8, :]
    merge(place_ref[0], got_ref, out_ref)


def exchange(value, groups):
    return lax.all_to_all(value, "context", 0, 0, axis_index_groups=groups, tiled=True)


def local(features, feat_weight, skip, residues, rates, norm_gain, attn_in):
    index = lax.axis_index("context")
    devices = lax.axis_size("context")
    place = index.astype(jnp.int32)[None]
    features = jnp.transpose(features, (1, 0, 2))
    attn_in = jnp.transpose(attn_in, (1, 0, 2))
    rim = lax.ppermute(
        features[:, TOK - (FEAT - 1) :], "context", [(s, s + 1) for s in range(devices - 1)]
    )

    coeff = residues * jnp.sqrt(-jnp.expm1(-2.0 * rates))
    inverse = jnp.exp(
        jnp.arange(HEAD // 2, dtype=F32) * (-2.0 * math.log(ROPE_BASE) / HEAD)
    )
    positions = (index * TOK + jnp.arange(TOK)).astype(F32)
    angle = positions[:, None] * inverse[None, :]
    cosine, sine = jnp.cos(angle), jnp.sin(angle)
    cosine = jnp.concatenate([cosine, cosine], 1)
    sine = jnp.concatenate([-sine, sine], 1)

    queries, pairs = call(
        rotate_kernel,
        [((16, TOK, HEAD), BF), ((HEADS_DEV, 2 * TOK, HEAD), BF)],
        [VMEM] * 3,
        1000000000,
    )(attn_in, cosine, sine)
    over_y = [(s, s + devices // 2) for s in range(devices // 2)]
    far_pairs = lax.ppermute(pairs, "context", over_y)
    queries = exchange(queries, Q_GROUPS)

    rim = jnp.pad(rim.astype(F32), ((0, 0), (6, 0), (0, 0)))
    states, gate, product = call(
        state_kernel,
        [((HEADS_DEV, MODES, HEAD), BF), ((TOK, CH), F32), ((TOK, CH), F32)],
        [VMEM] * 4,
        1000000,
    )(features, rim, jnp.pad(feat_weight, ((0, 0), (0, 5), (0, 0))), rates)
    far_states = lax.ppermute(states, "context", over_y)
    (near,) = call(
        near_kernel,
        [((TOK, CH), F32)],
        [VMEM] * 4,
        1000000,
        [pltpu.VMEM((2 * TOK, CH), F32), pltpu.VMEM((TOK, CH), F32)],
    )(product, coeff, rates, skip[None, :])
    quarters = jnp.transpose(rates.reshape(MODES, CH // 128, 128), (1, 0, 2))
    (both,) = call(join_kernel, [((8, 2 * PACK, HEAD), BF)], [VMEM] * 4, 50000000000)(
        pairs, states, far_pairs, far_states
    )
    queries, both, coeff, quarters, near, gain = lax.optimization_barrier(
        (queries, both, coeff, quarters, near, norm_gain[None, :])
    )
    got = exchange(both, KV_GROUPS)
    (partial,) = call(
        attend_kernel,
        [((16, TOK + 32, HEAD), BF)],
        [SMEM] + [VMEM] * 3,
        4000000000,
    )(place, queries, got, quarters)
    partial = exchange(partial, Q_GROUPS)

    gained, squares, attn_out = call(
        tail_kernel,
        [((TOK, CH), F32), ((8, 128), F32), ((TOK, CH), BF)],
        [SMEM] + [VMEM] * 6,
        1000000000,
    )(place, partial, coeff, rates, near, gate, gain)
    squares = lax.all_to_all(squares, "dp", 0, 0, tiled=True)
    (hyena_out,) = call(norm_kernel, [((TOK, CH), BF)], [VMEM] * 2, 100000000)(squares, gained)
    return (hyena_out, attn_out)


def solution(mesh):
    return jax.shard_map(
        local,
        mesh=mesh,
        in_specs=(
            P("context", None, "dp"),
            P(None, None, "dp"),
            P("dp"),
            P(None, "dp"),
            P(None, "dp"),
            P("dp"),
            P("context", None, "dp"),
        ),
        out_specs=(P("context", "dp"), P("context", "dp")),
        check_vma=False,
    )
```

```python
import functools
import itertools
import math

import jax
import jax.numpy as jnp
from jax import lax
from jax.experimental import pallas as pl
from jax.experimental.pallas import tpu as pltpu
from jax.sharding import PartitionSpec as P

DH = 4096
HEAD = 128
HEADS_DEV = 4
FEAT = 3
MODES = 16
TOK = 64
CH = 512
ROPE_BASE = 1000000.0
NEG = -1e30
PACK = 2 * TOK + MODES
WIDE = 512
BLOCKS = WIDE // TOK
BF = jnp.bfloat16
F32 = jnp.float32

DIGITS = {"y": (2, 32), "s": (2, 16), "r": (2, 8), "v": (4, 2), "u": (2, 1)}


def groups_over(*free):
    fixed = [d for d in DIGITS if d not in free]

    def places(names):
        return [
            sum(v * DIGITS[d][1] for v, d in zip(values, names))
            for values in itertools.product(*[range(DIGITS[d][0]) for d in names])
        ]

    return [[base + step for step in places(free)] for base in places(fixed)]


Q_GROUPS = groups_over("r", "v", "u")
KV_GROUPS = groups_over("s", "r", "u")

VMEM = pl.BlockSpec(memory_space=pltpu.VMEM)
SMEM = pl.BlockSpec(memory_space=pltpu.SMEM)


def call(kernel, outs, specs, flops, scratch=()):
    return pl.pallas_call(
        kernel,
        out_shape=[jax.ShapeDtypeStruct(s, d) for s, d in outs],
        in_specs=specs,
        out_specs=[VMEM] * len(outs),
        scratch_shapes=list(scratch),
        compiler_params=pltpu.CompilerParams(vmem_limit_bytes=16 * 1024 * 1024),
        cost_estimate=pl.CostEstimate(flops=flops, bytes_accessed=1000, transcendentals=0),
    )


def digits(index):
    return [(index // step) % size for size, step in DIGITS.values()]


def member(head, v):
    return (head // 2) * 8 + v * 2 + head % 2


def expand(rates, weights, start):
    ahead = (lax.broadcasted_iota(jnp.int32, (8, 128), 0) + start).astype(F32)
    bases = [jnp.exp(-rates[n : n + 1, :] * ahead) for n in range(MODES)]
    tiles = []
    for a in range(8):
        scaled = weights * jnp.exp(rates * (-8.0 * a))
        tiles.append(sum(bases[n] * scaled[n : n + 1, :] for n in range(MODES)))
    return tiles


def rotated(x, cosine, sine):
    x = x.astype(F32)
    return (x * cosine + pltpu.roll(x, HEAD // 2, 1) * sine).astype(BF)


def pair_kernel(attn_ref, cos_ref, sin_ref, kv_ref):
    cosine, sine = cos_ref[...], sin_ref[...]
    for h in range(HEADS_DEV):
        lanes = slice(h * HEAD, (h + 1) * HEAD)
        kv_ref[h, :TOK, :] = rotated(attn_ref[1, :, lanes], cosine, sine)
        kv_ref[h, TOK:, :] = attn_ref[2, :, lanes]


def query_kernel(attn_ref, cos_ref, sin_ref, q_ref):
    cosine, sine = cos_ref[...], sin_ref[...]
    for h in range(HEADS_DEV):
        turned = rotated(attn_ref[0, :, h * HEAD : (h + 1) * HEAD], cosine, sine)
        for v in range(4):
            q_ref[member(h, v)] = turned


def state_kernel(feat_ref, rim_ref, weight_ref, rates_ref, state_ref, gate_ref, prod_ref):
    groups = []
    for g in range(3):
        x = jnp.concatenate([rim_ref[g], feat_ref[g].astype(F32)], 0)
        total = weight_ref[0, g : g + 1, :] * x[8 : 8 + TOK]
        for o in range(1, FEAT):
            total = total + weight_ref[o, g : g + 1, :] * x[8 - o : 8 - o + TOK]
        groups.append(total)
    gate_ref[...] = groups[0]
    product = (groups[1] * groups[2]).astype(BF).astype(F32)
    prod_ref[...] = product
    back = (7 - lax.broadcasted_iota(jnp.int32, (8, 128), 0)).astype(F32)
    for part in range(CH // 128):
        lanes = slice(part * 128, (part + 1) * 128)
        step = jnp.exp(-8.0 * rates_ref[:, lanes])
        rows = []
        for n in range(MODES):
            total = product[:8, lanes]
            for a in range(1, 8):
                total = total * step[n : n + 1, :] + product[8 * a : 8 * a + 8, lanes]
            total = total * jnp.exp(-rates_ref[n : n + 1, lanes] * back)
            rows.append(jnp.sum(total, 0, keepdims=True))
        state_ref[part] = jnp.concatenate(rows, 0).astype(BF)


def join_kernel(pair_ref, state_ref, far_pair_ref, far_state_ref, out_ref):
    for peer in range(8):
        head = peer % 4
        out_ref[peer, : 2 * TOK, :] = pair_ref[head]
        out_ref[peer, 2 * TOK : PACK, :] = state_ref[head]
        out_ref[peer, PACK : PACK + 2 * TOK, :] = far_pair_ref[head]
        out_ref[peer, PACK + 2 * TOK :, :] = far_state_ref[head]


def near_kernel(prod_ref, coeff_ref, rates_ref, skip_ref, out_ref, padded, impulse):
    padded[:TOK, :] = jnp.zeros((TOK, CH), F32)
    padded[TOK:, :] = prod_ref[...]
    for part in range(CH // 128):
        lanes = slice(part * 128, (part + 1) * 128)
        rows = expand(rates_ref[:, lanes], coeff_ref[:, lanes], 0)
        for a in range(8):
            impulse[8 * a : 8 * a + 8, lanes] = rows[a]
        y = skip_ref[:1, lanes] * prod_ref[:, lanes]
        for t in range(TOK):
            y = y + impulse[t : t + 1, lanes] * padded[TOK - t : 2 * TOK - t, lanes]
        out_ref[:, lanes] = y


def write_messages(index, got_ref, rates_ref, out_ref):
    y, s, r, v, u = digits(index)
    decay = rates_ref[2 * r + u] * (-float(TOK))

    def faded(steps):
        return jnp.exp(decay * jnp.maximum(steps, 0).astype(F32))

    def when(condition):
        return jnp.where(condition, 1.0, 0.0).astype(F32)

    second = when(y == 1)
    own_states = [got_ref[i, 2 * TOK : PACK, :].astype(F32) for i in range(8)]
    other_states = [got_ref[i, PACK + 2 * TOK :, :].astype(F32) * second for i in range(8)]
    reach, close = {}, {}
    for vt in range(4):
        for du in (-1, 0, 1):
            steps = 2 * (vt - v) + du - 1
            reach[vt, du] = faded(steps + 8)
            close[vt, du] = faded(steps) * when(steps >= 0)
    for rt in range(2):
        before = [jnp.zeros((MODES, 128), F32) for _ in range(2)]
        level = [jnp.zeros((MODES, 128), F32) for _ in range(2)]
        for pair in range(4):
            gap = 16 * (s - pair // 2) + 8 * (rt - pair % 2)
            earlier = faded(gap - 8) * when(gap > 0)
            across = faded(gap + 24)
            for us in range(2):
                i = pair * 2 + us
                before[us] = before[us] + earlier * own_states[i] + across * other_states[i]
                level[us] = level[us] + when(gap == 0) * own_states[i]
        for vt in range(4):
            for ut in range(2):
                state = jnp.zeros((MODES, 128), F32)
                for us in range(2):
                    state = state + reach[vt, ut - us] * before[us] + close[vt, ut - us] * level[us]
                out_ref[rt * 8 + vt * 2 + ut, 80:96, :] = state.astype(BF)


def norm_kernel(square_ref, gained_ref, out_ref):
    total = jnp.sum(square_ref[...], 0, keepdims=True)
    total = jnp.transpose(jnp.broadcast_to(total, (128, 128)))[:TOK, :]
    factor = lax.rsqrt(total * (1.0 / DH) + 1e-06)
    for part in range(CH // 128):
        lanes = slice(part * 128, (part + 1) * 128)
        out_ref[:, lanes] = (gained_ref[:, lanes] * factor).astype(BF)


def attend(keys, values, query, mask):
    scores = lax.dot_general(
        query, keys, (((1,), (1,)), ((), ())), preferred_element_type=F32
    ) * (math.log2(math.e) / math.sqrt(HEAD))
    scores = mask(scores)
    top = jnp.max(scores, 1, keepdims=True)
    weights = jnp.exp2(scores - top)
    total = jnp.sum(weights, 1, keepdims=True)
    mixed = lax.dot_general(
        weights.astype(BF), values, (((1,), (0,)), ((), ())), preferred_element_type=F32
    )
    return top, total, mixed


def attend_kernel(place_ref, q_ref, got_ref, rates_ref, out_ref):
    y, s, _, v, _ = digits(place_ref[0])
    write_messages(place_ref[0], got_ref, rates_ref, out_ref)

    def half(first):
        keys = got_ref[:, first : first + TOK, :].reshape(8 * TOK, HEAD)
        return keys, got_ref[:, first + TOK : first + 2 * TOK, :].reshape(8 * TOK, HEAD)

    own, other = half(0), half(PACK)
    lane = lax.broadcasted_iota(jnp.int32, (1, 8 * TOK), 1)
    block = lane // TOK
    key_pos = ((block // 4) * 16 + ((block // 2) % 2) * 8 + 2 * v + block % 2) * TOK + lane % TOK
    which = lax.broadcasted_iota(jnp.int32, (16, 128), 0)

    def query_of(tile):
        return q_ref[tile * BLOCKS : (tile + 1) * BLOCKS].reshape(WIDE, HEAD)

    def own_part(tile):
        row = lax.broadcasted_iota(jnp.int32, (WIDE, 1), 0) + tile * WIDE
        q_pos = s * (16 * TOK) + row
        return attend(*own, query_of(tile), lambda t: jnp.where(key_pos <= q_pos, t, NEG))

    def write(tile, top, total, mixed):
        mixed = mixed.astype(BF).reshape(BLOCKS, TOK, HEAD)
        out_ref[tile * BLOCKS : (tile + 1) * BLOCKS, :TOK, :] = mixed
        level = jnp.broadcast_to(top + jnp.log2(total), (WIDE, 128))
        for pair in range(WIDE // 128):
            row = jnp.transpose(level[pair * 128 : (pair + 1) * 128])[:1, :]
            high = row.astype(BF).astype(F32)
            rest = row - high
            middle = rest.astype(BF).astype(F32)
            last = rest - middle
            stats = jnp.where(
                which == 0,
                high,
                jnp.where(which == 1, middle, jnp.where(which == 2, last, 0.0)),
            ).astype(BF)
            for b in range(2):
                out_ref[tile * BLOCKS + 2 * pair + b, TOK:80, :] = stats

    @pl.when(y == 0)
    def _():
        for tile in range(16 * TOK // WIDE):
            top, total, mixed = own_part(tile)
            write(tile, top, total, mixed * (1.0 / total))

    @pl.when(y == 1)
    def _():
        for tile in range(16 * TOK // WIDE):
            top_a, total_a, mixed_a = own_part(tile)
            top_b, total_b, mixed_b = attend(*other, query_of(tile), lambda t: t)
            top = jnp.maximum(top_a, top_b)
            scale_a, scale_b = jnp.exp2(top_a - top), jnp.exp2(top_b - top)
            total = total_a * scale_a + total_b * scale_b
            inverse = 1.0 / total
            write(tile, top, total, mixed_a * (scale_a * inverse) + mixed_b * (scale_b * inverse))


def merge(index, got_ref, out_ref):
    odd = index % 2
    levels = jnp.sum(got_ref[:, TOK:80, :].astype(F32), 1)
    levels = jnp.where(odd == 1, pltpu.roll(levels, TOK, 1), levels)
    weights = []
    for h in range(HEADS_DEV):
        part = jnp.concatenate([levels[member(h, k) : member(h, k) + 1] for k in range(4)], 0)
        part = jnp.exp2(part - jnp.max(part, 0, keepdims=True))
        weights.append(part / jnp.sum(part, 0, keepdims=True))
    weights = jnp.concatenate(weights + [jnp.zeros((112, 128), F32)], 0)
    weights = jnp.transpose(weights)[:TOK, :]
    for h in range(HEADS_DEV):
        total = jnp.zeros((TOK, HEAD), F32)
        for k in range(4):
            place = h * 4 + k
            got = got_ref[member(h, k), :TOK, :].astype(F32)
            total = total + weights[:, place : place + 1] * got
        out_ref[:, h * HEAD : (h + 1) * HEAD] = total.astype(BF)


def tail_kernel(
    place_ref, got_ref, coeff_ref, rates_ref, near_ref, gate_ref, gain_ref, gained_ref, square_ref, out_ref
):
    squares = jnp.zeros((TOK, 128), F32)
    for part in range(CH // 128):
        lanes = slice(part * 128, (part + 1) * 128)
        state = got_ref[member(part, 0), 80:96, :].astype(F32)
        for v in range(1, 4):
            state = state + got_ref[member(part, v), 80:96, :].astype(F32)
        tiles = expand(rates_ref[:, lanes], coeff_ref[:, lanes] * state, 1)
        gated = gate_ref[:, lanes] * (near_ref[:, lanes] + jnp.concatenate(tiles, 0))
        gained_ref[:, lanes] = gated * gain_ref[:, lanes]
        squares = squares + gated * gated
    total = jnp.broadcast_to(jnp.sum(squares, 1, keepdims=True), (TOK, 128))
    total = jnp.concatenate([total, jnp.zeros((TOK, 128), F32)], 0)
    square_ref[...] = jnp.transpose(total)[:8, :]
    merge(place_ref[0], got_ref, out_ref)


def exchange(value, groups):
    return lax.all_to_all(value, "context", 0, 0, axis_index_groups=groups, tiled=True)


def local(features, feat_weight, skip, residues, rates, norm_gain, attn_in):
    index = lax.axis_index("context")
    devices = lax.axis_size("context")
    place = index.astype(jnp.int32)[None]
    features = jnp.transpose(features, (1, 0, 2))
    attn_in = jnp.transpose(attn_in, (1, 0, 2))
    rim = lax.ppermute(
        features[:, TOK - (FEAT - 1) :], "context", [(s, s + 1) for s in range(devices - 1)]
    )

    coeff = residues * jnp.sqrt(-jnp.expm1(-2.0 * rates))
    inverse = jnp.exp(
        jnp.arange(HEAD // 2, dtype=F32) * (-2.0 * math.log(ROPE_BASE) / HEAD)
    )
    positions = (index * TOK + jnp.arange(TOK)).astype(F32)
    angle = positions[:, None] * inverse[None, :]
    cosine, sine = jnp.cos(angle), jnp.sin(angle)
    cosine = jnp.concatenate([cosine, cosine], 1)
    sine = jnp.concatenate([-sine, sine], 1)

    (pairs,) = call(
        pair_kernel, [((HEADS_DEV, 2 * TOK, HEAD), BF)], [VMEM] * 3, 1000000000
    )(attn_in, cosine, sine)
    pairs, cosine = lax.optimization_barrier((pairs, cosine))
    (queries,) = call(
        query_kernel, [((16, TOK, HEAD), BF)], [VMEM] * 3, 20000000000
    )(attn_in, cosine, sine)
    over_y = [(s, s + devices // 2) for s in range(devices // 2)]
    far_pairs = lax.ppermute(pairs, "context", over_y)
    queries = exchange(queries, Q_GROUPS)

    rim = jnp.pad(rim.astype(F32), ((0, 0), (6, 0), (0, 0)))
    states, gate, product = call(
        state_kernel,
        [((HEADS_DEV, MODES, HEAD), BF), ((TOK, CH), F32), ((TOK, CH), F32)],
        [VMEM] * 4,
        1000000,
    )(features, rim, jnp.pad(feat_weight, ((0, 0), (0, 5), (0, 0))), rates)
    far_states = lax.ppermute(states, "context", over_y)
    (near,) = call(
        near_kernel,
        [((TOK, CH), F32)],
        [VMEM] * 4,
        1000000,
        [pltpu.VMEM((2 * TOK, CH), F32), pltpu.VMEM((TOK, CH), F32)],
    )(product, coeff, rates, jnp.pad(skip[None, :], ((0, 7), (0, 0))))
    quarters = jnp.transpose(rates.reshape(MODES, CH // 128, 128), (1, 0, 2))
    (both,) = call(join_kernel, [((8, 2 * PACK, HEAD), BF)], [VMEM] * 4, 50000000000)(
        pairs, states, far_pairs, far_states
    )
    queries, both, coeff, quarters, near, gain = lax.optimization_barrier(
        (queries, both, coeff, quarters, near, norm_gain[None, :])
    )
    got = exchange(both, KV_GROUPS)
    (partial,) = call(
        attend_kernel,
        [((16, TOK + 32, HEAD), BF)],
        [SMEM] + [VMEM] * 3,
        4000000000,
    )(place, queries, got, quarters)
    partial = exchange(partial, Q_GROUPS)

    gained, squares, attn_out = call(
        tail_kernel,
        [((TOK, CH), F32), ((8, 128), F32), ((TOK, CH), BF)],
        [SMEM] + [VMEM] * 6,
        1000000000,
    )(place, partial, coeff, rates, near, gate, gain)
    squares = lax.all_to_all(squares, "dp", 0, 0, tiled=True)
    (hyena_out,) = call(norm_kernel, [((TOK, CH), BF)], [VMEM] * 2, 100000000)(squares, gained)
    return (hyena_out, attn_out)


def solution(mesh):
    return jax.shard_map(
        local,
        mesh=mesh,
        in_specs=(
            P("context", None, "dp"),
            P(None, None, "dp"),
            P("dp"),
            P(None, "dp"),
            P(None, "dp"),
            P("dp"),
            P("context", None, "dp"),
        ),
        out_specs=(P("context", "dp"), P("context", "dp")),
        check_vma=False,
    )
```

```python
import functools
import itertools
import math

import jax
import jax.numpy as jnp
from jax import lax
from jax.experimental import pallas as pl
from jax.experimental.pallas import tpu as pltpu
from jax.sharding import PartitionSpec as P

DH = 4096
HEAD = 128
HEADS_DEV = 4
FEAT = 3
MODES = 16
TOK = 64
CH = 512
ROPE_BASE = 1000000.0
NEG = -1e30
PACK = 2 * TOK + MODES
WIDE = 128
BLOCKS = WIDE // TOK
BF = jnp.bfloat16
F32 = jnp.float32

DIGITS = {"y": (2, 32), "s": (2, 16), "r": (2, 8), "v": (4, 2), "u": (2, 1)}


def groups_over(*free):
    fixed = [d for d in DIGITS if d not in free]

    def places(names):
        return [
            sum(v * DIGITS[d][1] for v, d in zip(values, names))
            for values in itertools.product(*[range(DIGITS[d][0]) for d in names])
        ]

    return [[base + step for step in places(free)] for base in places(fixed)]


Q_GROUPS = groups_over("r", "v", "u")
KV_GROUPS = groups_over("s", "r", "u")

VMEM = pl.BlockSpec(memory_space=pltpu.VMEM)
SMEM = pl.BlockSpec(memory_space=pltpu.SMEM)


def call(kernel, outs, specs, flops, scratch=()):
    return pl.pallas_call(
        kernel,
        out_shape=[jax.ShapeDtypeStruct(s, d) for s, d in outs],
        in_specs=specs,
        out_specs=[VMEM] * len(outs),
        scratch_shapes=list(scratch),
        compiler_params=pltpu.CompilerParams(vmem_limit_bytes=16 * 1024 * 1024),
        cost_estimate=pl.CostEstimate(flops=flops, bytes_accessed=1000, transcendentals=0),
    )


def digits(index):
    return [(index // step) % size for size, step in DIGITS.values()]


def member(head, v):
    return (head // 2) * 8 + v * 2 + head % 2


def expand(rates, weights, start):
    ahead = (lax.broadcasted_iota(jnp.int32, (8, 128), 0) + start).astype(F32)
    bases = [jnp.exp(-rates[n : n + 1, :] * ahead) for n in range(MODES)]
    tiles = []
    for a in range(8):
        scaled = weights * jnp.exp(rates * (-8.0 * a))
        tiles.append(sum(bases[n] * scaled[n : n + 1, :] for n in range(MODES)))
    return tiles


def rotate_kernel(attn_ref, cos_ref, sin_ref, q_ref, kv_ref):
    cosine, sine = cos_ref[...], sin_ref[...]
    for g in range(2):
        x = attn_ref[g].astype(F32)
        for h in range(HEADS_DEV):
            part = x[:, h * HEAD : (h + 1) * HEAD]
            turned = (part * cosine + pltpu.roll(part, HEAD // 2, 1) * sine).astype(BF)
            if g == 0:
                for v in range(4):
                    q_ref[member(h, v)] = turned
            else:
                kv_ref[h, :TOK, :] = turned
    for h in range(HEADS_DEV):
        kv_ref[h, TOK:, :] = attn_ref[2, :, h * HEAD : (h + 1) * HEAD]


def state_kernel(feat_ref, rim_ref, weight_ref, rates_ref, state_ref, gate_ref, prod_ref):
    groups = []
    for g in range(3):
        x = jnp.concatenate([rim_ref[g], feat_ref[g].astype(F32)], 0)
        total = weight_ref[0, g : g + 1, :] * x[8 : 8 + TOK]
        for o in range(1, FEAT):
            total = total + weight_ref[o, g : g + 1, :] * x[8 - o : 8 - o + TOK]
        groups.append(total)
    gate_ref[...] = groups[0]
    product = (groups[1] * groups[2]).astype(BF).astype(F32)
    prod_ref[...] = product
    back = (7 - lax.broadcasted_iota(jnp.int32, (8, 128), 0)).astype(F32)
    for part in range(CH // 128):
        lanes = slice(part * 128, (part + 1) * 128)
        step = jnp.exp(-8.0 * rates_ref[:, lanes])
        rows = []
        for n in range(MODES):
            total = product[:8, lanes]
            for a in range(1, 8):
                total = total * step[n : n + 1, :] + product[8 * a : 8 * a + 8, lanes]
            total = total * jnp.exp(-rates_ref[n : n + 1, lanes] * back)
            rows.append(jnp.sum(total, 0, keepdims=True))
        state_ref[part] = jnp.concatenate(rows, 0).astype(BF)


def join_kernel(pair_ref, state_ref, far_pair_ref, far_state_ref, out_ref):
    for peer in range(8):
        head = peer % 4
        out_ref[peer, : 2 * TOK, :] = pair_ref[head]
        out_ref[peer, 2 * TOK : PACK, :] = state_ref[head]
        out_ref[peer, PACK : PACK + 2 * TOK, :] = far_pair_ref[head]
        out_ref[peer, PACK + 2 * TOK :, :] = far_state_ref[head]


def near_kernel(prod_ref, coeff_ref, rates_ref, skip_ref, out_ref, padded, impulse):
    padded[:TOK, :] = jnp.zeros((TOK, CH), F32)
    padded[TOK:, :] = prod_ref[...]
    for part in range(CH // 128):
        lanes = slice(part * 128, (part + 1) * 128)
        rows = expand(rates_ref[:, lanes], coeff_ref[:, lanes], 0)
        for a in range(8):
            impulse[8 * a : 8 * a + 8, lanes] = rows[a]
        y = skip_ref[:1, lanes] * prod_ref[:, lanes]
        for t in range(TOK):
            y = y + impulse[t : t + 1, lanes] * padded[TOK - t : 2 * TOK - t, lanes]
        out_ref[:, lanes] = y


def write_messages(index, got_ref, rates_ref, out_ref):
    y, s, r, v, u = digits(index)
    decay = rates_ref[2 * r + u] * (-float(TOK))

    def faded(steps):
        return jnp.exp(decay * jnp.maximum(steps, 0).astype(F32))

    def when(condition):
        return jnp.where(condition, 1.0, 0.0).astype(F32)

    second = when(y == 1)
    own_states = [got_ref[i, 2 * TOK : PACK, :].astype(F32) for i in range(8)]
    other_states = [got_ref[i, PACK + 2 * TOK :, :].astype(F32) * second for i in range(8)]
    reach, close = {}, {}
    for vt in range(4):
        for du in (-1, 0, 1):
            steps = 2 * (vt - v) + du - 1
            reach[vt, du] = faded(steps + 8)
            close[vt, du] = faded(steps) * when(steps >= 0)
    for rt in range(2):
        before = [jnp.zeros((MODES, 128), F32) for _ in range(2)]
        level = [jnp.zeros((MODES, 128), F32) for _ in range(2)]
        for pair in range(4):
            gap = 16 * (s - pair // 2) + 8 * (rt - pair % 2)
            earlier = faded(gap - 8) * when(gap > 0)
            across = faded(gap + 24)
            for us in range(2):
                i = pair * 2 + us
                before[us] = before[us] + earlier * own_states[i] + across * other_states[i]
                level[us] = level[us] + when(gap == 0) * own_states[i]
        for vt in range(4):
            for ut in range(2):
                state = jnp.zeros((MODES, 128), F32)
                for us in range(2):
                    state = state + reach[vt, ut - us] * before[us] + close[vt, ut - us] * level[us]
                out_ref[rt * 8 + vt * 2 + ut, 80:96, :] = state.astype(BF)


def norm_kernel(square_ref, gained_ref, out_ref):
    total = jnp.sum(square_ref[...], 0, keepdims=True)
    total = jnp.transpose(jnp.broadcast_to(total, (128, 128)))[:TOK, :]
    factor = lax.rsqrt(total * (1.0 / DH) + 1e-06)
    for part in range(CH // 128):
        lanes = slice(part * 128, (part + 1) * 128)
        out_ref[:, lanes] = (gained_ref[:, lanes] * factor).astype(BF)


def attend(keys, values, query, mask):
    scores = lax.dot_general(
        query, keys, (((1,), (1,)), ((), ())), preferred_element_type=F32
    ) * (math.log2(math.e) / math.sqrt(HEAD))
    scores = mask(scores)
    top = jnp.max(scores, 1, keepdims=True)
    weights = jnp.exp2(scores - top)
    mixed = lax.dot_general(
        weights.astype(BF), values, (((1,), (0,)), ((), ())), preferred_element_type=F32
    )
    return top, mixed[:, HEAD:], mixed[:, :HEAD]


def attend_kernel(place_ref, q_ref, got_ref, rates_ref, out_ref):
    y, s, _, v, _ = digits(place_ref[0])
    write_messages(place_ref[0], got_ref, rates_ref, out_ref)

    def half(first):
        keys = got_ref[:, first : first + TOK, :].reshape(8 * TOK, HEAD)
        values = got_ref[:, first + TOK : first + 2 * TOK, :].reshape(8 * TOK, HEAD)
        return keys, jnp.concatenate([values, jnp.ones((8 * TOK, HEAD), BF)], 1)

    own, other = half(0), half(PACK)
    lane = lax.broadcasted_iota(jnp.int32, (1, 8 * TOK), 1)
    block = lane // TOK
    key_pos = ((block // 4) * 16 + ((block // 2) % 2) * 8 + 2 * v + block % 2) * TOK + lane % TOK
    which = lax.broadcasted_iota(jnp.int32, (16, 128), 0)

    def query_of(tile):
        return q_ref[tile * BLOCKS : (tile + 1) * BLOCKS].reshape(WIDE, HEAD)

    def own_part(tile):
        row = lax.broadcasted_iota(jnp.int32, (WIDE, 1), 0) + tile * WIDE
        q_pos = s * (16 * TOK) + row
        return attend(*own, query_of(tile), lambda t: jnp.where(key_pos <= q_pos, t, NEG))

    def write(tile, top, total, mixed):
        mixed = mixed.astype(BF).reshape(BLOCKS, TOK, HEAD)
        out_ref[tile * BLOCKS : (tile + 1) * BLOCKS, :TOK, :] = mixed
        level = jnp.broadcast_to(top + jnp.log2(total), (WIDE, 128))
        for pair in range(WIDE // 128):
            row = jnp.transpose(level[pair * 128 : (pair + 1) * 128])[:1, :]
            high = row.astype(BF).astype(F32)
            rest = row - high
            middle = rest.astype(BF).astype(F32)
            last = rest - middle
            stats = jnp.where(
                which == 0,
                high,
                jnp.where(which == 1, middle, jnp.where(which == 2, last, 0.0)),
            ).astype(BF)
            for b in range(2):
                out_ref[tile * BLOCKS + 2 * pair + b, TOK:80, :] = stats

    @pl.when(y == 0)
    def _():
        for tile in range(16 * TOK // WIDE):
            top, total, mixed = own_part(tile)
            write(tile, top, total, mixed * (1.0 / total))

    @pl.when(y == 1)
    def _():
        for tile in range(16 * TOK // WIDE):
            top_a, total_a, mixed_a = own_part(tile)
            top_b, total_b, mixed_b = attend(*other, query_of(tile), lambda t: t)
            top = jnp.maximum(top_a, top_b)
            scale_a, scale_b = jnp.exp2(top_a - top), jnp.exp2(top_b - top)
            total = total_a * scale_a + total_b * scale_b
            inverse = 1.0 / total
            write(tile, top, total, mixed_a * (scale_a * inverse) + mixed_b * (scale_b * inverse))


def merge(index, got_ref, out_ref):
    odd = index % 2
    levels = jnp.sum(got_ref[:, TOK:80, :].astype(F32), 1)
    levels = jnp.where(odd == 1, pltpu.roll(levels, TOK, 1), levels)
    weights = []
    for h in range(HEADS_DEV):
        part = jnp.concatenate([levels[member(h, k) : member(h, k) + 1] for k in range(4)], 0)
        part = jnp.exp2(part - jnp.max(part, 0, keepdims=True))
        weights.append(part / jnp.sum(part, 0, keepdims=True))
    weights = jnp.concatenate(weights + [jnp.zeros((112, 128), F32)], 0)
    weights = jnp.transpose(weights)[:TOK, :]
    for h in range(HEADS_DEV):
        total = jnp.zeros((TOK, HEAD), F32)
        for k in range(4):
            place = h * 4 + k
            got = got_ref[member(h, k), :TOK, :].astype(F32)
            total = total + weights[:, place : place + 1] * got
        out_ref[:, h * HEAD : (h + 1) * HEAD] = total.astype(BF)


def tail_kernel(
    place_ref, got_ref, coeff_ref, rates_ref, near_ref, gate_ref, gain_ref, gained_ref, square_ref, out_ref
):
    squares = jnp.zeros((TOK, 128), F32)
    for part in range(CH // 128):
        lanes = slice(part * 128, (part + 1) * 128)
        state = got_ref[member(part, 0), 80:96, :].astype(F32)
        for v in range(1, 4):
            state = state + got_ref[member(part, v), 80:96, :].astype(F32)
        tiles = expand(rates_ref[:, lanes], coeff_ref[:, lanes] * state, 1)
        gated = gate_ref[:, lanes] * (near_ref[:, lanes] + jnp.concatenate(tiles, 0))
        gained_ref[:, lanes] = gated * gain_ref[:, lanes]
        squares = squares + gated * gated
    total = jnp.broadcast_to(jnp.sum(squares, 1, keepdims=True), (TOK, 128))
    total = jnp.concatenate([total, jnp.zeros((TOK, 128), F32)], 0)
    square_ref[...] = jnp.transpose(total)[:8, :]
    merge(place_ref[0], got_ref, out_ref)


def exchange(value, groups):
    return lax.all_to_all(value, "context", 0, 0, axis_index_groups=groups, tiled=True)


def local(features, feat_weight, skip, residues, rates, norm_gain, attn_in):
    index = lax.axis_index("context")
    devices = lax.axis_size("context")
    place = index.astype(jnp.int32)[None]
    features = jnp.transpose(features, (1, 0, 2))
    attn_in = jnp.transpose(attn_in, (1, 0, 2))
    rim = lax.ppermute(
        features[:, TOK - (FEAT - 1) :], "context", [(s, s + 1) for s in range(devices - 1)]
    )

    coeff = residues * jnp.sqrt(-jnp.expm1(-2.0 * rates))
    inverse = jnp.exp(
        jnp.arange(HEAD // 2, dtype=F32) * (-2.0 * math.log(ROPE_BASE) / HEAD)
    )
    positions = (index * TOK + jnp.arange(TOK)).astype(F32)
    angle = positions[:, None] * inverse[None, :]
    cosine, sine = jnp.cos(angle), jnp.sin(angle)
    cosine = jnp.concatenate([cosine, cosine], 1)
    sine = jnp.concatenate([-sine, sine], 1)

    queries, pairs = call(
        rotate_kernel,
        [((16, TOK, HEAD), BF), ((HEADS_DEV, 2 * TOK, HEAD), BF)],
        [VMEM] * 3,
        1000000000,
    )(attn_in, cosine, sine)
    over_y = [(s, s + devices // 2) for s in range(devices // 2)]
    far_pairs = lax.ppermute(pairs, "context", over_y)
    queries = exchange(queries, Q_GROUPS)

    rim = jnp.pad(rim.astype(F32), ((0, 0), (6, 0), (0, 0)))
    states, gate, product = call(
        state_kernel,
        [((HEADS_DEV, MODES, HEAD), BF), ((TOK, CH), F32), ((TOK, CH), F32)],
        [VMEM] * 4,
        1000000,
    )(features, rim, jnp.pad(feat_weight, ((0, 0), (0, 5), (0, 0))), rates)
    far_states = lax.ppermute(states, "context", over_y)
    (near,) = call(
        near_kernel,
        [((TOK, CH), F32)],
        [VMEM] * 4,
        1000000,
        [pltpu.VMEM((2 * TOK, CH), F32), pltpu.VMEM((TOK, CH), F32)],
    )(product, coeff, rates, jnp.pad(skip[None, :], ((0, 7), (0, 0))))
    quarters = jnp.transpose(rates.reshape(MODES, CH // 128, 128), (1, 0, 2))
    (both,) = call(join_kernel, [((8, 2 * PACK, HEAD), BF)], [VMEM] * 4, 50000000000)(
        pairs, states, far_pairs, far_states
    )
    queries, both, coeff, quarters, near, gain = lax.optimization_barrier(
        (queries, both, coeff, quarters, near, norm_gain[None, :])
    )
    got = exchange(both, KV_GROUPS)
    (partial,) = call(
        attend_kernel,
        [((16, TOK + 32, HEAD), BF)],
        [SMEM] + [VMEM] * 3,
        4000000000,
    )(place, queries, got, quarters)
    partial = exchange(partial, Q_GROUPS)

    gained, squares, attn_out = call(
        tail_kernel,
        [((TOK, CH), F32), ((8, 128), F32), ((TOK, CH), BF)],
        [SMEM] + [VMEM] * 6,
        1000000000,
    )(place, partial, coeff, rates, near, gate, gain)
    squares = lax.all_to_all(squares, "dp", 0, 0, tiled=True)
    (hyena_out,) = call(norm_kernel, [((TOK, CH), BF)], [VMEM] * 2, 100000000)(squares, gained)
    return (hyena_out, attn_out)


def solution(mesh):
    return jax.shard_map(
        local,
        mesh=mesh,
        in_specs=(
            P("context", None, "dp"),
            P(None, None, "dp"),
            P("dp"),
            P(None, "dp"),
            P(None, "dp"),
            P("dp"),
            P("context", None, "dp"),
        ),
        out_specs=(P("context", "dp"), P("context", "dp")),
        check_vma=False,
    )
```

```python
import functools
import itertools
import math

import jax
import jax.numpy as jnp
from jax import lax
from jax.experimental import pallas as pl
from jax.experimental.pallas import tpu as pltpu
from jax.sharding import PartitionSpec as P

DH = 4096
HEAD = 128
HEADS_DEV = 4
FEAT = 3
MODES = 16
TOK = 64
CH = 512
ROPE_BASE = 1000000.0
NEG = -1e30
PACK = 2 * TOK + MODES
WIDE = 128
BLOCKS = WIDE // TOK
BF = jnp.bfloat16
F32 = jnp.float32

DIGITS = {"y": (2, 32), "s": (2, 16), "r": (2, 8), "v": (4, 2), "u": (2, 1)}


def groups_over(*free):
    fixed = [d for d in DIGITS if d not in free]

    def places(names):
        return [
            sum(v * DIGITS[d][1] for v, d in zip(values, names))
            for values in itertools.product(*[range(DIGITS[d][0]) for d in names])
        ]

    return [[base + step for step in places(free)] for base in places(fixed)]


Q_GROUPS = groups_over("r", "v", "u")
KV_GROUPS = groups_over("s", "r", "u")

VMEM = pl.BlockSpec(memory_space=pltpu.VMEM)
SMEM = pl.BlockSpec(memory_space=pltpu.SMEM)


def call(kernel, outs, specs, flops, scratch=()):
    return pl.pallas_call(
        kernel,
        out_shape=[jax.ShapeDtypeStruct(s, d) for s, d in outs],
        in_specs=specs,
        out_specs=[VMEM] * len(outs),
        scratch_shapes=list(scratch),
        compiler_params=pltpu.CompilerParams(vmem_limit_bytes=16 * 1024 * 1024),
        cost_estimate=pl.CostEstimate(flops=flops, bytes_accessed=1000, transcendentals=0),
    )


def digits(index):
    return [(index // step) % size for size, step in DIGITS.values()]


def member(head, v):
    return (head // 2) * 8 + v * 2 + head % 2


def expand(rates, weights, start):
    ahead = (lax.broadcasted_iota(jnp.int32, (8, 128), 0) + start).astype(F32)
    bases = [jnp.exp(-rates[n : n + 1, :] * ahead) for n in range(MODES)]
    tiles = []
    for a in range(8):
        scaled = weights * jnp.exp(rates * (-8.0 * a))
        tiles.append(sum(bases[n] * scaled[n : n + 1, :] for n in range(MODES)))
    return tiles


def rotate_kernel(attn_ref, cos_ref, sin_ref, q_ref, kv_ref):
    cosine, sine = cos_ref[...], sin_ref[...]
    for g in range(2):
        x = attn_ref[g].astype(F32)
        for h in range(HEADS_DEV):
            part = x[:, h * HEAD : (h + 1) * HEAD]
            turned = (part * cosine + pltpu.roll(part, HEAD // 2, 1) * sine).astype(BF)
            if g == 0:
                for v in range(4):
                    q_ref[member(h, v)] = turned
            else:
                kv_ref[h, :TOK, :] = turned
    for h in range(HEADS_DEV):
        kv_ref[h, TOK:, :] = attn_ref[2, :, h * HEAD : (h + 1) * HEAD]


def state_kernel(feat_ref, rim_ref, weight_ref, rates_ref, state_ref, gate_ref, prod_ref):
    groups = []
    for g in range(3):
        x = jnp.concatenate([rim_ref[g].astype(F32)[8:], feat_ref[g].astype(F32)], 0)
        total = weight_ref[0, g : g + 1, :] * x[8 : 8 + TOK]
        for o in range(1, FEAT):
            total = total + weight_ref[o, g : g + 1, :] * x[8 - o : 8 - o + TOK]
        groups.append(total)
    gate_ref[...] = groups[0]
    product = (groups[1] * groups[2]).astype(BF).astype(F32)
    prod_ref[...] = product
    back = (7 - lax.broadcasted_iota(jnp.int32, (8, 128), 0)).astype(F32)
    for part in range(CH // 128):
        lanes = slice(part * 128, (part + 1) * 128)
        step = jnp.exp(-8.0 * rates_ref[:, lanes])
        rows = []
        for n in range(MODES):
            total = product[:8, lanes]
            for a in range(1, 8):
                total = total * step[n : n + 1, :] + product[8 * a : 8 * a + 8, lanes]
            total = total * jnp.exp(-rates_ref[n : n + 1, lanes] * back)
            rows.append(jnp.sum(total, 0, keepdims=True))
        state_ref[part] = jnp.concatenate(rows, 0).astype(BF)


def join_kernel(pair_ref, state_ref, far_pair_ref, far_state_ref, out_ref):
    for peer in range(8):
        head = peer % 4
        out_ref[peer, : 2 * TOK, :] = pair_ref[head]
        out_ref[peer, 2 * TOK : PACK, :] = state_ref[head]
        out_ref[peer, PACK : PACK + 2 * TOK, :] = far_pair_ref[head]
        out_ref[peer, PACK + 2 * TOK :, :] = far_state_ref[head]


def near_kernel(prod_ref, coeff_ref, rates_ref, skip_ref, out_ref, padded, impulse):
    padded[:TOK, :] = jnp.zeros((TOK, CH), F32)
    padded[TOK:, :] = prod_ref[...]
    for part in range(CH // 128):
        lanes = slice(part * 128, (part + 1) * 128)
        rows = expand(rates_ref[:, lanes], coeff_ref[:, lanes], 0)
        for a in range(8):
            impulse[8 * a : 8 * a + 8, lanes] = rows[a]
        y = skip_ref[:1, lanes] * prod_ref[:, lanes]
        for t in range(TOK):
            y = y + impulse[t : t + 1, lanes] * padded[TOK - t : 2 * TOK - t, lanes]
        out_ref[:, lanes] = y


def write_messages(index, got_ref, rates_ref, out_ref):
    y, s, r, v, u = digits(index)
    decay = rates_ref[2 * r + u] * (-float(TOK))

    def faded(steps):
        return jnp.exp(decay * jnp.maximum(steps, 0).astype(F32))

    def when(condition):
        return jnp.where(condition, 1.0, 0.0).astype(F32)

    second = when(y == 1)
    own_states = [got_ref[i, 2 * TOK : PACK, :].astype(F32) for i in range(8)]
    other_states = [got_ref[i, PACK + 2 * TOK :, :].astype(F32) * second for i in range(8)]
    reach, close = {}, {}
    for vt in range(4):
        for du in (-1, 0, 1):
            steps = 2 * (vt - v) + du - 1
            reach[vt, du] = faded(steps + 8)
            close[vt, du] = faded(steps) * when(steps >= 0)
    for rt in range(2):
        before = [jnp.zeros((MODES, 128), F32) for _ in range(2)]
        level = [jnp.zeros((MODES, 128), F32) for _ in range(2)]
        for pair in range(4):
            gap = 16 * (s - pair // 2) + 8 * (rt - pair % 2)
            earlier = faded(gap - 8) * when(gap > 0)
            across = faded(gap + 24)
            for us in range(2):
                i = pair * 2 + us
                before[us] = before[us] + earlier * own_states[i] + across * other_states[i]
                level[us] = level[us] + when(gap == 0) * own_states[i]
        for vt in range(4):
            for ut in range(2):
                state = jnp.zeros((MODES, 128), F32)
                for us in range(2):
                    state = state + reach[vt, ut - us] * before[us] + close[vt, ut - us] * level[us]
                out_ref[rt * 8 + vt * 2 + ut, 80:96, :] = state.astype(BF)


def norm_kernel(square_ref, gained_ref, out_ref):
    total = jnp.sum(square_ref[...], 0, keepdims=True)
    total = jnp.transpose(jnp.broadcast_to(total, (128, 128)))[:TOK, :]
    factor = lax.rsqrt(total * (1.0 / DH) + 1e-06)
    for part in range(CH // 128):
        lanes = slice(part * 128, (part + 1) * 128)
        out_ref[:, lanes] = (gained_ref[:, lanes] * factor).astype(BF)


def attend(keys, values, query, mask):
    scores = lax.dot_general(
        query, keys, (((1,), (1,)), ((), ())), preferred_element_type=F32
    ) * (math.log2(math.e) / math.sqrt(HEAD))
    scores = mask(scores)
    top = jnp.max(scores, 1, keepdims=True)
    weights = jnp.exp2(scores - top)
    mixed = lax.dot_general(
        weights.astype(BF), values, (((1,), (0,)), ((), ())), preferred_element_type=F32
    )
    return top, mixed[:, HEAD:], mixed[:, :HEAD]


def attend_kernel(place_ref, q_ref, got_ref, rates_ref, out_ref):
    y, s, _, v, _ = digits(place_ref[0])
    write_messages(place_ref[0], got_ref, rates_ref, out_ref)

    def half(first):
        keys = got_ref[:, first : first + TOK, :].reshape(8 * TOK, HEAD)
        values = got_ref[:, first + TOK : first + 2 * TOK, :].reshape(8 * TOK, HEAD)
        return keys, jnp.concatenate([values, jnp.ones((8 * TOK, HEAD), BF)], 1)

    own, other = half(0), half(PACK)
    lane = lax.broadcasted_iota(jnp.int32, (1, 8 * TOK), 1)
    block = lane // TOK
    key_pos = ((block // 4) * 16 + ((block // 2) % 2) * 8 + 2 * v + block % 2) * TOK + lane % TOK
    which = lax.broadcasted_iota(jnp.int32, (16, 128), 0)

    def query_of(tile):
        return q_ref[tile * BLOCKS : (tile + 1) * BLOCKS].reshape(WIDE, HEAD)

    def own_part(tile):
        row = lax.broadcasted_iota(jnp.int32, (WIDE, 1), 0) + tile * WIDE
        q_pos = s * (16 * TOK) + row
        return attend(*own, query_of(tile), lambda t: jnp.where(key_pos <= q_pos, t, NEG))

    def write(tile, top, total, mixed):
        mixed = mixed.astype(BF).reshape(BLOCKS, TOK, HEAD)
        out_ref[tile * BLOCKS : (tile + 1) * BLOCKS, :TOK, :] = mixed
        level = jnp.broadcast_to(top + jnp.log2(total), (WIDE, 128))
        for pair in range(WIDE // 128):
            row = jnp.transpose(level[pair * 128 : (pair + 1) * 128])[:1, :]
            high = row.astype(BF).astype(F32)
            rest = row - high
            middle = rest.astype(BF).astype(F32)
            last = rest - middle
            stats = jnp.where(
                which == 0,
                high,
                jnp.where(which == 1, middle, jnp.where(which == 2, last, 0.0)),
            ).astype(BF)
            for b in range(2):
                out_ref[tile * BLOCKS + 2 * pair + b, TOK:80, :] = stats

    @pl.when(y == 0)
    def _():
        for tile in range(16 * TOK // WIDE):
            top, total, mixed = own_part(tile)
            write(tile, top, total, mixed * (1.0 / total))

    @pl.when(y == 1)
    def _():
        for tile in range(16 * TOK // WIDE):
            top_a, total_a, mixed_a = own_part(tile)
            top_b, total_b, mixed_b = attend(*other, query_of(tile), lambda t: t)
            top = jnp.maximum(top_a, top_b)
            scale_a, scale_b = jnp.exp2(top_a - top), jnp.exp2(top_b - top)
            total = total_a * scale_a + total_b * scale_b
            inverse = 1.0 / total
            write(tile, top, total, mixed_a * (scale_a * inverse) + mixed_b * (scale_b * inverse))


def merge(index, got_ref, out_ref):
    odd = index % 2
    levels = jnp.sum(got_ref[:, TOK:80, :].astype(F32), 1)
    levels = jnp.where(odd == 1, pltpu.roll(levels, TOK, 1), levels)
    weights = []
    for h in range(HEADS_DEV):
        part = jnp.concatenate([levels[member(h, k) : member(h, k) + 1] for k in range(4)], 0)
        part = jnp.exp2(part - jnp.max(part, 0, keepdims=True))
        weights.append(part / jnp.sum(part, 0, keepdims=True))
    weights = jnp.concatenate(weights + [jnp.zeros((112, 128), F32)], 0)
    weights = jnp.transpose(weights)[:TOK, :]
    for h in range(HEADS_DEV):
        total = jnp.zeros((TOK, HEAD), F32)
        for k in range(4):
            place = h * 4 + k
            got = got_ref[member(h, k), :TOK, :].astype(F32)
            total = total + weights[:, place : place + 1] * got
        out_ref[:, h * HEAD : (h + 1) * HEAD] = total.astype(BF)


def tail_kernel(
    place_ref, got_ref, coeff_ref, rates_ref, near_ref, gate_ref, gain_ref, gained_ref, square_ref, out_ref
):
    squares = jnp.zeros((TOK, 128), F32)
    for part in range(CH // 128):
        lanes = slice(part * 128, (part + 1) * 128)
        state = got_ref[member(part, 0), 80:96, :].astype(F32)
        for v in range(1, 4):
            state = state + got_ref[member(part, v), 80:96, :].astype(F32)
        tiles = expand(rates_ref[:, lanes], coeff_ref[:, lanes] * state, 1)
        gated = gate_ref[:, lanes] * (near_ref[:, lanes] + jnp.concatenate(tiles, 0))
        gained_ref[:, lanes] = gated * gain_ref[:, lanes]
        squares = squares + gated * gated
    total = jnp.broadcast_to(jnp.sum(squares, 1, keepdims=True), (TOK, 128))
    total = jnp.concatenate([total, jnp.zeros((TOK, 128), F32)], 0)
    square_ref[...] = jnp.transpose(total)[:8, :]
    merge(place_ref[0], got_ref, out_ref)


def exchange(value, groups):
    return lax.all_to_all(value, "context", 0, 0, axis_index_groups=groups, tiled=True)


def local(features, feat_weight, skip, residues, rates, norm_gain, attn_in):
    index = lax.axis_index("context")
    devices = lax.axis_size("context")
    place = index.astype(jnp.int32)[None]
    features = jnp.transpose(features, (1, 0, 2))
    attn_in = jnp.transpose(attn_in, (1, 0, 2))
    rim = lax.ppermute(
        features[:, TOK - 16 :], "context", [(s, s + 1) for s in range(devices - 1)]
    )

    coeff = residues * jnp.sqrt(-jnp.expm1(-2.0 * rates))
    inverse = jnp.exp(
        jnp.arange(HEAD // 2, dtype=F32) * (-2.0 * math.log(ROPE_BASE) / HEAD)
    )
    positions = (index * TOK + jnp.arange(TOK)).astype(F32)
    angle = positions[:, None] * inverse[None, :]
    cosine, sine = jnp.cos(angle), jnp.sin(angle)
    cosine = jnp.concatenate([cosine, cosine], 1)
    sine = jnp.concatenate([-sine, sine], 1)

    queries, pairs = call(
        rotate_kernel,
        [((16, TOK, HEAD), BF), ((HEADS_DEV, 2 * TOK, HEAD), BF)],
        [VMEM] * 3,
        1000000000,
    )(attn_in, cosine, sine)
    over_y = [(s, s + devices // 2) for s in range(devices // 2)]
    far_pairs = lax.ppermute(pairs, "context", over_y)
    queries = exchange(queries, Q_GROUPS)

    states, gate, product = call(
        state_kernel,
        [((HEADS_DEV, MODES, HEAD), BF), ((TOK, CH), F32), ((TOK, CH), F32)],
        [VMEM] * 4,
        1000000,
    )(features, rim, jnp.pad(feat_weight, ((0, 0), (0, 5), (0, 0))), rates)
    far_states = lax.ppermute(states, "context", over_y)
    (near,) = call(
        near_kernel,
        [((TOK, CH), F32)],
        [VMEM] * 4,
        1000000,
        [pltpu.VMEM((2 * TOK, CH), F32), pltpu.VMEM((TOK, CH), F32)],
    )(product, coeff, rates, jnp.pad(skip[None, :], ((0, 7), (0, 0))))
    quarters = jnp.transpose(rates.reshape(MODES, CH // 128, 128), (1, 0, 2))
    (both,) = call(join_kernel, [((8, 2 * PACK, HEAD), BF)], [VMEM] * 4, 50000000000)(
        pairs, states, far_pairs, far_states
    )
    queries, both, coeff, quarters, near, gain = lax.optimization_barrier(
        (queries, both, coeff, quarters, near, norm_gain[None, :])
    )
    got = exchange(both, KV_GROUPS)
    (partial,) = call(
        attend_kernel,
        [((16, TOK + 32, HEAD), BF)],
        [SMEM] + [VMEM] * 3,
        4000000000,
    )(place, queries, got, quarters)
    partial = exchange(partial, Q_GROUPS)

    gained, squares, attn_out = call(
        tail_kernel,
        [((TOK, CH), F32), ((8, 128), F32), ((TOK, CH), BF)],
        [SMEM] + [VMEM] * 6,
        1000000000,
    )(place, partial, coeff, rates, near, gate, gain)
    squares = lax.all_to_all(squares, "dp", 0, 0, tiled=True)
    (hyena_out,) = call(norm_kernel, [((TOK, CH), BF)], [VMEM] * 2, 100000000)(squares, gained)
    return (hyena_out, attn_out)


def solution(mesh):
    return jax.shard_map(
        local,
        mesh=mesh,
        in_specs=(
            P("context", None, "dp"),
            P(None, None, "dp"),
            P("dp"),
            P(None, "dp"),
            P(None, "dp"),
            P("dp"),
            P("context", None, "dp"),
        ),
        out_specs=(P("context", "dp"), P("context", "dp")),
        check_vma=False,
    )
```

```python
import functools
import itertools
import math

import jax
import jax.numpy as jnp
import numpy as np
from jax import lax
from jax.experimental import pallas as pl
from jax.experimental.pallas import tpu as pltpu
from jax.sharding import PartitionSpec as P

DH = 4096
HEAD = 128
HEADS_DEV = 4
FEAT = 3
MODES = 16
TOK = 64
CH = 512
ROPE_BASE = 1000000.0
NEG = -1e30
PACK = 2 * TOK + MODES
WIDE = 128
BLOCKS = WIDE // TOK
BF = jnp.bfloat16
F32 = jnp.float32

DIGITS = {"y": (2, 32), "s": (2, 16), "r": (2, 8), "v": (4, 2), "u": (2, 1)}


def groups_over(*free):
    fixed = [d for d in DIGITS if d not in free]

    def places(names):
        return [
            sum(v * DIGITS[d][1] for v, d in zip(values, names))
            for values in itertools.product(*[range(DIGITS[d][0]) for d in names])
        ]

    return [[base + step for step in places(free)] for base in places(fixed)]


Q_GROUPS = groups_over("r", "v", "u")
KV_GROUPS = groups_over("s", "r", "u")

VMEM = pl.BlockSpec(memory_space=pltpu.VMEM)
SMEM = pl.BlockSpec(memory_space=pltpu.SMEM)


def call(kernel, outs, specs, flops, scratch=()):
    return pl.pallas_call(
        kernel,
        out_shape=[jax.ShapeDtypeStruct(s, d) for s, d in outs],
        in_specs=specs,
        out_specs=[VMEM] * len(outs),
        scratch_shapes=list(scratch),
        compiler_params=pltpu.CompilerParams(vmem_limit_bytes=16 * 1024 * 1024),
        cost_estimate=pl.CostEstimate(flops=flops, bytes_accessed=1000, transcendentals=0),
    )


def digits(index):
    return [(index // step) % size for size, step in DIGITS.values()]


def member(head, v):
    return (head // 2) * 8 + v * 2 + head % 2


def expand(rates, weights, start):
    ahead = (lax.broadcasted_iota(jnp.int32, (8, 128), 0) + start).astype(F32)
    bases = [jnp.exp(-rates[n : n + 1, :] * ahead) for n in range(MODES)]
    tiles = []
    for a in range(8):
        scaled = weights * jnp.exp(rates * (-8.0 * a))
        tiles.append(sum(bases[n] * scaled[n : n + 1, :] for n in range(MODES)))
    return tiles


def rotate_kernel(attn_ref, cos_ref, sin_ref, q_ref, kv_ref):
    cosine, sine = cos_ref[...], sin_ref[...]
    for g in range(2):
        x = attn_ref[g].astype(F32)
        for h in range(HEADS_DEV):
            part = x[:, h * HEAD : (h + 1) * HEAD]
            turned = (part * cosine + pltpu.roll(part, HEAD // 2, 1) * sine).astype(BF)
            if g == 0:
                for v in range(4):
                    q_ref[member(h, v)] = turned
            else:
                kv_ref[h, :TOK, :] = turned
    for h in range(HEADS_DEV):
        kv_ref[h, TOK:, :] = attn_ref[2, :, h * HEAD : (h + 1) * HEAD]


def state_kernel(feat_ref, rim_ref, weight_ref, rates_ref, state_ref, gate_ref, prod_ref):
    groups = []
    for g in range(3):
        x = jnp.concatenate([rim_ref[g].astype(F32)[8:], feat_ref[g].astype(F32)], 0)
        total = weight_ref[0, g : g + 1, :] * x[8 : 8 + TOK]
        for o in range(1, FEAT):
            total = total + weight_ref[o, g : g + 1, :] * x[8 - o : 8 - o + TOK]
        groups.append(total)
    gate_ref[...] = groups[0]
    product = (groups[1] * groups[2]).astype(BF).astype(F32)
    prod_ref[...] = product
    back = (7 - lax.broadcasted_iota(jnp.int32, (8, 128), 0)).astype(F32)
    for part in range(CH // 128):
        lanes = slice(part * 128, (part + 1) * 128)
        step = jnp.exp(-8.0 * rates_ref[:, lanes])
        rows = []
        for n in range(MODES):
            total = product[:8, lanes]
            for a in range(1, 8):
                total = total * step[n : n + 1, :] + product[8 * a : 8 * a + 8, lanes]
            total = total * jnp.exp(-rates_ref[n : n + 1, lanes] * back)
            rows.append(jnp.sum(total, 0, keepdims=True))
        state_ref[part] = jnp.concatenate(rows, 0).astype(BF)


def join_kernel(pair_ref, state_ref, far_pair_ref, far_state_ref, out_ref):
    for peer in range(8):
        head = peer % 4
        out_ref[peer, : 2 * TOK, :] = pair_ref[head]
        out_ref[peer, 2 * TOK : PACK, :] = state_ref[head]
        out_ref[peer, PACK : PACK + 2 * TOK, :] = far_pair_ref[head]
        out_ref[peer, PACK + 2 * TOK :, :] = far_state_ref[head]


def near_kernel(prod_ref, coeff_ref, rates_ref, skip_ref, out_ref, padded, impulse):
    padded[:TOK, :] = jnp.zeros((TOK, CH), F32)
    padded[TOK:, :] = prod_ref[...]
    for part in range(CH // 128):
        lanes = slice(part * 128, (part + 1) * 128)
        rows = expand(rates_ref[:, lanes], coeff_ref[:, lanes], 0)
        for a in range(8):
            impulse[8 * a : 8 * a + 8, lanes] = rows[a]
        y = skip_ref[:1, lanes] * prod_ref[:, lanes]
        for t in range(TOK):
            y = y + impulse[t : t + 1, lanes] * padded[TOK - t : 2 * TOK - t, lanes]
        out_ref[:, lanes] = y


def write_messages(index, got_ref, rates_ref, out_ref):
    y, s, r, v, u = digits(index)
    decay = rates_ref[2 * r + u] * (-float(TOK))

    def faded(steps):
        return jnp.exp(decay * jnp.maximum(steps, 0).astype(F32))

    def when(condition):
        return jnp.where(condition, 1.0, 0.0).astype(F32)

    second = when(y == 1)
    own_states = [got_ref[i, 2 * TOK : PACK, :].astype(F32) for i in range(8)]
    other_states = [got_ref[i, PACK + 2 * TOK :, :].astype(F32) * second for i in range(8)]
    reach, close = {}, {}
    for vt in range(4):
        for du in (-1, 0, 1):
            steps = 2 * (vt - v) + du - 1
            reach[vt, du] = faded(steps + 8)
            close[vt, du] = faded(steps) * when(steps >= 0)
    for rt in range(2):
        before = [jnp.zeros((MODES, 128), F32) for _ in range(2)]
        level = [jnp.zeros((MODES, 128), F32) for _ in range(2)]
        for pair in range(4):
            gap = 16 * (s - pair // 2) + 8 * (rt - pair % 2)
            earlier = faded(gap - 8) * when(gap > 0)
            across = faded(gap + 24)
            for us in range(2):
                i = pair * 2 + us
                before[us] = before[us] + earlier * own_states[i] + across * other_states[i]
                level[us] = level[us] + when(gap == 0) * own_states[i]
        for vt in range(4):
            for ut in range(2):
                state = jnp.zeros((MODES, 128), F32)
                for us in range(2):
                    state = state + reach[vt, ut - us] * before[us] + close[vt, ut - us] * level[us]
                out_ref[rt * 8 + vt * 2 + ut, 80:96, :] = state.astype(BF)


def norm_kernel(square_ref, gained_ref, out_ref):
    total = jnp.sum(square_ref[...], 0, keepdims=True)
    total = jnp.transpose(jnp.broadcast_to(total, (128, 128)))[:TOK, :]
    factor = lax.rsqrt(total * (1.0 / DH) + 1e-06)
    for part in range(CH // 128):
        lanes = slice(part * 128, (part + 1) * 128)
        out_ref[:, lanes] = (gained_ref[:, lanes] * factor).astype(BF)


def attend(keys, values, query, mask):
    scores = lax.dot_general(
        query, keys, (((1,), (1,)), ((), ())), preferred_element_type=F32
    ) * (math.log2(math.e) / math.sqrt(HEAD))
    scores = mask(scores)
    top = jnp.max(scores, 1, keepdims=True)
    weights = jnp.exp2(scores - top)
    mixed = lax.dot_general(
        weights.astype(BF), values, (((1,), (0,)), ((), ())), preferred_element_type=F32
    )
    return top, mixed[:, HEAD:], mixed[:, :HEAD]


def attend_kernel(place_ref, q_ref, got_ref, rates_ref, out_ref):
    y, s, _, v, _ = digits(place_ref[0])
    write_messages(place_ref[0], got_ref, rates_ref, out_ref)

    def half(first):
        keys = got_ref[:, first : first + TOK, :].reshape(8 * TOK, HEAD)
        values = got_ref[:, first + TOK : first + 2 * TOK, :].reshape(8 * TOK, HEAD)
        return keys, jnp.concatenate([values, jnp.ones((8 * TOK, HEAD), BF)], 1)

    own, other = half(0), half(PACK)
    lane = lax.broadcasted_iota(jnp.int32, (1, 8 * TOK), 1)
    block = lane // TOK
    key_pos = ((block // 4) * 16 + ((block // 2) % 2) * 8 + 2 * v + block % 2) * TOK + lane % TOK
    which = lax.broadcasted_iota(jnp.int32, (16, 128), 0)

    def query_of(tile):
        return q_ref[tile * BLOCKS : (tile + 1) * BLOCKS].reshape(WIDE, HEAD)

    def own_part(tile):
        row = lax.broadcasted_iota(jnp.int32, (WIDE, 1), 0) + tile * WIDE
        q_pos = s * (16 * TOK) + row
        return attend(*own, query_of(tile), lambda t: jnp.where(key_pos <= q_pos, t, NEG))

    def write(tile, top, total, mixed):
        mixed = mixed.astype(BF).reshape(BLOCKS, TOK, HEAD)
        out_ref[tile * BLOCKS : (tile + 1) * BLOCKS, :TOK, :] = mixed
        level = jnp.broadcast_to(top + jnp.log2(total), (WIDE, 128))
        for pair in range(WIDE // 128):
            row = jnp.transpose(level[pair * 128 : (pair + 1) * 128])[:1, :]
            high = row.astype(BF).astype(F32)
            rest = row - high
            middle = rest.astype(BF).astype(F32)
            last = rest - middle
            stats = jnp.where(
                which == 0,
                high,
                jnp.where(which == 1, middle, jnp.where(which == 2, last, 0.0)),
            ).astype(BF)
            for b in range(2):
                out_ref[tile * BLOCKS + 2 * pair + b, TOK:80, :] = stats

    @pl.when(y == 0)
    def _():
        for tile in range(16 * TOK // WIDE):
            top, total, mixed = own_part(tile)
            write(tile, top, total, mixed * (1.0 / total))

    @pl.when(y == 1)
    def _():
        for tile in range(16 * TOK // WIDE):
            top_a, total_a, mixed_a = own_part(tile)
            top_b, total_b, mixed_b = attend(*other, query_of(tile), lambda t: t)
            top = jnp.maximum(top_a, top_b)
            scale_a, scale_b = jnp.exp2(top_a - top), jnp.exp2(top_b - top)
            total = total_a * scale_a + total_b * scale_b
            inverse = 1.0 / total
            write(tile, top, total, mixed_a * (scale_a * inverse) + mixed_b * (scale_b * inverse))


def merge(index, got_ref, out_ref):
    odd = index % 2
    levels = jnp.sum(got_ref[:, TOK:80, :].astype(F32), 1)
    levels = jnp.where(odd == 1, pltpu.roll(levels, TOK, 1), levels)
    weights = []
    for h in range(HEADS_DEV):
        part = jnp.concatenate([levels[member(h, k) : member(h, k) + 1] for k in range(4)], 0)
        part = jnp.exp2(part - jnp.max(part, 0, keepdims=True))
        weights.append(part / jnp.sum(part, 0, keepdims=True))
    weights = jnp.concatenate(weights + [jnp.zeros((112, 128), F32)], 0)
    weights = jnp.transpose(weights)[:TOK, :]
    for h in range(HEADS_DEV):
        total = jnp.zeros((TOK, HEAD), F32)
        for k in range(4):
            place = h * 4 + k
            got = got_ref[member(h, k), :TOK, :].astype(F32)
            total = total + weights[:, place : place + 1] * got
        out_ref[:, h * HEAD : (h + 1) * HEAD] = total.astype(BF)


def tail_kernel(
    place_ref, got_ref, coeff_ref, rates_ref, near_ref, gate_ref, gain_ref, gained_ref, square_ref, out_ref
):
    squares = jnp.zeros((TOK, 128), F32)
    for part in range(CH // 128):
        lanes = slice(part * 128, (part + 1) * 128)
        state = got_ref[member(part, 0), 80:96, :].astype(F32)
        for v in range(1, 4):
            state = state + got_ref[member(part, v), 80:96, :].astype(F32)
        tiles = expand(rates_ref[:, lanes], coeff_ref[:, lanes] * state, 1)
        gated = gate_ref[:, lanes] * (near_ref[:, lanes] + jnp.concatenate(tiles, 0))
        gained_ref[:, lanes] = gated * gain_ref[:, lanes]
        squares = squares + gated * gated
    total = jnp.broadcast_to(jnp.sum(squares, 1, keepdims=True), (TOK, 128))
    total = jnp.concatenate([total, jnp.zeros((TOK, 128), F32)], 0)
    square_ref[...] = jnp.transpose(total)[:8, :]
    merge(place_ref[0], got_ref, out_ref)


def exchange(value, groups):
    return lax.all_to_all(value, "context", 0, 0, axis_index_groups=groups, tiled=True)


def local(features, feat_weight, skip, residues, rates, norm_gain, attn_in):
    index = lax.axis_index("context")
    devices = lax.axis_size("context")
    place = index.astype(jnp.int32)[None]
    features = jnp.transpose(features, (1, 0, 2))
    attn_in = jnp.transpose(attn_in, (1, 0, 2))
    rim = lax.ppermute(
        features[:, TOK - 16 :], "context", [(s, s + 1) for s in range(devices - 1)]
    )

    coeff = residues * jnp.sqrt(-jnp.expm1(-2.0 * rates))
    steps = np.arange(TOK)[:, None] * ROPE_BASE ** (-2.0 * np.arange(HEAD // 2)[None, :] / HEAD)
    inner_cos, inner_sin = np.cos(steps).astype(np.float32), np.sin(steps).astype(np.float32)
    inverse = jnp.exp(jnp.arange(HEAD // 2, dtype=F32) * (-2.0 * math.log(ROPE_BASE) / HEAD))
    start = (index * TOK).astype(F32) * inverse[None, :]
    start_cos, start_sin = lax.optimization_barrier((jnp.cos(start), jnp.sin(start)))
    cosine = start_cos * inner_cos - start_sin * inner_sin
    sine = start_sin * inner_cos + start_cos * inner_sin
    cosine = jnp.concatenate([cosine, cosine], 1)
    sine = jnp.concatenate([-sine, sine], 1)

    queries, pairs = call(
        rotate_kernel,
        [((16, TOK, HEAD), BF), ((HEADS_DEV, 2 * TOK, HEAD), BF)],
        [VMEM] * 3,
        1000000000,
    )(attn_in, cosine, sine)
    over_y = [(s, s + devices // 2) for s in range(devices // 2)]
    far_pairs = lax.ppermute(pairs, "context", over_y)
    queries = exchange(queries, Q_GROUPS)

    states, gate, product = call(
        state_kernel,
        [((HEADS_DEV, MODES, HEAD), BF), ((TOK, CH), F32), ((TOK, CH), F32)],
        [VMEM] * 4,
        1000000,
    )(features, rim, jnp.pad(feat_weight, ((0, 0), (0, 5), (0, 0))), rates)
    far_states = lax.ppermute(states, "context", over_y)
    (near,) = call(
        near_kernel,
        [((TOK, CH), F32)],
        [VMEM] * 4,
        1000000,
        [pltpu.VMEM((2 * TOK, CH), F32), pltpu.VMEM((TOK, CH), F32)],
    )(product, coeff, rates, jnp.pad(skip[None, :], ((0, 7), (0, 0))))
    quarters = jnp.transpose(rates.reshape(MODES, CH // 128, 128), (1, 0, 2))
    (both,) = call(join_kernel, [((8, 2 * PACK, HEAD), BF)], [VMEM] * 4, 50000000000)(
        pairs, states, far_pairs, far_states
    )
    queries, both, coeff, quarters, near, gain = lax.optimization_barrier(
        (queries, both, coeff, quarters, near, norm_gain[None, :])
    )
    got = exchange(both, KV_GROUPS)
    (partial,) = call(
        attend_kernel,
        [((16, TOK + 32, HEAD), BF)],
        [SMEM] + [VMEM] * 3,
        4000000000,
    )(place, queries, got, quarters)
    partial = exchange(partial, Q_GROUPS)

    gained, squares, attn_out = call(
        tail_kernel,
        [((TOK, CH), F32), ((8, 128), F32), ((TOK, CH), BF)],
        [SMEM] + [VMEM] * 6,
        1000000000,
    )(place, partial, coeff, rates, near, gate, gain)
    squares = lax.all_to_all(squares, "dp", 0, 0, tiled=True)
    (hyena_out,) = call(norm_kernel, [((TOK, CH), BF)], [VMEM] * 2, 100000000)(squares, gained)
    return (hyena_out, attn_out)


def solution(mesh):
    return jax.shard_map(
        local,
        mesh=mesh,
        in_specs=(
            P("context", None, "dp"),
            P(None, None, "dp"),
            P("dp"),
            P(None, "dp"),
            P(None, "dp"),
            P("dp"),
            P("context", None, "dp"),
        ),
        out_specs=(P("context", "dp"), P("context", "dp")),
        check_vma=False,
    )
```

```python
import functools
import itertools
import math

import jax
import jax.numpy as jnp
from jax import lax
from jax.experimental import pallas as pl
from jax.experimental.pallas import tpu as pltpu
from jax.sharding import PartitionSpec as P

DH = 4096
HEAD = 128
HEADS_DEV = 4
FEAT = 3
MODES = 16
TOK = 64
CH = 512
ROPE_BASE = 1000000.0
NEG = -1e30
PACK = 2 * TOK + MODES
WIDE = 128
BLOCKS = WIDE // TOK
BF = jnp.bfloat16
F32 = jnp.float32

DIGITS = {"y": (2, 32), "s": (2, 16), "r": (2, 8), "v": (4, 2), "u": (2, 1)}


def groups_over(*free):
    fixed = [d for d in DIGITS if d not in free]

    def places(names):
        return [
            sum(v * DIGITS[d][1] for v, d in zip(values, names))
            for values in itertools.product(*[range(DIGITS[d][0]) for d in names])
        ]

    return [[base + step for step in places(free)] for base in places(fixed)]


Q_GROUPS = groups_over("r", "v", "u")
KV_GROUPS = groups_over("s", "r", "u")

VMEM = pl.BlockSpec(memory_space=pltpu.VMEM)
SMEM = pl.BlockSpec(memory_space=pltpu.SMEM)


def call(kernel, outs, specs, flops, scratch=()):
    return pl.pallas_call(
        kernel,
        out_shape=[jax.ShapeDtypeStruct(s, d) for s, d in outs],
        in_specs=specs,
        out_specs=[VMEM] * len(outs),
        scratch_shapes=list(scratch),
        compiler_params=pltpu.CompilerParams(vmem_limit_bytes=16 * 1024 * 1024),
        cost_estimate=pl.CostEstimate(flops=flops, bytes_accessed=1000, transcendentals=0),
    )


def digits(index):
    return [(index // step) % size for size, step in DIGITS.values()]


def member(head, v):
    return (head // 2) * 8 + v * 2 + head % 2


def expand(rates, weights, start):
    ahead = (lax.broadcasted_iota(jnp.int32, (8, 128), 0) + start).astype(F32)
    bases = [jnp.exp(-rates[n : n + 1, :] * ahead) for n in range(MODES)]
    tiles = []
    for a in range(8):
        scaled = weights * jnp.exp(rates * (-8.0 * a))
        tiles.append(sum(bases[n] * scaled[n : n + 1, :] for n in range(MODES)))
    return tiles


def rotated(x, cosine, sine):
    x = x.astype(F32)
    return (x * cosine + pltpu.roll(x, HEAD // 2, 1) * sine).astype(BF)


def pair_kernel(attn_ref, cos_ref, sin_ref, kv_ref):
    cosine, sine = cos_ref[...], sin_ref[...]
    for h in range(HEADS_DEV):
        lanes = slice(h * HEAD, (h + 1) * HEAD)
        kv_ref[h, :TOK, :] = rotated(attn_ref[1, :, lanes], cosine, sine)
        kv_ref[h, TOK:, :] = attn_ref[2, :, lanes]


def query_kernel(attn_ref, cos_ref, sin_ref, q_ref):
    cosine, sine = cos_ref[...], sin_ref[...]
    for h in range(HEADS_DEV):
        turned = rotated(attn_ref[0, :, h * HEAD : (h + 1) * HEAD], cosine, sine)
        for v in range(4):
            q_ref[member(h, v)] = turned


def state_kernel(feat_ref, rim_ref, weight_ref, rates_ref, state_ref, gate_ref, prod_ref):
    groups = []
    for g in range(3):
        x = jnp.concatenate([rim_ref[g], feat_ref[g].astype(F32)], 0)
        total = weight_ref[0, g : g + 1, :] * x[8 : 8 + TOK]
        for o in range(1, FEAT):
            total = total + weight_ref[o, g : g + 1, :] * x[8 - o : 8 - o + TOK]
        groups.append(total)
    gate_ref[...] = groups[0]
    product = (groups[1] * groups[2]).astype(BF).astype(F32)
    prod_ref[...] = product
    back = (7 - lax.broadcasted_iota(jnp.int32, (8, 128), 0)).astype(F32)
    for part in range(CH // 128):
        lanes = slice(part * 128, (part + 1) * 128)
        step = jnp.exp(-8.0 * rates_ref[:, lanes])
        rows = []
        for n in range(MODES):
            total = product[:8, lanes]
            for a in range(1, 8):
                total = total * step[n : n + 1, :] + product[8 * a : 8 * a + 8, lanes]
            total = total * jnp.exp(-rates_ref[n : n + 1, lanes] * back)
            rows.append(jnp.sum(total, 0, keepdims=True))
        state_ref[part] = jnp.concatenate(rows, 0).astype(BF)


def join_kernel(pair_ref, state_ref, far_pair_ref, far_state_ref, out_ref):
    for peer in range(8):
        head = peer % 4
        out_ref[peer, : 2 * TOK, :] = pair_ref[head]
        out_ref[peer, 2 * TOK : PACK, :] = state_ref[head]
        out_ref[peer, PACK : PACK + 2 * TOK, :] = far_pair_ref[head]
        out_ref[peer, PACK + 2 * TOK :, :] = far_state_ref[head]


def near_kernel(prod_ref, coeff_ref, rates_ref, skip_ref, out_ref, padded, impulse):
    padded[:TOK, :] = jnp.zeros((TOK, CH), F32)
    padded[TOK:, :] = prod_ref[...]
    for part in range(CH // 128):
        lanes = slice(part * 128, (part + 1) * 128)
        rows = expand(rates_ref[:, lanes], coeff_ref[:, lanes], 0)
        for a in range(8):
            impulse[8 * a : 8 * a + 8, lanes] = rows[a]
        y = skip_ref[:1, lanes] * prod_ref[:, lanes]
        for t in range(TOK):
            y = y + impulse[t : t + 1, lanes] * padded[TOK - t : 2 * TOK - t, lanes]
        out_ref[:, lanes] = y


def write_messages(index, got_ref, rates_ref, out_ref):
    y, s, r, v, u = digits(index)
    decay = rates_ref[2 * r + u] * (-float(TOK))

    def faded(steps):
        return jnp.exp(decay * jnp.maximum(steps, 0).astype(F32))

    def when(condition):
        return jnp.where(condition, 1.0, 0.0).astype(F32)

    second = when(y == 1)
    own_states = [got_ref[i, 2 * TOK : PACK, :].astype(F32) for i in range(8)]
    other_states = [got_ref[i, PACK + 2 * TOK :, :].astype(F32) * second for i in range(8)]
    reach, close = {}, {}
    for vt in range(4):
        for du in (-1, 0, 1):
            steps = 2 * (vt - v) + du - 1
            reach[vt, du] = faded(steps + 8)
            close[vt, du] = faded(steps) * when(steps >= 0)
    for rt in range(2):
        before = [jnp.zeros((MODES, 128), F32) for _ in range(2)]
        level = [jnp.zeros((MODES, 128), F32) for _ in range(2)]
        for pair in range(4):
            gap = 16 * (s - pair // 2) + 8 * (rt - pair % 2)
            earlier = faded(gap - 8) * when(gap > 0)
            across = faded(gap + 24)
            for us in range(2):
                i = pair * 2 + us
                before[us] = before[us] + earlier * own_states[i] + across * other_states[i]
                level[us] = level[us] + when(gap == 0) * own_states[i]
        for vt in range(4):
            for ut in range(2):
                state = jnp.zeros((MODES, 128), F32)
                for us in range(2):
                    state = state + reach[vt, ut - us] * before[us] + close[vt, ut - us] * level[us]
                out_ref[rt * 8 + vt * 2 + ut, 80:96, :] = state.astype(BF)


def norm_kernel(square_ref, gained_ref, out_ref):
    total = jnp.sum(square_ref[...], 0, keepdims=True)
    total = jnp.transpose(jnp.broadcast_to(total, (128, 128)))[:TOK, :]
    factor = lax.rsqrt(total * (1.0 / DH) + 1e-06)
    for part in range(CH // 128):
        lanes = slice(part * 128, (part + 1) * 128)
        out_ref[:, lanes] = (gained_ref[:, lanes] * factor).astype(BF)


def attend(keys, values, query, mask):
    scores = lax.dot_general(
        query, keys, (((1,), (1,)), ((), ())), preferred_element_type=F32
    ) * (math.log2(math.e) / math.sqrt(HEAD))
    scores = mask(scores)
    top = jnp.max(scores, 1, keepdims=True)
    weights = jnp.exp2(scores - top)
    mixed = lax.dot_general(
        weights.astype(BF), values, (((1,), (0,)), ((), ())), preferred_element_type=F32
    )
    return top, mixed[:, HEAD:], mixed[:, :HEAD]


def attend_kernel(place_ref, q_ref, got_ref, rates_ref, out_ref):
    y, s, _, v, _ = digits(place_ref[0])
    write_messages(place_ref[0], got_ref, rates_ref, out_ref)

    def half(first):
        keys = got_ref[:, first : first + TOK, :].reshape(8 * TOK, HEAD)
        values = got_ref[:, first + TOK : first + 2 * TOK, :].reshape(8 * TOK, HEAD)
        return keys, jnp.concatenate([values, jnp.ones((8 * TOK, HEAD), BF)], 1)

    own, other = half(0), half(PACK)
    lane = lax.broadcasted_iota(jnp.int32, (1, 8 * TOK), 1)
    block = lane // TOK
    key_pos = ((block // 4) * 16 + ((block // 2) % 2) * 8 + 2 * v + block % 2) * TOK + lane % TOK
    which = lax.broadcasted_iota(jnp.int32, (16, 128), 0)

    def query_of(tile):
        return q_ref[tile * BLOCKS : (tile + 1) * BLOCKS].reshape(WIDE, HEAD)

    def own_part(tile):
        row = lax.broadcasted_iota(jnp.int32, (WIDE, 1), 0) + tile * WIDE
        q_pos = s * (16 * TOK) + row
        return attend(*own, query_of(tile), lambda t: jnp.where(key_pos <= q_pos, t, NEG))

    def write(tile, top, total, mixed):
        mixed = mixed.astype(BF).reshape(BLOCKS, TOK, HEAD)
        out_ref[tile * BLOCKS : (tile + 1) * BLOCKS, :TOK, :] = mixed
        level = jnp.broadcast_to(top + jnp.log2(total), (WIDE, 128))
        for pair in range(WIDE // 128):
            row = jnp.transpose(level[pair * 128 : (pair + 1) * 128])[:1, :]
            high = row.astype(BF).astype(F32)
            rest = row - high
            middle = rest.astype(BF).astype(F32)
            last = rest - middle
            stats = jnp.where(
                which == 0,
                high,
                jnp.where(which == 1, middle, jnp.where(which == 2, last, 0.0)),
            ).astype(BF)
            for b in range(2):
                out_ref[tile * BLOCKS + 2 * pair + b, TOK:80, :] = stats

    @pl.when(y == 0)
    def _():
        for tile in range(16 * TOK // WIDE):
            top, total, mixed = own_part(tile)
            write(tile, top, total, mixed * (1.0 / total))

    @pl.when(y == 1)
    def _():
        for tile in range(16 * TOK // WIDE):
            top_a, total_a, mixed_a = own_part(tile)
            top_b, total_b, mixed_b = attend(*other, query_of(tile), lambda t: t)
            top = jnp.maximum(top_a, top_b)
            scale_a, scale_b = jnp.exp2(top_a - top), jnp.exp2(top_b - top)
            total = total_a * scale_a + total_b * scale_b
            inverse = 1.0 / total
            write(tile, top, total, mixed_a * (scale_a * inverse) + mixed_b * (scale_b * inverse))


def merge(index, got_ref, out_ref):
    odd = index % 2
    levels = jnp.sum(got_ref[:, TOK:80, :].astype(F32), 1)
    levels = jnp.where(odd == 1, pltpu.roll(levels, TOK, 1), levels)
    weights = []
    for h in range(HEADS_DEV):
        part = jnp.concatenate([levels[member(h, k) : member(h, k) + 1] for k in range(4)], 0)
        part = jnp.exp2(part - jnp.max(part, 0, keepdims=True))
        weights.append(part / jnp.sum(part, 0, keepdims=True))
    weights = jnp.concatenate(weights + [jnp.zeros((112, 128), F32)], 0)
    weights = jnp.transpose(weights)[:TOK, :]
    for h in range(HEADS_DEV):
        total = jnp.zeros((TOK, HEAD), F32)
        for k in range(4):
            place = h * 4 + k
            got = got_ref[member(h, k), :TOK, :].astype(F32)
            total = total + weights[:, place : place + 1] * got
        out_ref[:, h * HEAD : (h + 1) * HEAD] = total.astype(BF)


def tail_kernel(
    place_ref, got_ref, coeff_ref, rates_ref, near_ref, gate_ref, gain_ref, gained_ref, square_ref, out_ref
):
    squares = jnp.zeros((TOK, 128), F32)
    for part in range(CH // 128):
        lanes = slice(part * 128, (part + 1) * 128)
        state = got_ref[member(part, 0), 80:96, :].astype(F32)
        for v in range(1, 4):
            state = state + got_ref[member(part, v), 80:96, :].astype(F32)
        tiles = expand(rates_ref[:, lanes], coeff_ref[:, lanes] * state, 1)
        gated = gate_ref[:, lanes] * (near_ref[:, lanes] + jnp.concatenate(tiles, 0))
        gained_ref[:, lanes] = gated * gain_ref[:, lanes]
        squares = squares + gated * gated
    total = jnp.broadcast_to(jnp.sum(squares, 1, keepdims=True), (TOK, 128))
    total = jnp.concatenate([total, jnp.zeros((TOK, 128), F32)], 0)
    square_ref[...] = jnp.transpose(total)[:8, :]
    merge(place_ref[0], got_ref, out_ref)


def exchange(value, groups):
    return lax.all_to_all(value, "context", 0, 0, axis_index_groups=groups, tiled=True)


def local(features, feat_weight, skip, residues, rates, norm_gain, attn_in):
    index = lax.axis_index("context")
    devices = lax.axis_size("context")
    place = index.astype(jnp.int32)[None]
    features = jnp.transpose(features, (1, 0, 2))
    attn_in = jnp.transpose(attn_in, (1, 0, 2))
    rim = lax.ppermute(
        features[:, TOK - (FEAT - 1) :], "context", [(s, s + 1) for s in range(devices - 1)]
    )

    coeff = residues * jnp.sqrt(-jnp.expm1(-2.0 * rates))
    inverse = jnp.exp(
        jnp.arange(HEAD // 2, dtype=F32) * (-2.0 * math.log(ROPE_BASE) / HEAD)
    )
    positions = (index * TOK + jnp.arange(TOK)).astype(F32)
    angle = positions[:, None] * inverse[None, :]
    cosine, sine = jnp.cos(angle), jnp.sin(angle)
    cosine = jnp.concatenate([cosine, cosine], 1)
    sine = jnp.concatenate([-sine, sine], 1)

    (queries,) = call(query_kernel, [((16, TOK, HEAD), BF)], [VMEM] * 3, 1000000)(
        attn_in, cosine, sine
    )
    queries, cosine = lax.optimization_barrier((queries, cosine))
    (pairs,) = call(
        pair_kernel, [((HEADS_DEV, 2 * TOK, HEAD), BF)], [VMEM] * 3, 1000000
    )(attn_in, cosine, sine)
    over_y = [(s, s + devices // 2) for s in range(devices // 2)]
    far_pairs = lax.ppermute(pairs, "context", over_y)
    queries = exchange(queries, Q_GROUPS)

    rim = jnp.pad(rim.astype(F32), ((0, 0), (6, 0), (0, 0)))
    states, gate, product = call(
        state_kernel,
        [((HEADS_DEV, MODES, HEAD), BF), ((TOK, CH), F32), ((TOK, CH), F32)],
        [VMEM] * 4,
        1000000,
    )(features, rim, jnp.pad(feat_weight, ((0, 0), (0, 5), (0, 0))), rates)
    far_states = lax.ppermute(states, "context", over_y)
    (near,) = call(
        near_kernel,
        [((TOK, CH), F32)],
        [VMEM] * 4,
        1000000,
        [pltpu.VMEM((2 * TOK, CH), F32), pltpu.VMEM((TOK, CH), F32)],
    )(product, coeff, rates, jnp.pad(skip[None, :], ((0, 7), (0, 0))))
    quarters = jnp.transpose(rates.reshape(MODES, CH // 128, 128), (1, 0, 2))
    (both,) = call(join_kernel, [((8, 2 * PACK, HEAD), BF)], [VMEM] * 4, 50000000000)(
        pairs, states, far_pairs, far_states
    )
    queries, both, coeff, quarters, near, gain = lax.optimization_barrier(
        (queries, both, coeff, quarters, near, norm_gain[None, :])
    )
    got = exchange(both, KV_GROUPS)
    (partial,) = call(
        attend_kernel,
        [((16, TOK + 32, HEAD), BF)],
        [SMEM] + [VMEM] * 3,
        4000000000,
    )(place, queries, got, quarters)
    partial = exchange(partial, Q_GROUPS)

    gained, squares, attn_out = call(
        tail_kernel,
        [((TOK, CH), F32), ((8, 128), F32), ((TOK, CH), BF)],
        [SMEM] + [VMEM] * 6,
        1000000000,
    )(place, partial, coeff, rates, near, gate, gain)
    squares = lax.all_to_all(squares, "dp", 0, 0, tiled=True)
    (hyena_out,) = call(norm_kernel, [((TOK, CH), BF)], [VMEM] * 2, 100000000)(squares, gained)
    return (hyena_out, attn_out)


def solution(mesh):
    return jax.shard_map(
        local,
        mesh=mesh,
        in_specs=(
            P("context", None, "dp"),
            P(None, None, "dp"),
            P("dp"),
            P(None, "dp"),
            P(None, "dp"),
            P("dp"),
            P("context", None, "dp"),
        ),
        out_specs=(P("context", "dp"), P("context", "dp")),
        check_vma=False,
    )
```
